32 devices in a mesh: tower: 2 (over y), dp: 4 (over z), mp: 4 (over x, core).
Axes of the slice: x: 2, y: 2, z: 4, core: 2. Of those that a mesh axis runs over, the one named last changes fastest.
Arguments:
- tokens: bfloat16 [2, 4, 1024, 1024], P('tower', 'dp', 'mp'), may hold values from -6 to 6
- segment_ids: int32 [2, 4, 1024], P(None, 'dp'), may hold values from 0 to 7, never falling along the last dimension, each value on 1 to 512 neighbouring positions
- key_mask: int32 [2, 4, 1024], P(None, 'dp'), may hold values 0 or 1
- positives: int32 [4, 8], replicated, may hold values from 0 to 7, each once within a row
- w_qkv: bfloat16 [1024, 3, 1024], P(None, None, 'mp'), may hold values from -0.1875 to 0.1875
- b_qv: float32 [2, 1024], P(None, 'mp'), may hold values from -3 to 3
- w_out: bfloat16 [1024, 1024], P('mp'), may hold values from -0.75 to 0.75
- b_out: float32 [1024], replicated, may hold values from -2 to 2
- gain_one: float32 [1024], replicated, may hold values from 0.5 to 1.5
- shift_one: float32 [1024], replicated, may hold values from -2 to 2
- w_up: bfloat16 [1024, 4096], P(None, 'mp'), may hold values from -0.1875 to 0.1875
- b_up: float32 [4096], P('mp'), may hold values from -2 to 2
- w_down: bfloat16 [4096, 1024], P('mp'), may hold values from -0.09375 to 0.09375
- b_down: float32 [1024], replicated, may hold values from -2 to 2
- gain_two: float32 [1024], replicated, may hold values from 0.5 to 1.5
- shift_two: float32 [1024], replicated, may hold values from -2 to 2
- w_col: bfloat16 [1024, 1024], P('mp'), may hold values from -0.1875 to 0.1875
- b_col: float32 [1024], replicated, may hold values from -2 to 2
Outputs:
- encoded: bfloat16 [2, 4, 1024, 1024], P('tower', 'dp', 'mp')
- loss: float32 [], replicated
- col_scores: float32 [4, 8, 8], P('dp')
- d_tokens: bfloat16 [2, 4, 1024, 1024], P('tower', 'dp', 'mp')
- grad_qkv: float32 [1024, 3, 1024], P(None, None, 'mp')
- grad_qv_bias: float32 [2, 1024], P(None, 'mp')
- grad_out: float32 [1024, 1024], P('mp')
- grad_out_bias: float32 [1024], replicated
- grad_gain_one: float32 [1024], replicated
- grad_shift_one: float32 [1024], replicated
- grad_up: float32 [1024, 4096], P(None, 'mp')
- grad_up_bias: float32 [4096], P('mp')
- grad_down: float32 [4096, 1024], P('mp')
- grad_down_bias: float32 [1024], replicated
- grad_gain_two: float32 [1024], replicated
- grad_shift_two: float32 [1024], replicated
- grad_col: float32 [1024, 1024], P('mp')
- grad_col_bias: float32 [1024], replicated
The draws below stay inside these ranges and needn't reach their ends.
Inputs may be any that keep to these rules, and one draw needn't show every extreme that they name: `segment_ids`: in every row segment ids never fall, every id of 0 to 7 is present, and one segment holds exactly 512 tokens. `positives`: each row is a permutation of 0 to 7.
All inputs are finite; a program needn't handle non-finite values. No bound on the sum of `key_mask` on one device may be relied on, other than what follows from the above.
Results may differ from the reference program's by a relative error of at most 0.017.
Values may be sent and summed in bfloat16 or wider, within the bound.
No kernel may reach another device: no remote copies, remote signals or barrier semaphores. Data moves between devices by JAX's collectives and lax.ppermute only.
A program may use at most 128 MiB of HBM per device.

```python
import math
from functools import partial
import jax
import jax.numpy as jnp
import numpy as np
from jax import lax

D = 1024
FF = 4096
HEAD_DIM = 64
HEADS = 16
ROW_LEN = 1024
SEGS = 8
N_DP = 4


def plant(entries, rng, smallest, largest):
    dims = entries.shape
    spot = [jax.random.randint(jax.random.fold_in(rng, axis), (), 0, dims[axis]) for axis in range(len(dims))]
    entries = entries.at[tuple(spot)].set(smallest)
    longest = dims.index(max(dims))
    spot[longest] = (spot[longest] + 1) % dims[longest]
    return entries.at[tuple(spot)].set(largest)


def block_scale(rng, shape, pieces, low, high):
    factor_of = 1.0
    for dim, shards_of in pieces:
        heights = jax.random.uniform(jax.random.fold_in(jax.random.fold_in(rng, 6), dim), (shards_of,), jnp.float32, low / len(pieces), high / len(pieces))
        factor_of = factor_of * jnp.repeat(jnp.exp(heights), shape[dim] // shards_of).reshape((-1,) + (1,) * (len(shape) - 1 - dim))
    return factor_of


def profile(amount, total, most, slope):
    portions = [(1 << 20) // math.isqrt(rank ** slope) + 1 for rank in range(2, amount + 1)]
    spare, counts = total - most - (amount - 1), [1] * (amount - 1)
    while spare > 0:
        movable = [i for i in range(amount - 1) if counts[i] < most]
        mass, budget = sum([portions[i] for i in movable]), spare
        for i in movable:
            extra = min(most - counts[i], max(1, budget * portions[i] // mass), spare)
            counts[i] = counts[i] + extra
            spare = spare - extra
    return np.array([most] + counts)


def uneven(stream_key, number_of, total, limit, lean):
    if number_of == 2:
        one = jax.random.randint(stream_key, (), max(1, total - limit), min(limit, total - 1) + 1)
        return jnp.stack([one, total - one])
    lengths = jnp.asarray(profile(number_of, total, limit, lean), jnp.int32)
    pairs = (number_of - 1) // 2
    giver, sink = lengths[1:1 + 2 * pairs:2], lengths[2:2 + 2 * pairs:2]
    room = jnp.minimum(giver - 1, limit - sink)
    shifted = jax.random.randint(jax.random.fold_in(stream_key, 1), (pairs,), 0, 1 << 20) % (room + 1)
    lengths = lengths.at[1:1 + 2 * pairs:2].set(giver - shifted).at[2:2 + 2 * pairs:2].set(sink + shifted)
    return lengths[jax.random.permutation(jax.random.fold_in(stream_key, 2), number_of)]


def bell_draw(key, extent, scale, limit, split=(), kind=jnp.bfloat16):
    array = jax.random.normal(key, extent, jnp.float32) * scale
    if len(split) > 0:
        array = block_scale(key, extent, split, -0.22, 0.18) * array
    return jnp.clip(array, min=-limit, max=limit).astype(kind)


def setup_inputs(seed: int = 0) -> dict:
    arg_keys = jax.random.split(jax.random.key(seed), 19)
    tokens = bell_draw(arg_keys[0], (2, N_DP, ROW_LEN, D), 1.0, 6.0, ((0, 2), (1, 4), (2, 4)))
    segment_ids = jax.vmap(lambda own: jnp.searchsorted(jnp.cumsum(uneven(own, SEGS, ROW_LEN, ROW_LEN // 2, 2)), jnp.arange(ROW_LEN), side="right"))(jax.random.split(arg_keys[1], 2 * N_DP)).reshape((2, N_DP, ROW_LEN)).astype(jnp.int32)
    key_mask = plant((jax.random.randint(arg_keys[2], (2, N_DP, ROW_LEN), 0, 8) < 7).astype(jnp.int32), jax.random.fold_in(arg_keys[2], 1), 0, 1)
    positives = jax.vmap(lambda own: jax.random.permutation(own, SEGS))(jax.random.split(arg_keys[3], N_DP)).reshape((N_DP, SEGS)).astype(jnp.int32)
    w_qkv = bell_draw(arg_keys[4], (D, 3, D), D ** -0.5, 0.1875, ((2, 4),))
    b_qv = bell_draw(arg_keys[5], (2, D), 0.5, 3.0, ((1, 4),), jnp.float32)
    w_out = bell_draw(arg_keys[6], (D, D), HEAD_DIM ** -0.5, 0.75, ((0, 4),))
    b_out = bell_draw(arg_keys[7], (D,), 0.3, 2.0, (), jnp.float32)
    gain_one = jnp.clip(1.0 + 0.1 * jax.random.normal(arg_keys[8], (D,), jnp.float32), 0.5, 1.5)
    shift_one = bell_draw(arg_keys[9], (D,), 0.3, 2.0, (), jnp.float32)
    w_up = bell_draw(arg_keys[10], (D, FF), D ** -0.5, 0.1875, ((1, 4),))
    b_up = bell_draw(arg_keys[11], (FF,), 0.3, 2.0, ((0, 4),), jnp.float32)
    w_down = bell_draw(arg_keys[12], (FF, D), FF ** -0.5, 0.09375, ((0, 4),))
    b_down = bell_draw(arg_keys[13], (D,), 0.3, 2.0, (), jnp.float32)
    gain_two = jnp.clip(1.0 + 0.1 * jax.random.normal(arg_keys[14], (D,), jnp.float32), 0.5, 1.5)
    shift_two = bell_draw(arg_keys[15], (D,), 0.3, 2.0, (), jnp.float32)
    w_col = bell_draw(arg_keys[16], (D, D), D ** -0.5, 0.1875, ((0, 4),))
    b_col = bell_draw(arg_keys[17], (D,), 0.3, 2.0, (), jnp.float32)
    return dict(tokens=tokens, segment_ids=segment_ids, key_mask=key_mask, positives=positives, w_qkv=w_qkv, b_qv=b_qv, w_out=w_out, b_out=b_out, gain_one=gain_one, shift_one=shift_one, w_up=w_up, b_up=b_up, w_down=w_down, b_down=b_down, gain_two=gain_two, shift_two=shift_two, w_col=w_col, b_col=b_col)


EPS = 1e-05
NORM_EPS = 1e-06
SCALE_DENSE = 50.0
SCALE_COL = 50.0
SHARP = 20.0
BLOCK_ROWS = 512
HIGH = lax.Precision.HIGHEST

@jax.custom_vjp
def low(v):
    return lax.optimization_barrier(v.astype(jnp.bfloat16)).astype(jnp.float32)

@jax.custom_vjp
def low_back(v):
    return v

def low_keep(v):
    return (low(v), None)

def low_pass(kept, grad):
    return (grad,)

def back_keep(v):
    return (v, None)

def back_low(kept, grad):
    return (low(grad),)
low.defvjp(low_keep, low_pass)
low_back.defvjp(back_keep, back_low)

def matmul(first_op, second_op):
    return jnp.dot(first_op, second_op, precision=HIGH)

def layer_norm(values, gain_vec, shift_vec):
    row_mean = lax.optimization_barrier(jnp.mean(values, axis=-1, keepdims=True))
    centred = values - row_mean
    spread = lax.optimization_barrier(jnp.mean(centred * centred, axis=-1, keepdims=True))
    return centred * lax.rsqrt(spread + EPS) * gain_vec + shift_vec

def unit_rows(values):
    return values * lax.rsqrt(lax.optimization_barrier(jnp.sum(values * values, axis=-1, keepdims=True)) + NORM_EPS)

def row_tables(seg_row, mask_row):
    length = seg_row.shape[0]
    labels = jnp.arange(SEGS, dtype=jnp.int32)
    member = seg_row[None, :] == labels[:, None]
    starts = lax.optimization_barrier(jnp.sum((seg_row[None, :] < labels[:, None]).astype(jnp.int32), axis=1))
    places = jnp.arange(length, dtype=jnp.int32)
    cls_pick = places[None, :] == starts[:, None]
    is_valid = jnp.logical_or(mask_row > 0, jnp.any(cls_pick, axis=0))
    return (member, cls_pick, is_valid)

def soft_rows(masked):
    row_top = lax.optimization_barrier(jnp.max(masked, axis=-1, keepdims=True))
    exp_terms = jnp.exp(masked - row_top)
    return exp_terms / lax.optimization_barrier(jnp.sum(exp_terms, axis=-1, keepdims=True))

def attend(query_rows, key_rows, value_rows, seg_row, is_valid):
    length = query_rows.shape[0]
    block_rows = min(BLOCK_ROWS, length)
    blocks = length // block_rows
    key_heads = key_rows.reshape(length, HEADS, HEAD_DIM)
    value_heads = value_rows.reshape(length, HEADS, HEAD_DIM)

    def one_block(inputs):
        query_block, seg_block = inputs
        raw_scores = low_back(jnp.einsum('qhd,khd->hqk', query_block, key_heads, precision=HIGH) * 0.125)
        allowed = jnp.logical_and(seg_block[:, None] == seg_row[None, :], is_valid[None, :])
        masked = jnp.where(allowed[None], raw_scores, -1e+30)
        attn_probs = soft_rows(masked)
        mixed_out = jnp.einsum('hqk,khd->qhd', low(attn_probs), value_heads, precision=HIGH)
        return low(low_back(mixed_out))
    mixed_all = lax.map(jax.checkpoint(one_block), (query_rows.reshape(blocks, block_rows, HEADS, HEAD_DIM), seg_row.reshape(blocks, block_rows)))
    return mixed_all.reshape(length, HEADS * HEAD_DIM)

def encode_row(params, token_row, seg_row, is_valid):
    w_qkv, b_qv, w_out, b_out, gain_one, shift_one, w_up, b_up, w_down, b_down, gain_two, shift_two, w_col, b_col = params
    query_rows = low(low_back(matmul(token_row, w_qkv[:, 0]) + b_qv[0]))
    key_rows = low(low_back(matmul(token_row, w_qkv[:, 1])))
    value_rows = low(low_back(matmul(token_row, w_qkv[:, 2]) + b_qv[1]))
    context = attend(query_rows, key_rows, value_rows, seg_row, is_valid)
    attn_out = low_back(matmul(context, w_out)) + b_out
    hidden = layer_norm(token_row + attn_out, gain_one, shift_one)
    inner_act = low_back(matmul(low(hidden), w_up) + b_up)
    active = low(jax.nn.gelu(inner_act, approximate=False))
    ffn_out = low_back(matmul(active, w_down)) + b_down
    return layer_norm(hidden + ffn_out, gain_two, shift_two)

def one_row(params, inputs):
    token_row, seg_row, mask_row = inputs
    member, cls_pick, is_valid = row_tables(seg_row, mask_row)
    final_rows = encode_row(params, token_row, seg_row, is_valid)
    cls_raw = matmul(cls_pick.astype(jnp.float32), final_rows)
    cls_unit = low(unit_rows(cls_raw))
    col_pre = low_back(matmul(low(final_rows), params[12]) + params[13])
    col_vec = low(unit_rows(col_pre))
    return (final_rows, cls_unit, col_vec)

def pair_score(inputs):
    query_vecs, passage_vecs, seg_query, mask_query, seg_passage, mask_passage = inputs
    member_q, pick_q, valid_q = row_tables(seg_query, mask_query)
    member_p, pick_p, valid_p = row_tables(seg_passage, mask_passage)
    weight_q = jnp.logical_and(member_q, valid_q[None, :]).astype(jnp.float32)
    weight_p = jnp.logical_and(member_p, valid_p[None, :]).astype(jnp.float32)
    similar = low_back(matmul(query_vecs, passage_vecs.T))
    nearest = jnp.log(matmul(jnp.exp(SHARP * similar), weight_p.T)) / SHARP
    return matmul(weight_q, nearest) / lax.optimization_barrier(jnp.sum(weight_q, axis=1, keepdims=True))

def cross_entropy(logits, targets):
    columns = jnp.arange(logits.shape[1], dtype=jnp.int32)
    onehot = (targets[:, None] == columns[None, :]).astype(jnp.float32)
    return jnp.sum(jax.nn.logsumexp(logits, axis=1) - lax.optimization_barrier(jnp.sum(logits * onehot, axis=1)))

def total_loss(all_tokens, params, segment_ids, key_mask, positives):
    token_rows = all_tokens.reshape(2 * N_DP, ROW_LEN, D)
    seg_rows = segment_ids.reshape(2 * N_DP, ROW_LEN)
    mask_rows = key_mask.reshape(2 * N_DP, ROW_LEN)
    final_rows, cls_unit, col_vec = lax.map(jax.checkpoint(partial(one_row, params)), (token_rows, seg_rows, mask_rows))
    units = cls_unit.reshape(2, N_DP * SEGS, D)
    dense_logits = low_back(matmul(units[0], units[1].T) * SCALE_DENSE)
    targets = (jnp.arange(N_DP, dtype=jnp.int32)[:, None] * SEGS + positives).reshape(N_DP * SEGS)
    dense_loss = cross_entropy(dense_logits, targets)
    pairs = lax.map(jax.checkpoint(pair_score), (col_vec[:N_DP], col_vec[N_DP:], seg_rows[:N_DP], mask_rows[:N_DP], seg_rows[N_DP:], mask_rows[N_DP:]))
    col_logits = pairs.reshape(N_DP * SEGS, SEGS) * SCALE_COL
    col_loss = cross_entropy(col_logits, positives.reshape(N_DP * SEGS))
    return ((dense_loss + col_loss) / SEGS, (final_rows, pairs))

def reference(tokens, segment_ids, key_mask, positives, w_qkv, b_qv, w_out, b_out, gain_one, shift_one, w_up, b_up, w_down, b_down, gain_two, shift_two, w_col, b_col):
    params = tuple((weight.astype(jnp.float32) for weight in (w_qkv, b_qv, w_out, b_out, gain_one, shift_one, w_up, b_up, w_down, b_down, gain_two, shift_two, w_col, b_col)))
    start_rows = tokens.astype(jnp.float32)

    def objective(all_tokens, weights):
        return total_loss(all_tokens, weights, segment_ids, key_mask, positives)
    loss_sum, backward, extras = jax.vjp(objective, start_rows, params, has_aux=True)
    final_rows, pairs = extras
    grad_tokens, grads = backward(jnp.ones_like(loss_sum))
    encoded = final_rows.reshape(2, N_DP, ROW_LEN, D).astype(jnp.bfloat16)
    return (encoded, loss_sum, pairs, grad_tokens.astype(jnp.bfloat16), grads[0], grads[1], grads[2], grads[3], grads[4], grads[5], grads[6], grads[7], grads[8], grads[9], grads[10], grads[11], grads[12], grads[13])
```

```python
import math

import jax
import jax.numpy as jnp
from jax import lax
from jax.sharding import PartitionSpec as P

HEAD_DIM = 64
EPS = 1e-05
NORM_EPS = 1e-06
SCALE_DENSE = 50.0
SCALE_COL = 50.0
SHARP = 20.0
BLOCK_ROWS = 512
HIGH = lax.Precision.HIGHEST
BF = jnp.bfloat16
F32 = jnp.float32


def swap(block, axis, bit):
    count = lax.axis_size(axis)
    return lax.ppermute(block, axis, [(low, low ^ bit) for low in range(count)])


def gather_mp(own):
    near = swap(own, "mp", 1)
    far = swap(own, "mp", 2)
    return own, near, far, swap(far, "mp", 1)


def scatter_mp(own_half, far_half):
    count = own_half.shape[0] // 2
    far_sum = far_half[:count] + swap(far_half[count:].astype(BF), "mp", 1).astype(F32)
    arrived = swap(far_sum.astype(BF), "mp", 2)
    own_sum = own_half[:count] + swap(own_half[count:].astype(BF), "mp", 1).astype(F32)
    return own_sum + arrived.astype(F32)


def dp_bits():
    return [1 << k for k in range(int(math.log2(lax.axis_size("dp"))))]


def sum_rest(value, dim):
    hops = [("tower", 1)] + [("dp", bit) for bit in dp_bits()]
    value = value.astype(BF)
    for axis, bit in hops:
        half = value.shape[dim] // 2
        side = jnp.minimum(lax.axis_index(axis) & bit, 1)
        send = lax.dynamic_slice_in_dim(value, (1 - side) * half, half, dim)
        keep = lax.dynamic_slice_in_dim(value, side * half, half, dim)
        value = (keep.astype(F32) + swap(send, axis, bit).astype(F32)).astype(BF)
    for axis, bit in hops[::-1]:
        other = swap(value, axis, bit)
        first = (lax.axis_index(axis) & bit) == 0
        value = jnp.where(
            first,
            lax.concatenate([value, other], dim),
            lax.concatenate([other, value], dim),
        )
    return value.astype(F32)


def sum_small(value, hops):
    for axis, bit in hops:
        value = value + swap(value, axis, bit)
    return value


def relative(values, mp_index):
    shape = values.shape
    blocks = values.reshape(shape[:-1] + (2, 2, shape[-1] // 4))
    blocks = jnp.where(mp_index & 1, blocks[..., ::-1, :], blocks)
    blocks = jnp.where(mp_index & 2, blocks[..., ::-1, :, :], blocks)
    return blocks.reshape(shape)


def bdot(first_op, second_op):
    return jnp.dot(first_op, second_op, preferred_element_type=F32)


def nt_dot(first_op, second_op, precision=None):
    return lax.dot_general(
        first_op, second_op, (((1,), (1,)), ((), ())), precision=precision, preferred_element_type=F32
    )


def tn_dot(first_op, second_op, precision=None):
    return lax.dot_general(
        first_op, second_op, (((0,), (0,)), ((), ())), precision=precision, preferred_element_type=F32
    )


def fdot(first_op, second_op):
    return jnp.dot(first_op, second_op, precision=HIGH)


def norm_rows(values):
    row_mean = jnp.mean(values, axis=-1, keepdims=True)
    centred = values - row_mean
    scale = lax.rsqrt(jnp.mean(centred * centred, axis=-1, keepdims=True) + EPS)
    return centred * scale, scale


def norm_back(grad, normed, scale, gain_vec):
    scaled = grad * gain_vec
    mean_one = jnp.mean(scaled, axis=-1, keepdims=True)
    mean_two = jnp.mean(scaled * normed, axis=-1, keepdims=True)
    back = scale * (scaled - mean_one - normed * mean_two)
    return back, jnp.sum(grad * normed, axis=0), jnp.sum(grad, axis=0)


def unit_rows(values):
    scale = lax.rsqrt(jnp.sum(values * values, axis=-1, keepdims=True) + NORM_EPS)
    return values * scale, scale


def unit_back(grad, unit, scale):
    return scale * (grad - unit * jnp.sum(grad * unit, axis=-1, keepdims=True))


def cross_entropy(logits, targets):
    columns = jnp.arange(logits.shape[1], dtype=jnp.int32)
    onehot = (targets[:, None] == columns[None, :]).astype(F32)
    row_top = jnp.max(logits, axis=1, keepdims=True)
    exp_terms = jnp.exp(logits - row_top)
    row_total = jnp.sum(exp_terms, axis=1, keepdims=True)
    losses = row_top[:, 0] + jnp.log(row_total[:, 0]) - jnp.sum(logits * onehot, axis=1)
    return (losses, exp_terms / row_total - onehot)


def attend_forward(query_rows, key_rows, value_rows, seg_row, is_valid):
    length = query_rows.shape[0]
    head_count = query_rows.shape[1] // HEAD_DIM
    block_rows = min(BLOCK_ROWS, length)
    blocks = length // block_rows
    key_heads = key_rows.reshape(length, head_count, HEAD_DIM)
    value_heads = value_rows.reshape(length, head_count, HEAD_DIM)

    def one_block(inputs):
        query_block, seg_block = inputs
        raw_scores = (
            jnp.einsum("qhd,khd->hqk", query_block, key_heads, preferred_element_type=F32) * 0.125
        )
        allowed = jnp.logical_and(seg_block[:, None] == seg_row[None, :], is_valid[None, :])
        masked = jnp.where(allowed[None], raw_scores, -1e30)
        row_top = jnp.max(masked, axis=-1, keepdims=True)
        exp_terms = jnp.exp(masked - row_top)
        row_total = jnp.sum(exp_terms, axis=-1, keepdims=True)
        attn_probs = (exp_terms / row_total).astype(BF)
        mixed_out = jnp.einsum("hqk,khd->qhd", attn_probs, value_heads, preferred_element_type=F32)
        return (mixed_out.astype(BF), (row_top + jnp.log(row_total))[..., 0])

    mixed_all, log_total = lax.map(
        one_block,
        (
            query_rows.reshape(blocks, block_rows, head_count, HEAD_DIM),
            seg_row.reshape(blocks, block_rows),
        ),
    )
    return (mixed_all.reshape(length, head_count * HEAD_DIM), log_total)


def attend_backward(query_rows, key_rows, value_rows, grad_mixed, seg_row, is_valid, log_total):
    length = query_rows.shape[0]
    head_count = query_rows.shape[1] // HEAD_DIM
    block_rows = min(BLOCK_ROWS, length)
    blocks = length // block_rows
    key_heads = key_rows.reshape(length, head_count, HEAD_DIM)
    value_heads = value_rows.reshape(length, head_count, HEAD_DIM)

    def one_block(carry, inputs):
        key_acc, value_acc = carry
        query_block, seg_block, grad_block, total_block = inputs
        raw_scores = (
            jnp.einsum("qhd,khd->hqk", query_block, key_heads, preferred_element_type=F32) * 0.125
        )
        allowed = jnp.logical_and(seg_block[:, None] == seg_row[None, :], is_valid[None, :])
        masked = jnp.where(allowed[None], raw_scores, -1e30)
        attn_probs = jnp.exp(masked - total_block[..., None])
        grad_probs = jnp.einsum("qhd,khd->hqk", grad_block, value_heads, preferred_element_type=F32)
        row_dot = jnp.sum(attn_probs * grad_probs, axis=-1, keepdims=True)
        grad_scores = (attn_probs * (grad_probs - row_dot)).astype(BF)
        grad_query = (
            jnp.einsum("hqk,khd->qhd", grad_scores, key_heads, preferred_element_type=F32) * 0.125
        )
        key_acc = (
            key_acc
            + jnp.einsum("hqk,qhd->khd", grad_scores, query_block, preferred_element_type=F32) * 0.125
        )
        value_acc = value_acc + jnp.einsum(
            "hqk,qhd->khd", attn_probs.astype(BF), grad_block, preferred_element_type=F32
        )
        return ((key_acc, value_acc), grad_query.astype(BF))

    zero_acc = jnp.zeros((length, head_count, HEAD_DIM), F32)
    shaped = (blocks, block_rows, head_count, HEAD_DIM)
    (key_acc, value_acc), grad_query = lax.scan(
        one_block,
        (zero_acc, zero_acc),
        (
            query_rows.reshape(shaped),
            seg_row.reshape(blocks, block_rows),
            grad_mixed.reshape(shaped),
            log_total,
        ),
    )
    flat_shape = (length, head_count * HEAD_DIM)
    return (
        grad_query.reshape(flat_shape),
        key_acc.reshape(flat_shape).astype(BF),
        value_acc.reshape(flat_shape).astype(BF),
    )


def gelu_pair(inner):
    cdf = 0.5 + 0.5 * lax.erf(inner * math.sqrt(0.5))
    density = jnp.exp(-0.5 * inner * inner) * (1.0 / math.sqrt(2.0 * math.pi))
    return (inner * cdf).astype(BF), (cdf + inner * density).astype(BF)


def per_device(
    tokens,
    segment_ids,
    key_mask,
    positives,
    w_qkv,
    b_qv,
    w_out,
    b_out,
    gain_one,
    shift_one,
    w_up,
    b_up,
    w_down,
    b_down,
    gain_two,
    shift_two,
    w_col,
    b_col,
):
    own_rows = tokens[0, 0]
    own_count, model_dim = own_rows.shape
    pair_count = 2 * own_count
    mp_index = lax.axis_index("mp")
    is_query = lax.axis_index("tower") == 0
    dp_index = lax.axis_index("dp")
    dp_size = lax.axis_size("dp")
    seg_count = positives.shape[1]
    labels = jnp.arange(seg_count, dtype=jnp.int32)
    rel = lambda values: relative(values, mp_index)

    seg_pair = segment_ids[:, 0]
    starts = jnp.concatenate(
        [jnp.ones((2, 1), bool), seg_pair[:, 1:] != seg_pair[:, :-1]], axis=1
    )
    valid_pair = jnp.logical_or(key_mask[:, 0] > 0, starts)
    seg_rel = rel(seg_pair)
    start_rel = rel(starts.astype(jnp.int32)) > 0
    valid_rel = rel(valid_pair.astype(jnp.int32)) > 0
    seg_row = jnp.where(is_query, seg_rel[0], seg_rel[1])
    is_valid = jnp.where(is_query, valid_rel[0], valid_rel[1])
    start_row = jnp.where(is_query, start_rel[0], start_rel[1])
    members = seg_rel[:, None, :] == labels[None, :, None]
    weights = jnp.logical_and(members, valid_rel[:, None, :]).astype(F32)
    weight_q, weight_p = weights[0], weights[1]
    size_q = jnp.sum(weight_q, axis=1, keepdims=True)
    own_pick = jnp.logical_and(
        seg_row[None, :own_count] == labels[:, None], start_row[None, :own_count]
    ).astype(F32)

    x_chunks = gather_mp(own_rows)
    w_three = jnp.transpose(w_qkv, (1, 0, 2))
    x_near = jnp.concatenate(x_chunks[:2])
    x_far = jnp.concatenate(x_chunks[2:])

    def project(rows):
        return (
            (bdot(rows, w_three[0]) + b_qv[0]).astype(BF),
            bdot(rows, w_three[1]).astype(BF),
            (bdot(rows, w_three[2]) + b_qv[1]).astype(BF),
        )

    near_qkv, far_qkv = project(x_near), project(x_far)
    query_rows, key_rows, value_rows = (
        jnp.concatenate([near, far]) for near, far in zip(near_qkv, far_qkv)
    )
    context, log_total = attend_forward(query_rows, key_rows, value_rows, seg_row, is_valid)
    attn_sum = scatter_mp(bdot(context[:pair_count], w_out), bdot(context[pair_count:], w_out))
    normed_one, scale_one = norm_rows(own_rows.astype(F32) + attn_sum + b_out)
    hidden = normed_one * gain_one + shift_one

    col_chunks = gather_mp(w_col)
    col_near = jnp.where(
        mp_index & 1,
        jnp.concatenate([col_chunks[1], col_chunks[0]]),
        jnp.concatenate([col_chunks[0], col_chunks[1]]),
    )
    col_far = jnp.where(
        mp_index & 1,
        jnp.concatenate([col_chunks[3], col_chunks[2]]),
        jnp.concatenate([col_chunks[2], col_chunks[3]]),
    )
    col_weight = jnp.where(
        mp_index & 2, jnp.concatenate([col_far, col_near]), jnp.concatenate([col_near, col_far])
    )

    h_chunks = gather_mp(hidden.astype(BF))
    h_near, h_far = jnp.concatenate(h_chunks[:2]), jnp.concatenate(h_chunks[2:])
    act_near, slope_near = gelu_pair(bdot(h_near, w_up) + b_up)
    act_far, slope_far = gelu_pair(bdot(h_far, w_up) + b_up)
    ffn_sum = scatter_mp(bdot(act_near, w_down), bdot(act_far, w_down))
    normed_two, scale_two = norm_rows(hidden + ffn_sum + b_down)
    final_rows = normed_two * gain_two + shift_two
    encoded = final_rows.astype(BF)

    col_unit, col_scale = unit_rows(bdot(encoded, col_weight) + b_col)
    col_vec = col_unit.astype(BF)
    cls_unit, cls_scale = unit_rows(fdot(own_pick, final_rows))
    cls_own = cls_unit.astype(BF)
    half = own_count // 2
    other_a = swap(col_vec[:half], "tower", 1)
    other_b = swap(col_vec[half:], "tower", 1)
    cls_pair = jnp.concatenate([cls_own, swap(cls_own, "tower", 1)])
    far_a = swap(other_a, "mp", 2)
    far_b = swap(other_b, "mp", 2)
    cls_pair = sum_small(cls_pair, [("mp", 2), ("mp", 1)])
    other_near = jnp.concatenate([other_a, other_b])
    other_far = jnp.concatenate([far_a, far_b])
    others = jnp.concatenate(
        [other_near, swap(other_near, "mp", 1), other_far, swap(other_far, "mp", 1)]
    )

    exp_terms = jnp.exp(SHARP * nt_dot(col_vec, others))
    zero_sums = jnp.zeros((seg_count, 3 * own_count), F32)
    sums_q = nt_dot(weight_p, exp_terms, HIGH)
    sums_p = jnp.dot(weight_p[:, :own_count], exp_terms, precision=HIGH)
    sum_terms = jnp.where(is_query, jnp.concatenate([sums_q, zero_sums], axis=1), sums_p)

    def flip(values, bit):
        blocks = values.reshape(seg_count, 2, 2, own_count)
        blocks = blocks[:, ::-1] if bit == 2 else blocks[:, :, ::-1]
        return blocks.reshape(values.shape)

    sum_terms = sum_terms + flip(swap(sum_terms, "mp", 2), 2)
    sum_terms = sum_terms + flip(swap(sum_terms, "mp", 1), 1)
    nearest = jnp.log(sum_terms) / SHARP
    pair_score = nt_dot(weight_q, nearest, HIGH) / size_q
    positive_row = lax.dynamic_index_in_dim(positives, dp_index, 0, keepdims=False)
    col_losses, col_grad = cross_entropy(pair_score * SCALE_COL, positive_row)
    grad_pair = col_grad / seg_count * SCALE_COL
    grad_nearest = tn_dot(grad_pair / size_q, weight_q, HIGH)
    grad_sums = grad_nearest / (SHARP * sum_terms)
    left = jnp.where(is_query, grad_sums[:, :own_count], weight_p[:, :own_count])
    right = jnp.where(is_query, weight_p, grad_sums)
    grad_similar = (tn_dot(left, right, HIGH) * exp_terms * SHARP).astype(BF)
    grad_vec = bdot(grad_similar, others)
    grad_col_pre = unit_back(grad_vec, col_unit, col_scale).astype(BF)

    cls_all = cls_pair[None]
    order = dp_index[None]
    for bit in dp_bits():
        cls_all = jnp.concatenate([cls_all, swap(cls_all, "dp", bit)])
        order = jnp.concatenate([order, order ^ bit])
    cls_all = cls_all.reshape(dp_size, 2, seg_count, model_dim)
    cls_mine = cls_all[:, 0].reshape(dp_size * seg_count, model_dim)
    cls_theirs = cls_all[:, 1].reshape(dp_size * seg_count, model_dim)
    queries = jnp.where(is_query, cls_mine, cls_theirs)
    passages = jnp.where(is_query, cls_theirs, cls_mine)
    dense_logits = nt_dot(queries, passages) * SCALE_DENSE
    blocks = jnp.arange(dp_size, dtype=jnp.int32)[:, None]
    targets = (blocks * seg_count + positives[order]).reshape(dp_size * seg_count)
    dense_losses, dense_grad = cross_entropy(dense_logits, targets)
    dense_grad = (dense_grad / seg_count).astype(BF)
    grad_q = bdot(dense_grad[:seg_count], passages)
    grad_p = tn_dot(dense_grad[:, :seg_count], queries)
    grad_cls = jnp.where(is_query, grad_q, grad_p) * SCALE_DENSE
    grad_final = tn_dot(own_pick, unit_back(grad_cls, cls_unit, cls_scale), HIGH)
    loss_share = (jnp.sum(dense_losses[:seg_count]) + jnp.sum(col_losses)) / seg_count

    grad_final = grad_final + nt_dot(grad_col_pre, col_weight)
    grad_two, grad_gain_two, grad_shift_two = norm_back(
        grad_final, normed_two, scale_two, gain_two
    )
    grad_down_bias = jnp.sum(grad_two, axis=0)
    grad_col_bias = jnp.sum(grad_col_pre.astype(F32), axis=0)

    g_chunks = gather_mp(grad_two.astype(BF))
    g_near, g_far = jnp.concatenate(g_chunks[:2]), jnp.concatenate(g_chunks[2:])
    inner_near = (nt_dot(g_near, w_down) * slope_near.astype(F32)).astype(BF)
    inner_far = (nt_dot(g_far, w_down) * slope_far.astype(F32)).astype(BF)
    hidden_share = scatter_mp(nt_dot(inner_near, w_up), nt_dot(inner_far, w_up))
    grad_one, grad_gain_one, grad_shift_one = norm_back(
        grad_two + hidden_share, normed_one, scale_one, gain_one
    )
    grad_out_bias = jnp.sum(grad_one, axis=0)

    grad_down = sum_rest(tn_dot(act_near, g_near) + tn_dot(act_far, g_far), 0)
    grad_up = sum_rest(tn_dot(h_near, inner_near) + tn_dot(h_far, inner_far), 0)
    grad_up_bias = jnp.sum(inner_near.astype(F32), axis=0) + jnp.sum(
        inner_far.astype(F32), axis=0
    )
    col_part = tn_dot(rel(encoded), grad_col_pre)
    grad_col = sum_rest(scatter_mp(col_part[:pair_count], col_part[pair_count:]), 0)

    a_chunks = gather_mp(grad_one.astype(BF))
    a_near, a_far = jnp.concatenate(a_chunks[:2]), jnp.concatenate(a_chunks[2:])
    grad_context = jnp.concatenate([nt_dot(a_near, w_out), nt_dot(a_far, w_out)]).astype(BF)
    grad_out = sum_rest(
        tn_dot(context[:pair_count], a_near) + tn_dot(context[pair_count:], a_far), 0
    )
    grads = attend_backward(
        query_rows, key_rows, value_rows, grad_context, seg_row, is_valid, log_total
    )
    grad_x = [
        sum(nt_dot(grad[part], w_three[c]) for c, grad in enumerate(grads))
        for part in (slice(0, pair_count), slice(pair_count, 2 * pair_count))
    ]
    grad_input = grad_one + scatter_mp(grad_x[0], grad_x[1])
    grad_qkv = jnp.stack(
        [tn_dot(x_near, grad[:pair_count]) + tn_dot(x_far, grad[pair_count:]) for grad in grads]
    )
    grad_qkv = jnp.transpose(sum_rest(grad_qkv, 1), (1, 0, 2))
    d_tokens = grad_input.astype(BF).reshape(1, 1, own_count, model_dim)

    rest_hops = [("tower", 1)] + [("dp", bit) for bit in dp_bits()]
    share = loss_share / (2 * lax.axis_size("mp"))
    shared = jnp.stack(
        [
            grad_col_bias,
            grad_out_bias,
            grad_gain_one,
            grad_shift_one,
            grad_down_bias,
            grad_gain_two,
            grad_shift_two,
            jnp.broadcast_to(share, (model_dim,)),
        ]
    )
    shared = sum_small(shared, [("mp", 2), ("mp", 1)])
    shared = sum_small(jnp.concatenate([shared, grad_up_bias[None]]), rest_hops)
    qv_bias = sum_small(
        jnp.stack([jnp.sum(grads[0].astype(F32), axis=0), jnp.sum(grads[2].astype(F32), axis=0)]),
        rest_hops,
    )
    return (
        encoded.reshape(1, 1, own_count, model_dim),
        shared[7, 0],
        pair_score.reshape(1, seg_count, seg_count),
        d_tokens,
        grad_qkv,
        qv_bias,
        grad_out,
        shared[1],
        shared[2],
        shared[3],
        grad_up,
        shared[8],
        grad_down,
        shared[4],
        shared[5],
        shared[6],
        grad_col,
        shared[0],
    )


def solution(mesh):
    return jax.shard_map(
        per_device,
        mesh=mesh,
        in_specs=(
            P("tower", "dp", "mp", None),
            P(None, "dp", None),
            P(None, "dp", None),
            P(),
            P(None, None, "mp"),
            P(None, "mp"),
            P("mp", None),
            P(),
            P(),
            P(),
            P(None, "mp"),
            P("mp"),
            P("mp", None),
            P(),
            P(),
            P(),
            P("mp", None),
            P(),
        ),
        out_specs=(
            P("tower", "dp", "mp", None),
            P(),
            P("dp", None, None),
            P("tower", "dp", "mp", None),
            P(None, None, "mp"),
            P(None, "mp"),
            P("mp", None),
            P(),
            P(),
            P(),
            P(None, "mp"),
            P("mp"),
            P("mp", None),
            P(),
            P(),
            P(),
            P("mp", None),
            P(),
        ),
        check_vma=False,
    )
```

```python
import functools
import math

import jax
import jax.numpy as jnp
from jax import lax
from jax.experimental import pallas as pl
from jax.experimental.pallas import tpu as pltpu
from jax.sharding import PartitionSpec as P

HEAD_DIM = 64
EPS = 1e-05
NORM_EPS = 1e-06
SCALE_DENSE = 50.0
SCALE_COL = 50.0
SHARP = 20.0
HIGH = lax.Precision.HIGHEST
BF = jnp.bfloat16
F32 = jnp.float32
I32 = jnp.int32
LANES = 128
MIB = 1 << 20


def swap(block, axis, bit):
    count = lax.axis_size(axis)
    return lax.ppermute(block, axis, [(low, low ^ bit) for low in range(count)])


def after(value, *first):
    return lax.optimization_barrier((value,) + first)[0]


class Stream:
    def __init__(self, value):
        self.value = value


class Kept:
    def __init__(self, value):
        self.value = value


class Out:
    def __init__(self, shape, dtype):
        self.spec = (shape, dtype)


class KeptOut:
    def __init__(self, shape, dtype):
        self.spec = (shape, dtype)


class Arriving:
    def __init__(self, buffer, copy):
        self.buffer, self.copy, self.shape = buffer, copy, buffer.shape

    def wait(self):
        if self.copy is not None:
            self.copy.wait()
            self.copy = None

    def __getitem__(self, index):
        self.wait()
        return self.buffer[index]


class Leaving:
    def __init__(self, buffer, copy):
        self.buffer, self.copy, self.shape, self.dtype = buffer, copy, buffer.shape, buffer.dtype
        self.started = False

    def __setitem__(self, index, value):
        self.buffer[index] = value

    def flush(self):
        self.started = True
        self.copy.start()


MICROS = dict(
    project=1.0, attend=3.7, norm_one=1.5, feed_forward=3.0, feed_far=2.4, feed_keep=2.5,
    place_col=1.0, heads=2.0, heads_keep=2.2, similar=1.8, dense=0.8, scores=4.5, feed_back=2.5,
    weight_grad=4.0, turned_grad=1.5, norm_one_back=1.9, attend_back=8.0, input_grad=1.4,
    place_wide=2.3, place_last=3.0,
)


def call(body, name, ins, outs, scratch=(), semaphores=0, limit=8):
    streams = [v.value for v in ins if isinstance(v, Stream)]
    leaving = [v.spec for v in outs if isinstance(v, Out)]
    values = [
        pltpu.with_memory_space_constraint(v.value, pltpu.HBM)
        if isinstance(v, (Stream, Kept))
        else v
        for v in ins
    ]

    def spec_of(v):
        if isinstance(v, (Stream, Kept, Out, KeptOut)):
            return pl.BlockSpec(memory_space=pltpu.HBM)
        if not isinstance(v, tuple) and v.ndim == 1 and v.dtype == I32:
            return pl.BlockSpec(memory_space=pltpu.SMEM)
        return pl.BlockSpec(memory_space=pltpu.VMEM)

    specs = [v.spec if isinstance(v, (Out, KeptOut)) else v for v in outs]
    sems = len(streams) + len(leaving) + semaphores

    def kernel(*refs):
        refs = list(refs)
        in_refs, refs = refs[: len(ins)], refs[len(ins) :]
        out_refs, refs = refs[: len(outs)], refs[len(outs) :]
        in_buffers, refs = refs[: len(streams)], refs[len(streams) :]
        out_buffers, refs = refs[: len(leaving)], refs[len(leaving) :]
        own, tail = refs[: len(scratch)], refs[len(scratch) :]
        place = 0
        args = []
        for v, ref in zip(ins, in_refs):
            if isinstance(v, Stream):
                copy = pltpu.make_async_copy(ref, in_buffers[place], tail[0].at[place])
                copy.start()
                ref = Arriving(in_buffers[place], copy)
                place += 1
            args.append(ref)
        results = []
        for v, ref in zip(outs, out_refs):
            if isinstance(v, Out):
                buffer = out_buffers[place - len(streams)]
                ref = Leaving(buffer, pltpu.make_async_copy(buffer, ref, tail[0].at[place]))
                place += 1
            results.append(ref)
        more = [tail[0].at[place + k] for k in range(semaphores)]
        body(*args, *results, *own, *more)
        for ref in args:
            if isinstance(ref, Arriving):
                ref.wait()
        sent = [ref for ref in results if isinstance(ref, Leaving)]
        for ref in sent:
            if not ref.started:
                ref.flush()
        for ref in sent:
            ref.copy.wait()

    shapes = [(v.shape, v.dtype) for v in streams] + leaving + list(scratch)
    scratch_shapes = [pltpu.VMEM(shape, dtype) for shape, dtype in shapes]
    if sems:
        scratch_shapes.append(pltpu.SemaphoreType.DMA((sems,)))
    return pl.pallas_call(
        kernel,
        in_specs=[spec_of(v) for v in ins],
        out_specs=[spec_of(v) for v in outs],
        out_shape=[
            (pltpu.HBM if isinstance(v, (Out, KeptOut)) else jax.ShapeDtypeStruct)(*spec)
            for v, spec in zip(outs, specs)
        ],
        scratch_shapes=scratch_shapes,
        compiler_params=pltpu.CompilerParams(vmem_limit_bytes=limit * MIB),
        cost_estimate=pl.CostEstimate(
            flops=int(MICROS[name] * 1e9), bytes_accessed=int(MICROS[name] * 1e6), transcendentals=0
        ),
        name=name,
    )(*values)


def nn(left, right, precision=None):
    return lax.dot_general(
        left, right, (((1,), (0,)), ((), ())), precision=precision, preferred_element_type=F32
    )


def nt(left, right, precision=None):
    return lax.dot_general(
        left, right, (((1,), (1,)), ((), ())), precision=precision, preferred_element_type=F32
    )


def tn(left, right, precision=None):
    return lax.dot_general(
        left, right, (((0,), (0,)), ((), ())), precision=precision, preferred_element_type=F32
    )


def total(values):
    return jnp.sum(values, axis=0, keepdims=True)


def centre(values):
    return values - jnp.mean(values, axis=-1, keepdims=True)


def spread_of(centred):
    return lax.rsqrt(jnp.mean(centred * centred, axis=-1, keepdims=True) + EPS)


def norm_back(grad, normed, scale, gain):
    scaled = grad * gain
    mean_one = jnp.mean(scaled, axis=-1, keepdims=True)
    mean_two = jnp.mean(scaled * normed, axis=-1, keepdims=True)
    return scale * (scaled - mean_one - normed * mean_two)


def unit_rows(values):
    scale = lax.rsqrt(jnp.sum(values * values, axis=-1, keepdims=True) + NORM_EPS)
    return values * scale, scale


def unit_back(grad, unit, scale):
    return scale * (grad - unit * jnp.sum(grad * unit, axis=-1, keepdims=True))


def flagged(flag, shape):
    return (jnp.zeros(shape, I32) + flag) > 0


def project_body(first, second, weight, bias, query, key, value):
    count = first.shape[0]
    for place, source in enumerate((first, second)):
        rows = slice(place * count, (place + 1) * count)
        block = source[...]
        query[rows, :] = (nn(block, weight[0]) + bias[0:1, :]).astype(BF)
        key[rows, :] = nn(block, weight[1]).astype(BF)
        value[rows, :] = (nn(block, weight[2]) + bias[1:2, :]).astype(BF)


def head_masks(rows, heads):
    lanes = lax.broadcasted_iota(I32, rows.shape, 1) // HEAD_DIM
    return [jnp.where(lanes == head, rows, jnp.zeros_like(rows)) for head in range(heads)]


def allowed_pairs(seg_key, seg_query):
    return jnp.concatenate([seg_key] * (seg_query.shape[1] // LANES), axis=1) == seg_query


def attend_body(
    seg_key, seg_query, query, key_near, key_far, val_near, val_far,
    log_total, context_one, context_two, keys, values_t, context_t,
):
    half = key_near.shape[0]
    heads = query.shape[1] // HEAD_DIM
    keys[:half, :], keys[half:, :] = key_near[...], key_far[...]
    values_t[:, :half], values_t[:, half:] = val_near[...].T, val_far[...].T
    allowed = allowed_pairs(seg_key[...], seg_query[0:1, :])
    queries = head_masks(query[...] * BF(0.125), heads)

    def scores(head):
        return jnp.where(allowed, nt(keys[...], queries[head]), -1e30)

    current = scores(0)
    for head in range(heads):
        later = scores(head + 1) if head + 1 < heads else None
        rows = slice(head * HEAD_DIM, (head + 1) * HEAD_DIM)
        top = jnp.max(current, axis=0, keepdims=True)
        exp_terms = jnp.exp(current - top)
        norm = total(exp_terms)
        context_t[rows, :] = nn(values_t[rows, :], exp_terms.astype(BF)) * (1.0 / norm)
        log_total[head : head + 1, :] = top + jnp.log(norm)
        current = later
    log_total[heads:, :] = jnp.zeros((8 - heads, half), F32)
    log_total.flush()
    count = context_one.shape[0]
    context_one[...] = context_t[:, :count].T.astype(BF)
    context_two[...] = context_t[:, count:].T.astype(BF)


def attend_back_body(
    seg_key, seg_query, log_total, grad_one, grad_two, query, context_one, context_two,
    key_near, key_far, val_near, val_far, *refs, last,
):
    if last:
        key_before, value_before, gq, gk, gv, bias, keys, values, keys_t, grad_t = refs[:10]
        key_sum, value_sum, bias_before = refs[10], refs[11], None
    else:
        gq, key_sum, value_sum, bias, keys, values, keys_t, grad_t = refs
    half = key_near.shape[0]
    width = query.shape[1]
    heads = width // HEAD_DIM
    picked = (
        lax.broadcasted_iota(I32, (8, width), 1) // HEAD_DIM
        == lax.broadcasted_iota(I32, (8, width), 0)
    ).astype(F32)
    keys[:half, :], keys[half:, :] = key_near[...], key_far[...]
    values[:half, :], values[half:, :] = val_near[...], val_far[...]
    keys_t[...] = keys[...].T
    grad_context = jnp.concatenate([grad_one[...], grad_two[...]], axis=0)
    mixed = jnp.concatenate([context_one[...], context_two[...]], axis=0)
    allowed = allowed_pairs(seg_key[...], seg_query[0:1, :])
    dots = nt(picked, grad_context.astype(F32) * mixed.astype(F32), HIGH)
    queries = head_masks(query[...] * BF(0.125), heads)
    grad_heads = head_masks(grad_context, heads)

    def start(head):
        return nt(keys[...], queries[head]), nt(values[...], grad_heads[head])

    current = start(0)
    for head in range(heads):
        later = start(head + 1) if head + 1 < heads else None
        rows = slice(head * HEAD_DIM, (head + 1) * HEAD_DIM)
        raw, grad_probs = current
        probs = jnp.where(allowed, jnp.exp(raw - log_total[head : head + 1, :]), 0.0)
        grad_scores = (probs * (grad_probs - dots[head : head + 1, :])).astype(BF)
        add_v = nn(probs.astype(BF), grad_heads[head])
        add_k = nn(grad_scores, queries[head])
        if head:
            value_sum[...] += add_v
            key_sum[...] += add_k
        elif last:
            value_sum[...] = value_before[...] + add_v
            key_sum[...] = key_before[...] + add_k
        else:
            value_sum[...], key_sum[...] = add_v, add_k
        grad_t[rows, :] = nn(keys_t[rows, :], grad_scores)
        current = later
    grad_query = (grad_t[...].T * 0.125).astype(BF)
    gq[...] = grad_query
    bias[...] = jnp.zeros_like(bias)
    bias[0:1, :] = total(grad_query.astype(F32))
    if last:
        gk[...] = key_sum[...].astype(BF)
        grad_value = value_sum[...].astype(BF)
        gv[...] = grad_value
        bias[1:2, :] = total(grad_value.astype(F32))


def norm_one_body(
    tower, rows, mixed_0, mixed_1, mixed_2, mixed_3, w_0, w_1, w_2, w_3, w_2_more, w_3_more,
    b_out, gain, shift, hidden, centred,
):
    summed = rows[...].astype(F32) + b_out[...]
    summed = summed + nn(mixed_0[...], w_0[...]) + nn(mixed_1[...], w_1[...])
    here, there = lane_halves(tower, w_2)
    for mixed, weight, more in ((mixed_2, w_2, w_2_more), (mixed_3, w_3, w_3_more)):
        summed = summed + nn(mixed[:, here], weight[...]) + nn(mixed[:, there], more[...])
    middle = centre(summed)
    hidden[...] = (middle * spread_of(middle) * gain[...] + shift[...]).astype(BF)
    centred[...] = middle


def lane_halves(tower, part):
    size = part.shape[0]
    return (
        pl.ds(pl.multiple_of(tower[0] * size, size), size),
        pl.ds(pl.multiple_of((1 - tower[0]) * size, size), size),
    )


def gelu_pair(inner):
    cdf = 0.5 + 0.5 * lax.erf(inner * math.sqrt(0.5))
    density = jnp.exp(-0.5 * inner * inner) * (1.0 / math.sqrt(2.0 * math.pi))
    return (inner * cdf).astype(BF), (cdf + inner * density).astype(BF)


def ffn_body(
    first, second, w_up, b_up, w_down,
    active_one, active_two, slope_one, slope_two, part_one, part_two,
):
    inners = [nn(first[...], w_up[...]) + b_up[...]]
    inners.append(nn(second[...], w_up[...]) + b_up[...])
    places = ((active_one, slope_one, part_one), (active_two, slope_two, part_two))
    for inner, (active, slope, part) in zip(inners, places):
        act, active_slope = gelu_pair(inner)
        active[...] = act
        active.flush()
        slope[...] = active_slope
        slope.flush()
        part[...] = nn(act, w_down[...]).astype(BF)


def ffn_only_body(first, second, w_up, b_up, w_down, part_one, part_two):
    inners = [nn(second[...], w_up[...]) + b_up[...]]
    inners.append(nn(first[...], w_up[...]) + b_up[...])
    for inner, part in zip(inners, (part_two, part_one)):
        act = (inner * (0.5 + 0.5 * lax.erf(inner * math.sqrt(0.5)))).astype(BF)
        part[...] = nn(act, w_down[...]).astype(BF)


def ffn_keep_body(
    first, second, w_up, b_up,
    active_one, active_two, slope_one, slope_two, copy_one, copy_two,
):
    copy_one[...], copy_two[...] = first[...], second[...]
    copy_one.flush()
    copy_two.flush()
    for rows, active, slope in ((first, active_one, slope_one), (second, active_two, slope_two)):
        active[...], slope[...] = gelu_pair(nn(rows[...], w_up[...]) + b_up[...])
        active.flush()
        slope.flush()


def head_rows(centred, gain_one, shift_one, part, near, far, b_down, gain, shift):
    hidden = centred[...] * spread_of(centred[...]) * gain_one[...] + shift_one[...]
    summed = part[...].astype(F32) + near[...].astype(F32) + far[...].astype(F32)
    middle = centre(hidden + summed + b_down[...])
    return middle, middle * spread_of(middle) * gain[...] + shift[...]


def head_body(
    centred, gain_one, shift_one, part, near, far, b_down, gain, shift,
    col_weight, b_col, pick, cls_own, send_a, send_b,
):
    _, final = head_rows(centred, gain_one, shift_one, part, near, far, b_down, gain, shift)
    col, _ = unit_rows(nn(final.astype(BF), col_weight[...]) + b_col[...])
    cls, _ = unit_rows(nn(pick[...], final, HIGH))
    count = send_b.shape[0]
    col = col.astype(BF)
    padded = jnp.concatenate([cls, jnp.zeros_like(cls)], axis=0).astype(BF)
    cls_own[...] = padded
    send_a[:count, :] = col[:count]
    send_a[count:, :] = padded
    send_b[...] = col[count:]


def head_keep_body(
    centred, gain_one, shift_one, part, near, far, b_down, gain, shift,
    col_weight, b_col, pick, encoded, middle, col_pre, cls_raw,
):
    kept, final = head_rows(centred, gain_one, shift_one, part, near, far, b_down, gain, shift)
    middle[...] = kept
    middle.flush()
    encoded[...] = final.astype(BF)
    encoded.flush()
    col_pre[...] = nn(final.astype(BF), col_weight[...]) + b_col[...]
    col_pre.flush()
    cls_raw[...] = nn(pick[...], final, HIGH)


def similar_body(
    is_query, own_a, own_b, *refs
):
    pieces, (weight_p, exp_terms, others, sums), sems = refs[:8], refs[8:12], refs[12:]
    half = own_b.shape[0]
    count = 2 * half
    copies = []
    for place, piece in enumerate(pieces):
        rows = pl.ds(place * half, half)
        copies.append(
            pltpu.make_async_copy(piece.at[pl.ds(0, half)], others.at[rows], sems[place])
        )
        copies[-1].start()
    own = jnp.concatenate([own_a[:half, :], own_b[...]], axis=0)
    weight = weight_p[...].astype(BF)
    for copy in copies:
        copy.wait()
    terms = jnp.exp(SHARP * nt(own, others[...]))
    exp_terms[...] = terms
    high = terms.astype(BF)
    low = (terms - high.astype(F32)).astype(BF)
    sums_q = nt(weight, high) + nt(weight, low)
    sums_p = nn(weight[:, :count], high) + nn(weight[:, :count], low)
    sums_q = jnp.concatenate([sums_q, jnp.zeros((sums_q.shape[0], 3 * count), F32)], axis=1)
    sums[...] = jnp.where(flagged(is_query[0], sums_p.shape), sums_q, sums_p)


def dense_body(is_query, vectors, targets, cls_raw, grad_cls, loss):
    block = vectors[...]
    shape = (block.shape[0], block.shape[0])
    segs = cls_raw.shape[0]
    query_kind = 1 - is_query[0]
    row_kind = lax.broadcasted_iota(I32, shape, 0) // segs % 2
    col_kind = lax.broadcasted_iota(I32, shape, 1) // segs % 2
    is_row = row_kind == query_kind
    paired = jnp.logical_and(is_row, col_kind != query_kind)
    logits = jnp.where(paired, nt(block, block) * SCALE_DENSE, -1e30)
    onehot = targets[...]
    top = jnp.max(logits, axis=1, keepdims=True)
    exp_terms = jnp.where(paired, jnp.exp(logits - top), 0.0)
    norm = jnp.sum(exp_terms, axis=1, keepdims=True)
    norm = jnp.where(norm > 0.0, norm, 1.0)
    grad = ((exp_terms / norm - onehot) * (1.0 / segs)).astype(BF)
    grad = jnp.where(paired, grad, jnp.zeros_like(grad))
    hit = jnp.sum(jnp.where(paired, logits * onehot, 0.0), axis=1, keepdims=True)
    losses = top + jnp.log(norm) - hit
    rows = lax.broadcasted_iota(I32, losses.shape, 0)
    mine = jnp.logical_and(rows < 2 * segs, rows // segs % 2 == query_kind)
    loss[...] = jnp.zeros_like(loss) + jnp.sum(jnp.where(mine, losses, 0.0))
    grad_rows = nn(grad[: 2 * segs], block)[:segs]
    grad_cols = tn(grad[:, : 2 * segs], block)[:segs]
    own = jnp.where(flagged(is_query[0], grad_rows.shape), grad_rows, grad_cols) * SCALE_DENSE
    grad_cls[...] = unit_back(own, *unit_rows(cls_raw[...]))


def score_body(
    is_query, sums, exp_terms, others, weight_q, weight_p, target, col_pre,
    col_weight, grad_cls, dense_loss, pick, middle, gain,
    grad_pre, grad_two, grad_two_b, small, scores,
):
    count = exp_terms.shape[0]
    segs = weight_q.shape[0]
    seg_sums = sums[...]
    w_q, w_p = weight_q[...], weight_p[...]
    size = jnp.sum(w_q, axis=1, keepdims=True)
    nearest = jnp.log(seg_sums) * (1.0 / SHARP)
    pair = nt(w_q, nearest, HIGH) / size
    scores[...] = pair
    logits = pair * SCALE_COL
    onehot = target[...]
    top = jnp.max(logits, axis=1, keepdims=True)
    terms = jnp.exp(logits - top)
    norm = jnp.sum(terms, axis=1, keepdims=True)
    losses = top + jnp.log(norm) - jnp.sum(logits * onehot, axis=1, keepdims=True)
    loss = jnp.sum(losses) + dense_loss[0:1, 0:1]
    grad_pair = (terms / norm - onehot) * (SCALE_COL / segs) / size
    grad_sums = tn(grad_pair, w_q, HIGH) / (SHARP * seg_sums)
    left = jnp.where(
        flagged(is_query[0], (segs, count)), grad_sums[:, :count], w_p[:, :count]
    )
    right = jnp.where(flagged(is_query[0], w_p.shape), w_p, grad_sums)
    grad_similar = (tn(left, right, HIGH) * (exp_terms[...] * SHARP)).astype(BF)
    grad_vec = nn(grad_similar, others[...])
    pre = unit_back(grad_vec, *unit_rows(col_pre[...])).astype(BF)
    grad_pre[...] = pre
    grad_final = nt(pre, col_weight[...]) + tn(pick[...], grad_cls[...], HIGH)
    spread = spread_of(middle[...])
    unit = middle[...] * spread
    back = norm_back(grad_final, unit, spread, gain[...])
    grad_two[...] = back
    grad_two.flush()
    grad_two_b[...] = back.astype(BF)
    small[0:1, :] = total(pre.astype(F32))
    small[1:2, :] = total(back)
    small[2:3, :] = total(grad_final * unit)
    small[3:4, :] = total(grad_final)
    small[4:5, :] = jnp.zeros((1, unit.shape[1]), F32) + loss
    small[5:8, :] = jnp.zeros((3, unit.shape[1]), F32)


def ffn_back_body(
    first, second, slope_one, slope_two, w_down, w_up,
    inner_one, inner_two, part_one, part_two, bias,
):
    raws = [nt(first[...], w_down[...]), nt(second[...], w_down[...])]
    bias_sum = jnp.zeros((1, slope_one.shape[1]), F32)
    places = ((slope_one, inner_one, part_one), (slope_two, inner_two, part_two))
    for raw, (slope, inner, part) in zip(raws, places):
        grad = (raw * slope[...].astype(F32)).astype(BF)
        inner[...] = grad
        inner.flush()
        bias_sum = bias_sum + total(grad.astype(F32))
        part[...] = nt(grad, w_up[...]).astype(BF)
    bias[...] = bias_sum


def norm_one_back_body(
    tower, grad_two, part, near, far, centred, gain, w_0, w_1, w_2, w_3, w_2_more, w_3_more,
    grad_one, grad_b, small, mixed_0, mixed_1, mixed_2, mixed_3,
):
    grad = (
        grad_two[...]
        + part[...].astype(F32)
        + near[...].astype(F32)
        + far[...].astype(F32)
    )
    spread = spread_of(centred[...])
    unit = centred[...] * spread
    back = norm_back(grad, unit, spread, gain[...])
    grad_one[...] = back
    grad_one.flush()
    rounded = back.astype(BF)
    grad_b[...] = rounded
    grad_b.flush()
    here, there = lane_halves(tower, w_2)
    for weight, more, mixed in ((w_3, w_3_more, mixed_3), (w_2, w_2_more, mixed_2)):
        mixed[:, here] = nt(rounded, weight[...]).astype(BF)
        mixed[:, there] = nt(rounded, more[...]).astype(BF)
    mixed_1[...] = nt(rounded, w_1[...]).astype(BF)
    mixed_0[...] = nt(rounded, w_0[...]).astype(BF)
    small[0:1, :] = total(back)
    small[1:2, :] = total(grad * unit)
    small[2:3, :] = total(grad)
    small[3:8, :] = jnp.zeros((5, unit.shape[1]), F32)


def input_grad_body(grad_query, grad_key, grad_value, weight, part_one, part_two, *, start):
    count = part_one.shape[0]
    for place, out in ((1, part_two), (0, part_one)):
        own = slice(place * count, (place + 1) * count)
        rows = slice(start + place * count, start + (place + 1) * count)
        out[...] = (
            nt(grad_query[own, :], weight[0])
            + nt(grad_key[rows, :], weight[1])
            + nt(grad_value[rows, :], weight[2])
        ).astype(BF)


def order_rows(place, source, out, size):
    for block in range(source.shape[1] // size):
        start = pl.multiple_of((jnp.int32(block) ^ place) * size, size)
        out[block * size : (block + 1) * size, :] = source[:, pl.ds(start, size)].T


def weight_grad_body(place, *refs, lefts, rights, cuts):
    left = refs[:lefts]
    right = refs[lefts : lefts + sum(rights)]
    outs, (ordered, joined) = refs[lefts + sum(rights) : -2], refs[-2:]
    token = 0
    for part in left:
        tokens = slice(token, token + part.shape[0])
        order_rows(place[0], part, ordered.at[:, tokens], LANES)
        token += part.shape[0]
    at = 0
    lane = 0
    for group in rights:
        token = 0
        for part in right[at : at + group]:
            rows, lanes = part.shape
            joined[token : token + rows, lane : lane + lanes] = part[...]
            token += rows
        at += group
        lane += lanes
    half = ordered.shape[0] // 2
    lane = 0
    for cut, (keep, send) in zip(cuts, zip(outs[::2], outs[1::2])):
        lanes = slice(lane, lane + cut)
        for rows, out in ((slice(half, 2 * half), send), (slice(0, half), keep)):
            out[...] = nn(ordered[rows, :], joined[:, lanes]).astype(BF)
            if isinstance(out, Leaving):
                out.flush()
        lane += cut


def turned_grad_body(place, mp_place, grad, *refs, rows):
    left, (part_0, part_1, part_2, part_3, ordered) = refs[:-5], refs[-5:]
    order_rows(place[0], grad, ordered, LANES)
    for block, out in ((3, part_3), (2, part_2), (1, part_1), (0, part_0)):
        if len(left) == 1:
            start = pl.multiple_of((jnp.int32(block) ^ mp_place[0]) * rows, rows)
            right = left[0][:, pl.ds(start, rows)]
        else:
            right = left[block][...]
        out[...] = nn(ordered[...], right).astype(BF)


def place_col_body(mp_place, tower, w_0, w_1, w_2, w_3, w_2_more, w_3_more, out):
    count = w_0.shape[0]
    here, there = lane_halves(tower, w_2)
    for block, parts in enumerate(((w_0,), (w_1,), (w_2, w_2_more), (w_3, w_3_more))):
        start = pl.multiple_of((jnp.int32(block) ^ mp_place[0]) * count, count)
        if len(parts) == 1:
            out[pl.ds(start, count), :] = parts[0][...]
        else:
            size = parts[0].shape[0]
            out[pl.ds(pl.multiple_of(start + tower[0] * size, size), size), :] = parts[0][...]
            out[pl.ds(pl.multiple_of(start + (1 - tower[0]) * size, size), size), :] = parts[1][...]


def copy_out(copies, source, target, sem):
    copies.append(pltpu.make_async_copy(source, target, sem))
    copies[-1].start()


def place_wide_body(place, *refs, size):
    parts, (out, buffer), sems = refs[:4], refs[4:6], refs[6:]
    copies = []
    cut = parts[0].shape[1]
    for block in range(8):
        here = pl.ds(block * size, size)
        start = pl.multiple_of((jnp.int32(block) ^ place[0]) * size, size)
        row = block % 4 * size
        for column in range(2):
            part = parts[2 * column + block // 4]
            lanes = slice(column * cut, (column + 1) * cut)
            buffer[here, lanes] = part[row : row + size, :].astype(F32)
        copy_out(copies, buffer.at[here], out.at[pl.ds(start, size)], sems[block])
    for copy in copies:
        copy.wait()


def place_last_body(
    place, one, one_more, two, two_more, qkv, out, col, buffer, *sems, size
):
    copies = []
    width = qkv.shape[2]
    for block in range(8):
        here = pl.ds(block * size, size)
        start = pl.multiple_of((jnp.int32(block) ^ place[0]) * size, size)
        rows = slice(block % 4 * size, (block % 4 + 1) * size)
        first, second = ((one, two), (one_more, two_more))[block // 4]
        for kind in range(3):
            source, lane = ((first, 0), (first, width), (second, 0))[kind]
            buffer[kind, here, :] = source[rows, lane : lane + width].astype(F32)
            copy_out(
                copies,
                buffer.at[kind, here],
                qkv.at[kind, pl.ds(start, size)],
                sems[3 * block + kind],
            )
        out[:, pl.ds(start, size)] = second[rows, width : 2 * width].astype(F32).T
        col[:, pl.ds(start, size)] = second[rows, 2 * width :].astype(F32).T
    for copy in copies:
        copy.wait()


def dp_bits():
    return [1 << k for k in range(int(math.log2(lax.axis_size("dp"))))]


def add(*values):
    return sum(value.astype(F32) for value in values).astype(BF)


def side_of(axis, bit):
    return jnp.minimum(lax.axis_index(axis) & bit, 1)


def join(value, other, axis, bit):
    return jnp.where(
        side_of(axis, bit) == 0,
        jnp.concatenate([value, other]),
        jnp.concatenate([other, value]),
    )


def more_bits():
    return [("dp", bit) for bit in dp_bits()[2:]]


def sum_more(value):
    for axis, bit in more_bits():
        half = value.shape[0] // 2
        side = side_of(axis, bit)
        sent = lax.dynamic_slice_in_dim(value, (1 - side) * half, half, 0)
        kept = lax.dynamic_slice_in_dim(value, side * half, half, 0)
        value = add(kept, swap(sent, axis, bit))
    for axis, bit in more_bits()[::-1]:
        value = join(value, swap(value, axis, bit), axis, bit)
    return value


HOPS = (("tower", 1), ("dp", 1), ("dp", 2))


class Unit:
    def __init__(self, keep, send):
        self.value, self.send, self.stage = keep, send, 0

    def launch(self):
        axis, bit = HOPS[min(self.stage, 5 - self.stage)]
        return swap(self.send, axis, bit)

    def land(self, got):
        self.stage += 1
        if self.stage <= 3:
            value = self.value.astype(F32) + got.astype(F32)
            if self.stage < 3:
                half = value.shape[0] // 2
                self.value, self.send = value[:half], value[half:].astype(BF)
            else:
                self.send = sum_more(value.astype(BF))
        elif self.stage < 6:
            self.send = jnp.concatenate([self.send, got])
        else:
            self.halves = (self.send, got)


class Small:
    def __init__(self, value):
        self.send, self.stage = value, 0

    def launch(self):
        return swap(self.send, *HOPS[self.stage])

    def land(self, got):
        self.stage += 1
        self.send = self.send + got
        if self.stage == 3:
            for axis, bit in more_bits():
                self.send = self.send + swap(self.send, axis, bit)


def together(*values):
    return lax.optimization_barrier(values)


def phase(units, moves=(), fill=None):
    ready = [value for value, _ in moves] + [unit.send for unit in units]
    flights = [swap(value, *hop) for value, hop in moves]
    flights += [unit.launch() for unit in units]
    filled = fill(lambda value: after(value, *ready)) if fill else ()
    landed = together(*flights, *filled)
    for unit, got in zip(units, landed[len(moves) :]):
        unit.land(got)
    return landed[: len(moves)], landed[len(flights) :]


def place_of(hops):
    place = 0
    for axis, bit in hops:
        place = place * 2 + side_of(axis, bit)
    return place[None].astype(I32)


def relative(values, mp_index):
    size = values.shape[-1] // 4
    blocks = [values[..., k * size : (k + 1) * size] for k in range(4)]
    values = jnp.where(mp_index & 1, jnp.concatenate([blocks[k ^ 1] for k in range(4)], -1), values)
    blocks = [values[..., k * size : (k + 1) * size] for k in range(4)]
    return jnp.where(mp_index & 2, jnp.concatenate([blocks[k ^ 2] for k in range(4)], -1), values)


def flip(values, bit):
    size = values.shape[-1] // 4
    return jnp.concatenate([values[:, (k ^ bit) * size :][:, :size] for k in range(4)], axis=1)


def per_device(
    tokens,
    segment_ids,
    key_mask,
    positives,
    w_qkv,
    b_qv,
    w_out,
    b_out,
    gain_one,
    shift_one,
    w_up,
    b_up,
    w_down,
    b_down,
    gain_two,
    shift_two,
    w_col,
    b_col,
):
    own_rows = tokens[0, 0]
    count, model_dim = own_rows.shape
    pair, width = 2 * count, w_out.shape[0]
    half = count // 2
    units = w_up.shape[1]
    segs = positives.shape[1]
    dp_size = lax.axis_size("dp")
    mp_index = lax.axis_index("mp")
    dp_index = lax.axis_index("dp")
    tower = lax.axis_index("tower")
    is_query = tower == 0
    query_flag = (1 - tower)[None].astype(I32)
    mp_place = mp_index[None].astype(I32)
    rest_place = place_of(HOPS)
    tower_place = tower[None].astype(I32)
    labels = jnp.arange(segs, dtype=I32)
    row = lambda vector: vector[None, :]
    block_bf = ((count, model_dim), BF)
    block_f32 = ((count, model_dim), F32)

    def core(block):
        return swap(block, "mp", 1)

    def across(block):
        return swap(block, "mp", 2)

    x_0, x_1, x_2 = own_rows, core(own_rows), across(own_rows)
    w_three = jnp.transpose(w_qkv, (1, 0, 2))

    seg_pair = segment_ids[:, 0]
    starts = jnp.concatenate([jnp.ones((2, 1), bool), seg_pair[:, 1:] != seg_pair[:, :-1]], axis=1)
    valid_pair = jnp.logical_or(key_mask[:, 0] > 0, starts)
    codes = relative(seg_pair + 16 * valid_pair.astype(I32) + 32 * starts.astype(I32), mp_index)
    seg_rel, valid_rel = codes & 15, (codes & 16) > 0
    code_row = jnp.where(is_query, codes[0], codes[1])
    seg_row = code_row & 15
    seg_key = jnp.broadcast_to(
        jnp.where((code_row & 16) > 0, seg_row, -1)[:, None], (4 * count, LANES)
    )
    seg_query = jnp.broadcast_to(seg_row[None, :], (8, 4 * count))
    members = seg_rel[:, None, :] == labels[None, :, None]
    weights = jnp.logical_and(members, valid_rel[:, None, :]).astype(F32)
    weight_q, weight_p = weights[0], weights[1]
    pick = (code_row[None, :count] - 32 == labels[:, None] + 16).astype(F32)
    order = dp_index ^ jnp.arange(dp_size, dtype=I32)
    kinds = jnp.arange(2, dtype=I32)[None, :, None]
    targets = (
        jnp.arange(dp_size, dtype=I32)[:, None, None] * 2 * segs
        + (1 - tower) * segs
        + positives[order][:, None, :]
    )
    targets = jnp.where(kinds == tower, targets, -1).reshape(2 * dp_size * segs)
    paired = (targets[:, None] == jnp.arange(2 * dp_size * segs, dtype=I32)).astype(F32)
    positive_row = lax.dynamic_index_in_dim(positives, dp_index, 0, keepdims=False)
    positive_row = (positive_row[:, None] == labels).astype(F32)

    half_bf = ((pair, width), BF)
    mixed_bf = ((count, width), BF)
    x_hop, core_hop, y_hop = ("mp", 2), ("mp", 1), ("tower", 1)

    def project(first, second):
        return call(project_body, "project", [first, second, w_three, b_qv], [half_bf] * 3)

    near_qkv = project(x_0, x_1)
    halves = [
        lax.dynamic_slice_in_dim(weight, tower * half, half, 0) for weight in (w_out, w_col)
    ]
    x_2, w_out_half, w_col_half = together(
        x_2, *halves, near_qkv, seg_key, seg_query, weight_q, weight_p, pick, paired, positive_row
    )[:3]
    x_3 = core(x_2)
    out_1, out_2, col_1, col_2 = core(w_out), across(w_out_half), core(w_col), across(w_col_half)
    far_qkv = project(Stream(x_2), Stream(x_3))
    key_values = [near_qkv[1], far_qkv[1], near_qkv[2], far_qkv[2]]
    seg_query_near, seg_query_far = seg_query[:, :pair], seg_query[:, pair:]

    def attend(seg_half, query):
        return call(
            attend_body,
            "attend",
            [seg_key, seg_half, query, *key_values],
            [Out((8, pair), F32), mixed_bf, mixed_bf],
            [((4 * count, width), BF), ((width, 4 * count), BF), ((width, pair), F32)],
        )

    total_far, mixed_far_2, mixed_far_3 = attend(seg_query_far, far_qkv[0])
    mixed_far_2, mixed_far_3, out_2, out_1 = together(mixed_far_2, mixed_far_3, out_2, out_1)
    (mixed_2, mixed_1_2, out_2_more), (total_near, mixed_0, mixed_near_1, col_2, col_1) = phase(
        (),
        [(mixed_far_2, x_hop), (mixed_far_3, x_hop), (out_2, y_hop)],
        lambda late: [*attend(seg_query_near, late(near_qkv[0])), col_2, col_1],
    )
    mixed_1, mixed_3 = core(mixed_near_1), core(mixed_1_2)
    outs = [w_out, out_1, out_2, core(out_2), out_2_more, core(out_2_more)]
    col_3 = core(col_2)
    mixed = [mixed_0, mixed_1, mixed_2, mixed_3]
    hidden, centred_one = call(
        norm_one_body,
        "norm_one",
        [tower_place, own_rows, *mixed, *outs, row(b_out), row(gain_one), row(shift_one)],
        [block_bf, block_f32],
    )

    h_0, h_1 = hidden, core(hidden)
    kept_bf = Out((count, units), BF)
    (h_2, col_2_more), (act_0, act_1, slope_0, slope_1, part_0, part_1) = phase(
        (),
        [(hidden, x_hop), (col_2, y_hop)],
        lambda late: call(
            ffn_body,
            "feed_forward",
            [h_0, h_1, w_up, row(b_up), w_down],
            [kept_bf] * 4 + [Out(*block_bf), block_bf],
        ),
    )
    h_3, col_3_more = core(h_2), core(col_2_more)
    part_2, part_3 = call(
        ffn_only_body,
        "feed_far",
        [h_2, h_3, w_up, row(b_up), w_down],
        [block_bf] * 2,
    )
    near_sum = core(part_1)
    joined = add(part_2, core(part_3))
    joined, near_sum = together(joined, near_sum)
    (arrived,), (act_2, act_3, slope_2, slope_3, h_2_kept, h_3_kept, col_weight) = phase(
        (),
        [(joined, x_hop)],
        lambda late: [
            *call(
                ffn_keep_body,
                "feed_keep",
                [late(h_2), h_3, w_up, row(b_up)],
                [kept_bf] * 4 + [Out(*block_bf)] * 2,
            ),
            *call(
                place_col_body,
                "place_col",
                [mp_place, tower_place, w_col, late(col_1), col_2, col_3, col_2_more, col_3_more],
                [((model_dim, model_dim), BF)],
            ),
        ],
    )
    ins = [centred_one, row(gain_one), row(shift_one), part_0, near_sum, arrived]
    ins += [row(b_down), row(gain_two), row(shift_two), col_weight, row(b_col), pick]
    cls_own, send_a, send_b = call(
        head_body,
        "heads",
        ins,
        [((2 * segs, model_dim), BF), ((half + 2 * segs, model_dim), BF)]
        + [((half, model_dim), BF)],
    )

    (other_a,), (encoded, middle, col_pre, cls_raw) = phase(
        (),
        [(send_a, y_hop)],
        lambda late: call(
            head_keep_body,
            "heads_keep",
            [late(centred_one)] + ins[1:],
            [Out(*block_bf), Out(*block_f32), Out(*block_f32), Out((segs, model_dim), F32)],
        ),
    )
    (other_b, far_a, cls_far, near_a), _ = phase(
        (), [(send_b, y_hop), (other_a, x_hop), (cls_own, x_hop), (other_a, core_hop)]
    )
    cls_own = add(cls_own, cls_far)
    (far_b, near_b, diag_a, cls_near), _ = phase(
        (), [(other_b, x_hop), (other_b, core_hop), (far_a, core_hop), (cls_own, core_hop)]
    )
    cls_own = add(cls_own, cls_near)[:segs]
    cls_other = add(*[piece[half : half + segs] for piece in (other_a, near_a, far_a, diag_a)])
    cls_all = jnp.concatenate([cls_own, cls_other])
    diag_b = core(far_b)
    pieces = [other_a, other_b, near_a, near_b, far_a, far_b, diag_a, diag_b]
    exp_terms, others, sums = call(
        similar_body,
        "similar",
        [query_flag, Stream(send_a), Stream(send_b), *map(Kept, pieces), weight_p],
        [((count, 4 * count), F32), ((4 * count, model_dim), BF), ((segs, 4 * count), F32)],
        semaphores=8,
    )
    (swapped, cls_swapped), _ = phase((), [(sums, x_hop), (cls_all, ("dp", 1))])
    sums = sums + flip(swapped, 2)
    cls_all = jnp.concatenate([cls_all, cls_swapped])
    (swapped, cls_swapped), _ = phase((), [(sums, core_hop), (cls_all, ("dp", 2))])
    sums = sums + flip(swapped, 1)
    cls_all = jnp.concatenate([cls_all, cls_swapped])
    for bit in dp_bits()[2:]:
        cls_all = jnp.concatenate([cls_all, swap(cls_all, "dp", bit)])
    grad_cls, dense_loss = call(
        dense_body,
        "dense",
        [query_flag, cls_all, paired, cls_raw],
        [((segs, model_dim), F32), ((8, LANES), F32)],
    )
    grad_pre, grad_two, grad_two_b, small_two, pair_score = call(
        score_body,
        "scores",
        [query_flag, sums, exp_terms, others, weight_q, weight_p, positive_row]
        + [col_pre, col_weight, grad_cls, dense_loss, pick, middle, row(gain_two)],
        [block_bf, Out(*block_f32), block_bf, ((8, model_dim), F32), ((segs, segs), F32)],
        limit=10,
    )

    def feed_back(first, second, slope_one, slope_two, part):
        return call(
            ffn_back_body,
            "feed_back",
            [first, second, slope_one, slope_two, w_down, w_up],
            [kept_bf] * 2 + [part, block_bf, ((1, units), F32)],
        )

    def weight_grad(left, right, cuts):
        columns = sum(cuts)
        tokens = sum(part.value.shape[0] for part in left)
        rows = left[0].value.shape[1]
        shapes = [((rows // 2, cut), BF) for cut in cuts]
        outs = [Out(*shape) for cut in shapes for shape in (cut, cut)]
        outs[1] = shapes[0]
        return call(
            functools.partial(
                weight_grad_body,
                lefts=len(left),
                rights=[len(parts) for parts in right],
                cuts=cuts,
            ),
            "weight_grad",
            [rest_place, *left, *[part for parts in right for part in parts]],
            outs,
            [((rows, tokens), BF), ((tokens, columns), BF)],
            limit=20,
        )

    def streams(*values):
        return [Stream(value) for value in values]

    def turned_grad(grad, left):
        return call(
            functools.partial(turned_grad_body, rows=count),
            "turned_grad",
            [rest_place, mp_place, grad, *left],
            [Out((model_dim, count), BF)] * 2 + [((model_dim, count), BF)] * 2,
            [((model_dim, count), BF)],
        )

    g_0, g_1 = grad_two_b, core(grad_two_b)

    def near_back(late):
        backs = feed_back(g_0, g_1, slope_0, slope_1, Out(*block_bf))
        return [*backs, *turned_grad(after(grad_pre, backs[3]), [Stream(encoded)])]

    (g_2,), (inner_0, inner_1, part_0, part_1, bias_near, *col_parts) = phase(
        (), [(grad_two_b, x_hop)], near_back
    )
    g_3 = core(g_2)
    inner_2, inner_3, part_2, part_3, bias_far = feed_back(g_2, g_3, slope_2, slope_3, block_bf)
    cut = model_dim // 2
    (near_sum, arrived, col_near), down = phase(
        (),
        [(part_1, core_hop), (part_3, core_hop), (after(col_parts[3], part_3), core_hop)],
        lambda late: weight_grad(
            streams(act_0, act_1, act_2, act_3),
            [[Stream(g_0), Stream(g_1), late(g_2), g_3]],
            [cut, cut],
        ),
    )
    down = [Unit(*down[:2]), Unit(*down[2:])]
    joined = add(part_2, arrived)
    (arrived,), up = phase(
        down[:1],
        [(joined, x_hop)],
        lambda late: weight_grad(
            streams(late(h_0), h_1, h_2_kept, h_3_kept),
            [streams(inner_0, inner_1, inner_2, inner_3)],
            [cut, cut],
        ),
    )
    up = [Unit(*up[:2]), Unit(*up[2:])]
    grad_one, grad_one_b, small_one, back_0, back_1, back_2, back_3 = call(
        norm_one_back_body,
        "norm_one_back",
        [tower_place, grad_two, part_0, near_sum, arrived, centred_one, row(gain_one), *outs],
        [Out(*block_f32), Out(*block_bf), ((8, model_dim), F32)] + [mixed_bf] * 4,
        limit=12,
    )

    back_1, back_3 = core(back_1), core(back_3)
    all_bf, all_f32 = ((4 * count, width), BF), ((4 * count, width), F32)
    back_scratch = [all_bf] * 2 + [((width, 4 * count), BF), ((width, pair), F32)]

    def back_ins(seg_half, log_total, grads, query, mixed_pair):
        return streams(seg_key, seg_half, log_total) + grads + streams(
            query, *mixed_pair, *key_values
        )

    (back_2, back_3), (grad_q_near, key_sum, value_sum, bias_near_q) = phase(
        [down[1], down[0]],
        [(back_2, x_hop), (back_3, x_hop)],
        lambda late: call(
            functools.partial(attend_back_body, last=False),
            "attend_back",
            back_ins(
                seg_query_near,
                total_near,
                [late(back_0), back_1],
                near_qkv[0],
                (mixed_0, mixed_near_1),
            ),
            [half_bf, all_f32, all_f32, ((8, width), F32)],
            back_scratch,
            limit=16,
        ),
    )
    col_joined = add(col_parts[2], col_near)
    small = jnp.concatenate([small_two, small_one])

    def far_back(late):
        backs = call(
            functools.partial(attend_back_body, last=True),
            "attend_back",
            back_ins(
                seg_query_far,
                total_far,
                [late(back_2), back_3],
                far_qkv[0],
                (mixed_far_2, mixed_far_3),
            )
            + [key_sum, value_sum],
            [half_bf, all_bf, all_bf, ((8, width), F32)],
            back_scratch + [all_f32, all_f32],
            limit=16,
        )
        return [*backs, *turned_grad(after(grad_one_b, backs[1]), streams(*mixed))]

    (col_far, small_far), (grad_q_far, grad_k, grad_v, bias_far_v, *out_parts) = phase(
        [up[0], down[1], down[0]], [(col_joined, x_hop), (small, x_hop)], far_back
    )
    small = small + small_far
    (out_near, out_near_1, col_near_1, small_near), _ = phase(
        (),
        [(out_parts[3], core_hop), (out_parts[1], core_hop)]
        + [(col_parts[1], core_hop), (small, core_hop)],
    )
    small = jnp.concatenate([small + small_near, bias_near + bias_far])
    col_t = add(col_parts[0], col_near_1, col_far)
    out_joined = add(out_parts[2], out_near)

    def input_grad(grad_query, start):
        return call(
            functools.partial(input_grad_body, start=start),
            "input_grad",
            [*streams(grad_query, grad_k, grad_v, w_three)],
            [block_bf] * 2,
        )

    def own_grads(late):
        first = weight_grad(
            streams(late(x_0), x_1, x_2, x_3),
            [streams(grad_q_near, grad_q_far), streams(grad_k), streams(grad_v)],
            [2 * width, width],
        )
        return [*first, *input_grad(after(grad_q_far, first[1]), pair)]

    (out_far,), (keep_1, send_1, keep_2, send_2, part_2, part_3) = phase(
        [up[1], up[0], down[1], down[0]], [(out_joined, x_hop)], own_grads
    )
    out_t = add(out_parts[0], out_near_1, out_far)
    rest = [Unit(keep_1, send_1)]
    rows = model_dim // 2
    rest.append(
        Unit(
            *(
                jnp.concatenate([value, out_t[side], col_t[side]], axis=1)
                for value, side in ((keep_2, slice(0, rows)), (send_2, slice(rows, None)))
            )
        )
    )
    (arrived,), _ = phase((), [(part_3, core_hop)])
    joined = add(part_2, arrived)
    small = Small(small)
    qv_bias = Small(bias_far_v + bias_near_q)
    (arrived,), (part_0, part_1) = phase(
        [rest[0], up[1], up[0], down[1], down[0], small],
        [(joined, x_hop)],
        lambda late: input_grad(late(grad_q_near), 0),
    )
    (near_sum,), _ = phase(
        [rest[1], rest[0], up[1], up[0], down[1], small, qv_bias], [(part_1, core_hop)]
    )
    grad_input = (
        grad_one + part_0.astype(F32) + near_sum.astype(F32) + arrived.astype(F32)
    )
    d_tokens = grad_input.astype(BF).reshape(1, 1, count, model_dim)
    _, (d_tokens,) = phase(
        [down[0], rest[1], rest[0], up[1], up[0], small, qv_bias], (), lambda late: [d_tokens]
    )
    phase([down[1], rest[1], rest[0], up[1], qv_bias])

    def place_wide(late, first, second):
        halves = [late(first.halves[0]), first.halves[1], *second.halves]
        shape = (model_dim, 2 * halves[0].shape[1])
        return call(
            functools.partial(place_wide_body, size=model_dim // 8),
            "place_wide",
            [rest_place, *streams(*halves)],
            [KeptOut(shape, F32)],
            [(shape, F32)],
            semaphores=8,
        )

    _, (grad_down,) = phase(
        [up[0], rest[1], rest[0]], (), lambda late: place_wide(late, *down)
    )
    phase([up[1], rest[1]])
    _, (grad_up,) = phase([rest[0]], (), lambda late: place_wide(late, *up))
    phase([rest[1]])
    grad_qkv, grad_out, grad_col = call(
        functools.partial(place_last_body, size=model_dim // 8),
        "place_last",
        [rest_place, *streams(*rest[0].halves, *rest[1].halves)],
        [KeptOut((3, model_dim, width), F32)] + [Out((width, model_dim), F32)] * 2,
        [((3, model_dim, width), F32)],
        semaphores=24,
    )
    small, qv_bias = small.send, qv_bias.send
    loss = small[4, 0] * (1.0 / (segs * 2 * lax.axis_size("mp")))
    return (
        encoded.reshape(1, 1, count, model_dim),
        loss,
        pair_score.reshape(1, segs, segs),
        d_tokens,
        jnp.transpose(grad_qkv, (1, 0, 2)),
        qv_bias[:2],
        grad_out,
        small[8],
        small[9],
        small[10],
        grad_up,
        small[16],
        grad_down,
        small[1],
        small[2],
        small[3],
        grad_col,
        small[0],
    )


def solution(mesh):
    return jax.shard_map(
        per_device,
        mesh=mesh,
        in_specs=(
            P("tower", "dp", "mp", None),
            P(None, "dp", None),
            P(None, "dp", None),
            P(),
            P(None, None, "mp"),
            P(None, "mp"),
            P("mp", None),
            P(),
            P(),
            P(),
            P(None, "mp"),
            P("mp"),
            P("mp", None),
            P(),
            P(),
            P(),
            P("mp", None),
            P(),
        ),
        out_specs=(
            P("tower", "dp", "mp", None),
            P(),
            P("dp", None, None),
            P("tower", "dp", "mp", None),
            P(None, None, "mp"),
            P(None, "mp"),
            P("mp", None),
            P(),
            P(),
            P(),
            P(None, "mp"),
            P("mp"),
            P("mp", None),
            P(),
            P(),
            P(),
            P("mp", None),
            P(),
        ),
        check_vma=False,
    )
```

```python
import functools
import math

import jax
import jax.numpy as jnp
from jax import lax
from jax.experimental import pallas as pl
from jax.experimental.pallas import tpu as pltpu
from jax.sharding import PartitionSpec as P

HEAD_DIM = 64
EPS = 1e-05
NORM_EPS = 1e-06
SCALE_DENSE = 50.0
SCALE_COL = 50.0
SHARP = 20.0
HIGH = lax.Precision.HIGHEST
BF = jnp.bfloat16
F32 = jnp.float32
I32 = jnp.int32
LANES = 128
MIB = 1 << 20


def swap(block, axis, bit):
    count = lax.axis_size(axis)
    return lax.ppermute(block, axis, [(low, low ^ bit) for low in range(count)])


def after(value, *first):
    return lax.optimization_barrier((value,) + first)[0]


class Stream:
    def __init__(self, value):
        self.value = value


class Kept:
    def __init__(self, value):
        self.value = value


class Out:
    def __init__(self, shape, dtype):
        self.spec = (shape, dtype)


class KeptOut:
    def __init__(self, shape, dtype):
        self.spec = (shape, dtype)


class Arriving:
    def __init__(self, buffer, copy):
        self.buffer, self.copy, self.shape = buffer, copy, buffer.shape

    def wait(self):
        if self.copy is not None:
            self.copy.wait()
            self.copy = None

    def __getitem__(self, index):
        self.wait()
        return self.buffer[index]


class Leaving:
    def __init__(self, buffer, copy):
        self.buffer, self.copy, self.shape, self.dtype = buffer, copy, buffer.shape, buffer.dtype
        self.started = False

    def __setitem__(self, index, value):
        self.buffer[index] = value

    def __getitem__(self, index):
        return self.buffer[index]

    def flush(self):
        self.started = True
        self.copy.start()


MICROS = dict(
    project=1.0, norm_two_back=2.0, attend=3.7, norm_one=1.5, feed_forward=3.0, feed_far=2.4, feed_keep=2.5,
    place_col=1.0, heads=2.0, heads_keep=2.2, similar=1.8, dense=0.8, scores=3.0, feed_back=2.5,
    weight_grad=0.1, turned_grad=0.1, norm_one_back=1.9, attend_back=0.1, input_grad=0.1,
    place_wide=0.1, place_qk=0.1, place_last=0.1,
)


def call(body, name, ins, outs, scratch=(), semaphores=0, limit=8, alias=None):
    streams = [v.value for v in ins if isinstance(v, Stream)]
    leaving = [v.spec for v in outs if isinstance(v, Out)]
    values = [
        pltpu.with_memory_space_constraint(v.value, pltpu.HBM)
        if isinstance(v, (Stream, Kept))
        else v
        for v in ins
    ]

    def spec_of(v):
        if isinstance(v, (Stream, Kept, Out, KeptOut)):
            return pl.BlockSpec(memory_space=pltpu.HBM)
        if not isinstance(v, tuple) and v.ndim == 1 and v.dtype == I32:
            return pl.BlockSpec(memory_space=pltpu.SMEM)
        return pl.BlockSpec(memory_space=pltpu.VMEM)

    specs = [v.spec if isinstance(v, (Out, KeptOut)) else v for v in outs]
    sems = len(streams) + len(leaving) + semaphores

    def kernel(*refs):
        refs = list(refs)
        in_refs, refs = refs[: len(ins)], refs[len(ins) :]
        out_refs, refs = refs[: len(outs)], refs[len(outs) :]
        in_buffers, refs = refs[: len(streams)], refs[len(streams) :]
        out_buffers, refs = refs[: len(leaving)], refs[len(leaving) :]
        own, tail = refs[: len(scratch)], refs[len(scratch) :]
        place = 0
        args = []
        for v, ref in zip(ins, in_refs):
            if isinstance(v, Stream):
                copy = pltpu.make_async_copy(ref, in_buffers[place], tail[0].at[place])
                copy.start()
                ref = Arriving(in_buffers[place], copy)
                place += 1
            args.append(ref)
        results = []
        for v, ref in zip(outs, out_refs):
            if isinstance(v, Out):
                buffer = out_buffers[place - len(streams)]
                ref = Leaving(buffer, pltpu.make_async_copy(buffer, ref, tail[0].at[place]))
                place += 1
            results.append(ref)
        more = [tail[0].at[place + k] for k in range(semaphores)]
        body(*args, *results, *own, *more)
        for ref in args:
            if isinstance(ref, Arriving):
                ref.wait()
        sent = [ref for ref in results if isinstance(ref, Leaving)]
        for ref in sent:
            if not ref.started:
                ref.flush()
        for ref in sent:
            ref.copy.wait()

    shapes = [(v.shape, v.dtype) for v in streams] + leaving + list(scratch)
    scratch_shapes = [pltpu.VMEM(shape, dtype) for shape, dtype in shapes]
    if sems:
        scratch_shapes.append(pltpu.SemaphoreType.DMA((sems,)))
    return pl.pallas_call(
        kernel,
        in_specs=[spec_of(v) for v in ins],
        out_specs=[spec_of(v) for v in outs],
        out_shape=[
            (pltpu.HBM if isinstance(v, (Out, KeptOut)) else jax.ShapeDtypeStruct)(*spec)
            for v, spec in zip(outs, specs)
        ],
        scratch_shapes=scratch_shapes,
        compiler_params=pltpu.CompilerParams(vmem_limit_bytes=limit * MIB),
        cost_estimate=pl.CostEstimate(
            flops=int(MICROS[name] * 1e9), bytes_accessed=int(MICROS[name] * 1e6), transcendentals=0
        ),
        input_output_aliases=alias or {},
        name=name,
    )(*values)


def nn(left, right, precision=None):
    return lax.dot_general(
        left, right, (((1,), (0,)), ((), ())), precision=precision, preferred_element_type=F32
    )


def nt(left, right, precision=None):
    return lax.dot_general(
        left, right, (((1,), (1,)), ((), ())), precision=precision, preferred_element_type=F32
    )


def tn(left, right, precision=None):
    return lax.dot_general(
        left, right, (((0,), (0,)), ((), ())), precision=precision, preferred_element_type=F32
    )


def total(values):
    return jnp.sum(values, axis=0, keepdims=True)


def centre(values):
    return values - jnp.mean(values, axis=-1, keepdims=True)


def spread_of(centred):
    return lax.rsqrt(jnp.mean(centred * centred, axis=-1, keepdims=True) + EPS)


def norm_back(grad, normed, scale, gain):
    scaled = grad * gain
    mean_one = jnp.mean(scaled, axis=-1, keepdims=True)
    mean_two = jnp.mean(scaled * normed, axis=-1, keepdims=True)
    return scale * (scaled - mean_one - normed * mean_two)


def unit_rows(values):
    scale = lax.rsqrt(jnp.sum(values * values, axis=-1, keepdims=True) + NORM_EPS)
    return values * scale, scale


def unit_back(grad, unit, scale):
    return scale * (grad - unit * jnp.sum(grad * unit, axis=-1, keepdims=True))


def flagged(flag, shape):
    return (jnp.zeros(shape, I32) + flag) > 0


def project_body(first, second, weight, bias, query, key, value, *kept):
    count = first.shape[0]
    copies = []
    if kept:
        *kept, sem_one, sem_two = kept
        for source, out, sem in zip((first, second), kept, (sem_one, sem_two)):
            copy_out(copies, source, out, sem)
    for place, source in enumerate((first, second)):
        rows = slice(place * count, (place + 1) * count)
        block = source[...]
        query[rows, :] = (nn(block, weight[0]) + bias[0:1, :]).astype(BF)
        key[rows, :] = nn(block, weight[1]).astype(BF)
        value[rows, :] = (nn(block, weight[2]) + bias[1:2, :]).astype(BF)
    for copy in copies:
        copy.wait()


def head_masks(rows, heads):
    lanes = lax.broadcasted_iota(I32, rows.shape, 1) // HEAD_DIM
    return [jnp.where(lanes == head, rows, jnp.zeros_like(rows)) for head in range(heads)]


def allowed_pairs(seg_key, seg_query):
    return jnp.concatenate([seg_key] * (seg_query.shape[1] // LANES), axis=1) == seg_query


def attend_body(
    seg_key, seg_query, query, key_near, key_far, val_near, val_far,
    log_total, context_one, context_two, keys, values_t, context_t,
):
    half = key_near.shape[0]
    heads = query.shape[1] // HEAD_DIM
    keys[:half, :], keys[half:, :] = key_near[...], key_far[...]
    values_t[:, :half], values_t[:, half:] = val_near[...].T, val_far[...].T
    allowed = allowed_pairs(seg_key[...], seg_query[0:1, :])
    queries = head_masks(query[...] * BF(0.125), heads)

    def scores(head):
        return jnp.where(allowed, nt(keys[...], queries[head]), -1e30)

    current = scores(0)
    for head in range(heads):
        later = scores(head + 1) if head + 1 < heads else None
        rows = slice(head * HEAD_DIM, (head + 1) * HEAD_DIM)
        top = jnp.max(current, axis=0, keepdims=True)
        exp_terms = jnp.exp(current - top)
        norm = total(exp_terms)
        context_t[rows, :] = nn(values_t[rows, :], exp_terms.astype(BF)) * (1.0 / norm)
        log_total[head : head + 1, :] = top + jnp.log(norm)
        current = later
    log_total[heads:, :] = jnp.zeros((8 - heads, half), F32)
    log_total.flush()
    count = context_one.shape[0]
    context_one[...] = context_t[:, :count].T.astype(BF)
    context_two[...] = context_t[:, count:].T.astype(BF)


def attend_back_body(
    seg_key, seg_query, log_total, grad_one, grad_two, query, context_one, context_two,
    key_near, key_far, val_near, val_far, *refs, lanes, last,
):
    if last:
        key_before, value_before, gq, gk, gv, bias, keys, values, keys_t, grad_t = refs[:10]
        key_sum, value_sum, bias_before = refs[10], refs[11], None
    else:
        gq, key_sum, value_sum, bias, keys, values, keys_t, grad_t = refs
    half = key_near.shape[0]
    width = query.shape[1]
    heads = width // HEAD_DIM
    picked = (
        lax.broadcasted_iota(I32, (8, width), 1) // HEAD_DIM
        == lax.broadcasted_iota(I32, (8, width), 0)
    ).astype(F32)
    keys[:half, :], keys[half:, :] = key_near[...], key_far[...]
    values[:half, :], values[half:, :] = val_near[...], val_far[...]
    keys_t[...] = keys[...].T
    grad_context = jnp.concatenate(
        [grad[:, lane : lane + width] for grad, lane in zip((grad_one, grad_two), lanes)], axis=0
    )
    mixed = jnp.concatenate([context_one[...], context_two[...]], axis=0)
    allowed = allowed_pairs(seg_key[...], seg_query[0:1, :])
    dots = nt(picked, grad_context.astype(F32) * mixed.astype(F32), HIGH)
    queries = head_masks(query[...] * BF(0.125), heads)
    grad_heads = head_masks(grad_context, heads)

    def start(head):
        return nt(keys[...], queries[head]), nt(values[...], grad_heads[head])

    current = start(0)
    for head in range(heads):
        later = start(head + 1) if head + 1 < heads else None
        rows = slice(head * HEAD_DIM, (head + 1) * HEAD_DIM)
        raw, grad_probs = current
        probs = jnp.where(allowed, jnp.exp(raw - log_total[head : head + 1, :]), 0.0)
        grad_scores = (probs * (grad_probs - dots[head : head + 1, :])).astype(BF)
        add_v = nn(probs.astype(BF), grad_heads[head])
        add_k = nn(grad_scores, queries[head])
        if head:
            value_sum[...] += add_v
            key_sum[...] += add_k
        elif last:
            value_sum[...] = value_before[...] + add_v
            key_sum[...] = key_before[...] + add_k
        else:
            value_sum[...], key_sum[...] = add_v, add_k
        grad_t[rows, :] = nn(keys_t[rows, :], grad_scores)
        current = later
    grad_query = (grad_t[...].T * 0.125).astype(BF)
    gq[...] = grad_query
    bias[...] = jnp.zeros_like(bias)
    bias[0:1, :] = total(grad_query.astype(F32))
    if last:
        gk[...] = key_sum[...].astype(BF)
        grad_value = value_sum[...].astype(BF)
        gv[...] = grad_value
        bias[1:2, :] = total(grad_value.astype(F32))


def norm_one_body(
    tower, rows, mixed_0, mixed_1, mixed_2, mixed_3, w_0, w_1, w_2, w_3, w_2_more, w_3_more,
    b_out, gain, shift, hidden, centred,
):
    summed = rows[...].astype(F32) + b_out[...]
    summed = summed + nn(mixed_0[...], w_0[...]) + nn(mixed_1[...], w_1[...])
    here, there = lane_halves(tower, w_2)
    for mixed, weight, more in ((mixed_2, w_2, w_2_more), (mixed_3, w_3, w_3_more)):
        summed = summed + nn(mixed[:, here], weight[...]) + nn(mixed[:, there], more[...])
    middle = centre(summed)
    hidden[...] = (middle * spread_of(middle) * gain[...] + shift[...]).astype(BF)
    centred[...] = middle


def lane_halves(tower, part):
    size = part.shape[0]
    return (
        pl.ds(pl.multiple_of(tower[0] * size, size), size),
        pl.ds(pl.multiple_of((1 - tower[0]) * size, size), size),
    )


def gelu_pair(inner):
    cdf = 0.5 + 0.5 * lax.erf(inner * math.sqrt(0.5))
    density = jnp.exp(-0.5 * inner * inner) * (1.0 / math.sqrt(2.0 * math.pi))
    return (inner * cdf).astype(BF), (cdf + inner * density).astype(BF)


def ffn_body(
    first, second, w_up, b_up, w_down,
    active_one, active_two, slope_one, slope_two, part_one, part_two,
):
    inners = [nn(first[...], w_up[...]) + b_up[...]]
    inners.append(nn(second[...], w_up[...]) + b_up[...])
    places = ((active_one, slope_one, part_one), (active_two, slope_two, part_two))
    for inner, (active, slope, part) in zip(inners, places):
        act, active_slope = gelu_pair(inner)
        active[...] = act
        active.flush()
        slope[...] = active_slope
        slope.flush()
        part[...] = nn(act, w_down[...]).astype(BF)


def ffn_only_body(first, second, w_up, b_up, w_down, part_one, part_two):
    inners = [nn(second[...], w_up[...]) + b_up[...]]
    inners.append(nn(first[...], w_up[...]) + b_up[...])
    for inner, part in zip(inners, (part_two, part_one)):
        act = (inner * (0.5 + 0.5 * lax.erf(inner * math.sqrt(0.5)))).astype(BF)
        part[...] = nn(act, w_down[...]).astype(BF)


def ffn_keep_body(
    first, second, w_up, b_up,
    active_one, active_two, slope_one, slope_two, copy_one, copy_two,
):
    copy_one[...], copy_two[...] = first[...], second[...]
    copy_one.flush()
    copy_two.flush()
    for rows, active, slope in ((first, active_one, slope_one), (second, active_two, slope_two)):
        active[...], slope[...] = gelu_pair(nn(rows[...], w_up[...]) + b_up[...])
        active.flush()
        slope.flush()


def head_rows(centred, gain_one, shift_one, part, near, far, b_down, gain, shift):
    hidden = centred[...] * spread_of(centred[...]) * gain_one[...] + shift_one[...]
    summed = part[...].astype(F32) + near[...].astype(F32) + far[...].astype(F32)
    middle = centre(hidden + summed + b_down[...])
    return middle, middle * spread_of(middle) * gain[...] + shift[...]


def head_body(
    centred, gain_one, shift_one, part, near, far, b_down, gain, shift,
    col_weight, b_col, pick, cls_own, send, send_half,
):
    _, final = head_rows(centred, gain_one, shift_one, part, near, far, b_down, gain, shift)
    col, _ = unit_rows(nn(final.astype(BF), col_weight[...]) + b_col[...])
    cls, _ = unit_rows(nn(pick[...], final, HIGH))
    count = send_half.shape[0]
    col = col.astype(BF)
    cls_own[...] = jnp.concatenate([cls, jnp.zeros_like(cls)], axis=0).astype(BF)
    send[...] = col
    send_half[...] = col[count:]


def head_keep_body(
    centred, gain_one, shift_one, part, near, far, b_down, gain, shift,
    col_weight, b_col, pick, encoded, middle, col_pre, cls_raw,
):
    kept, final = head_rows(centred, gain_one, shift_one, part, near, far, b_down, gain, shift)
    middle[...] = kept
    middle.flush()
    encoded[...] = final.astype(BF)
    encoded.flush()
    col_pre[...] = nn(final.astype(BF), col_weight[...]) + b_col[...]
    col_pre.flush()
    cls_raw[...] = nn(pick[...], final, HIGH)


def similar_body(is_query, own, *refs):
    pieces, (weight_p, exp_terms, others, sums), sems = refs[:6], refs[6:10], refs[10:]
    count = own.shape[0]
    copies = []
    row = 0
    for piece, sem in zip(pieces, sems):
        rows = piece.shape[0]
        copy_out(copies, piece, others.at[pl.ds(row, rows)], sem)
        row += rows
    weight = weight_p[...].astype(BF)
    for copy in copies:
        copy.wait()
    terms = jnp.exp(SHARP * nt(own[...], others[...]))
    exp_terms[...] = terms
    high = terms.astype(BF)
    low = (terms - high.astype(F32)).astype(BF)
    sums_q = nt(weight, high) + nt(weight, low)
    sums_p = nn(weight[:, :count], high) + nn(weight[:, :count], low)
    sums_q = jnp.concatenate([sums_q, jnp.zeros((sums_q.shape[0], 3 * count), F32)], axis=1)
    sums[...] = jnp.where(flagged(is_query[0], sums_p.shape), sums_q, sums_p)


def dense_body(is_query, vectors, targets, cls_raw, grad_cls, loss):
    block = vectors[...]
    shape = (block.shape[0], block.shape[0])
    segs = cls_raw.shape[0]
    kind_rows = block.shape[0] // 2
    query_kind = 1 - is_query[0]
    row_kind = lax.broadcasted_iota(I32, shape, 0) // kind_rows
    col_kind = lax.broadcasted_iota(I32, shape, 1) // kind_rows
    paired = jnp.logical_and(row_kind == query_kind, col_kind != query_kind)
    logits = jnp.where(paired, nt(block, block) * SCALE_DENSE, -1e30)
    onehot = targets[...]
    top = jnp.max(logits, axis=1, keepdims=True)
    exp_terms = jnp.where(paired, jnp.exp(logits - top), 0.0)
    norm = jnp.sum(exp_terms, axis=1, keepdims=True)
    norm = jnp.where(norm > 0.0, norm, 1.0)
    grad = ((exp_terms / norm - onehot) * (1.0 / segs)).astype(BF)
    grad = jnp.where(paired, grad, jnp.zeros_like(grad))
    hit = jnp.sum(jnp.where(paired, logits * onehot, 0.0), axis=1, keepdims=True)
    losses = top + jnp.log(norm) - hit
    rows = lax.broadcasted_iota(I32, losses.shape, 0) - query_kind * kind_rows
    mine = jnp.logical_and(rows >= 0, rows < segs)
    loss[...] = jnp.zeros_like(loss) + jnp.sum(jnp.where(mine, losses, 0.0))
    grad_rows = nn(grad[: 2 * segs], block)[:segs]
    grad_cols = tn(grad[:, : 2 * segs], block)[:segs]
    own = jnp.where(flagged(is_query[0], grad_rows.shape), grad_rows, grad_cols) * SCALE_DENSE
    grad_cls[...] = unit_back(own, *unit_rows(cls_raw[...]))


def score_body(
    is_query, sums, exp_terms, others, weight_q, weight_p, target, col_pre,
    grad_pre, col_bias, loss, scores,
):
    count = exp_terms.shape[0]
    segs = weight_q.shape[0]
    seg_sums = sums[...]
    w_q, w_p = weight_q[...], weight_p[...]
    size = jnp.sum(w_q, axis=1, keepdims=True)
    nearest = jnp.log(seg_sums) * (1.0 / SHARP)
    pair = nt(w_q, nearest, HIGH) / size
    scores[...] = pair
    logits = pair * SCALE_COL
    onehot = target[...]
    top = jnp.max(logits, axis=1, keepdims=True)
    terms = jnp.exp(logits - top)
    norm = jnp.sum(terms, axis=1, keepdims=True)
    losses = top + jnp.log(norm) - jnp.sum(logits * onehot, axis=1, keepdims=True)
    loss[...] = jnp.zeros_like(loss) + jnp.sum(losses)
    grad_pair = (terms / norm - onehot) * (SCALE_COL / segs) / size
    grad_sums = tn(grad_pair, w_q, HIGH) / (SHARP * seg_sums)
    left = jnp.where(
        flagged(is_query[0], (segs, count)), grad_sums[:, :count], w_p[:, :count]
    )
    right = jnp.where(flagged(is_query[0], w_p.shape), w_p, grad_sums)
    grad_similar = (tn(left, right, HIGH) * (exp_terms[...] * SHARP)).astype(BF)
    grad_vec = nn(grad_similar, others[...])
    pre = unit_back(grad_vec, *unit_rows(col_pre[...])).astype(BF)
    grad_pre[...] = pre
    col_bias[...] = total(pre.astype(F32))


def norm_two_back_body(
    grad_pre, col_weight, grad_cls, pick, middle, gain, col_bias, col_loss, dense_loss,
    grad_two, grad_b, grad_kept, small,
):
    grad_final = nt(grad_pre[...], col_weight[...]) + tn(pick[...], grad_cls[...], HIGH)
    spread = spread_of(middle[...])
    unit = middle[...] * spread
    back = norm_back(grad_final, unit, spread, gain[...])
    grad_b[...] = back.astype(BF)
    grad_kept[...] = back.astype(BF)
    grad_kept.flush()
    grad_two[...] = back
    grad_two.flush()
    small[0:1, :] = col_bias[...]
    small[1:2, :] = total(back)
    small[2:3, :] = total(grad_final * unit)
    small[3:4, :] = total(grad_final)
    small[4:5, :] = jnp.zeros((1, unit.shape[1]), F32) + (col_loss[0:1, 0:1] + dense_loss[0:1, 0:1])
    small[5:8, :] = jnp.zeros((3, unit.shape[1]), F32)


def ffn_back_body(
    first, second, slope_one, slope_two, w_down, w_up,
    inner_one, inner_two, part_one, part_two, bias,
):
    bias_sum = jnp.zeros((1, slope_one.shape[1]), F32)
    raws = [nt(second[...], w_down[...]), nt(first[...], w_down[...])]
    for raw, slope, inner in zip(raws, (slope_two, slope_one), (inner_two, inner_one)):
        grad = (raw * slope[...].astype(F32)).astype(BF)
        inner[...] = grad
        inner.flush()
        bias_sum = bias_sum + total(grad.astype(F32))
    part_two[...] = nt(inner_two[...], w_up[...]).astype(BF)
    part_one[...] = nt(inner_one[...], w_up[...]).astype(BF)
    bias[...] = bias_sum


def norm_one_back_body(
    tower, grad_two, part, near, far, centred, gain, w_0, w_1, w_2, w_3, w_2_more, w_3_more,
    grad_one, grad_b, small, mixed_0, mixed_2, mixed_13,
):
    grad = (
        grad_two[...]
        + part[...].astype(F32)
        + near[...].astype(F32)
        + far[...].astype(F32)
    )
    spread = spread_of(centred[...])
    unit = centred[...] * spread
    back = norm_back(grad, unit, spread, gain[...])
    grad_one[...] = back
    grad_one.flush()
    rounded = back.astype(BF)
    grad_b[...] = rounded
    grad_b.flush()
    width = mixed_0.shape[1]
    size = w_2.shape[0]
    for weight, more, mixed, lane in (
        (w_3, w_3_more, mixed_13, width), (w_2, w_2_more, mixed_2, 0)
    ):
        for part, side in ((weight, tower[0]), (more, 1 - tower[0])):
            lanes = pl.ds(pl.multiple_of(side * size + lane, size), size)
            mixed[:, lanes] = nt(rounded, part[...]).astype(BF)
    mixed_13[:, :width] = nt(rounded, w_1[...]).astype(BF)
    mixed_0[...] = nt(rounded, w_0[...]).astype(BF)
    small[0:1, :] = total(back)
    small[1:2, :] = total(grad * unit)
    small[2:3, :] = total(grad)
    small[3:8, :] = jnp.zeros((5, unit.shape[1]), F32)


def input_grad_body(
    query_near, query_far, grad_key, grad_value, weight, part_0, part_2, part_31
):
    count = part_0.shape[0]
    places = ((3, part_31, 0), (1, part_31, count), (2, part_2, 0), (0, part_0, 0))
    for block, out, row in places:
        own = slice(block % 2 * count, (block % 2 + 1) * count)
        rows = slice(block * count, (block + 1) * count)
        out[row : row + count, :] = (
            nt((query_near, query_far)[block // 2][own, :], weight[0])
            + nt(grad_key[rows, :], weight[1])
            + nt(grad_value[rows, :], weight[2])
        ).astype(BF)


def order_rows(place, source, out, size):
    for block in range(source.shape[1] // size):
        start = pl.multiple_of((jnp.int32(block) ^ place) * size, size)
        out[block * size : (block + 1) * size, :] = source[:, pl.ds(start, size)].T


def weight_grad_body(place, *refs, lefts, rights, cuts):
    left = refs[:lefts]
    right = refs[lefts : lefts + sum(rights)]
    outs, (ordered, joined) = refs[lefts + sum(rights) : -2], refs[-2:]
    token = 0
    for part in left:
        tokens = slice(token, token + part.shape[0])
        order_rows(place[0], part, ordered.at[:, tokens], LANES)
        token += part.shape[0]
    at = 0
    lane = 0
    for group in rights:
        token = 0
        for part in right[at : at + group]:
            rows, lanes = part.shape
            joined[token : token + rows, lane : lane + lanes] = part[...]
            token += rows
        at += group
        lane += lanes
    half = ordered.shape[0] // 2
    lane = 0
    for cut, (keep, send) in zip(cuts, zip(outs[::2], outs[1::2])):
        lanes = slice(lane, lane + cut)
        for rows, out in ((slice(half, 2 * half), send), (slice(0, half), keep)):
            out[...] = nn(ordered[rows, :], joined[:, lanes]).astype(BF)
            if isinstance(out, Leaving):
                out.flush()
        lane += cut


def turned_grad_body(place, mp_place, grad, *refs, rows):
    left, (part_0, part_2, part_31, ordered) = refs[:-4], refs[-4:]
    order_rows(place[0], grad, ordered, LANES)
    outs = ((0, part_0, 0), (2, part_2, 0), (3, part_31, 0), (1, part_31, rows))
    for block, out, lane in outs:
        if len(left) == 1:
            start = pl.multiple_of((jnp.int32(block) ^ mp_place[0]) * rows, rows)
            right = left[0][:, pl.ds(start, rows)]
        else:
            right = left[block][...]
        out[:, lane : lane + rows] = nn(ordered[...], right).astype(BF)
        if isinstance(out, Leaving):
            out.flush()


def place_col_body(mp_place, tower, w_0, w_1, w_2, w_3, w_2_more, w_3_more, out):
    count = w_0.shape[0]
    here, there = lane_halves(tower, w_2)
    for block, parts in enumerate(((w_0,), (w_1,), (w_2, w_2_more), (w_3, w_3_more))):
        start = pl.multiple_of((jnp.int32(block) ^ mp_place[0]) * count, count)
        if len(parts) == 1:
            out[pl.ds(start, count), :] = parts[0][...]
        else:
            size = parts[0].shape[0]
            out[pl.ds(pl.multiple_of(start + tower[0] * size, size), size), :] = parts[0][...]
            out[pl.ds(pl.multiple_of(start + (1 - tower[0]) * size, size), size), :] = parts[1][...]


def copy_out(copies, source, target, sem):
    copies.append(pltpu.make_async_copy(source, target, sem))
    copies[-1].start()


def place_wide_body(place, *refs, size):
    parts, (out, buffer), sems = refs[:4], refs[4:6], refs[6:]
    copies = []
    cut = parts[0].shape[1]
    for block in range(8):
        here = pl.ds(block * size, size)
        start = pl.multiple_of((jnp.int32(block) ^ place[0]) * size, size)
        row = block % 4 * size
        for column in range(2):
            part = parts[2 * column + block // 4]
            lanes = slice(column * cut, (column + 1) * cut)
            buffer[here, lanes] = part[row : row + size, :].astype(F32)
        copy_out(copies, buffer.at[here], out.at[pl.ds(start, size)], sems[block])
    for copy in copies:
        copy.wait()


def place_qk_body(place, one, one_more, qkv, buffer, *sems, size):
    copies = []
    width = qkv.shape[2]
    for block in range(8):
        here = pl.ds(block * size, size)
        start = pl.multiple_of((jnp.int32(block) ^ place[0]) * size, size)
        rows = slice(block % 4 * size, (block % 4 + 1) * size)
        part = (one, one_more)[block // 4]
        for kind in range(2):
            lanes = slice(kind * width, (kind + 1) * width)
            buffer[kind, here, :] = part[rows, lanes].astype(F32)
            copy_out(
                copies,
                buffer.at[kind, here],
                qkv.at[kind, pl.ds(start, size)],
                sems[2 * block + kind],
            )
    for copy in copies:
        copy.wait()


def place_last_body(place, one, one_more, before, qkv, out, col, buffer, *sems, size):
    copies = []
    width = qkv.shape[2]
    for block in range(8):
        here = pl.ds(block * size, size)
        start = pl.multiple_of((jnp.int32(block) ^ place[0]) * size, size)
        rows = slice(block % 4 * size, (block % 4 + 1) * size)
        part = (one, one_more)[block // 4]
        buffer[here, :] = part[rows, :width].astype(F32)
        copy_out(copies, buffer.at[here], qkv.at[2, pl.ds(start, size)], sems[block])
        out[:, pl.ds(start, size)] = part[rows, width : 2 * width].astype(F32).T
        col[:, pl.ds(start, size)] = part[rows, 2 * width :].astype(F32).T
    out.flush()
    col.flush()
    for copy in copies:
        copy.wait()


def dp_bits():
    return [1 << k for k in range(int(math.log2(lax.axis_size("dp"))))]


def add(*values):
    return sum(value.astype(F32) for value in values).astype(BF)


def side_of(axis, bit):
    return jnp.minimum(lax.axis_index(axis) & bit, 1)


def join(value, other, axis, bit):
    return jnp.where(
        side_of(axis, bit) == 0,
        jnp.concatenate([value, other]),
        jnp.concatenate([other, value]),
    )


def more_bits():
    return [("dp", bit) for bit in dp_bits()[2:]]


def sum_more(value):
    for axis, bit in more_bits():
        half = value.shape[0] // 2
        side = side_of(axis, bit)
        sent = lax.dynamic_slice_in_dim(value, (1 - side) * half, half, 0)
        kept = lax.dynamic_slice_in_dim(value, side * half, half, 0)
        value = add(kept, swap(sent, axis, bit))
    for axis, bit in more_bits()[::-1]:
        value = join(value, swap(value, axis, bit), axis, bit)
    return value


HOPS = (("tower", 1), ("dp", 1), ("dp", 2))


class Unit:
    def __init__(self, keep, send):
        self.value, self.send, self.stage = keep, send, 0

    def hop(self):
        return HOPS[min(self.stage, 5 - self.stage)]

    def land(self, got):
        self.stage += 1
        if self.stage <= 3:
            value = self.value.astype(F32) + got.astype(F32)
            if self.stage < 3:
                half = value.shape[0] // 2
                self.value, self.send = value[:half], value[half:].astype(BF)
            else:
                self.send = sum_more(value.astype(BF))
        elif self.stage < 6:
            self.send = jnp.concatenate([self.send, got])
        else:
            self.halves = (self.send, got)


class Small:
    def __init__(self, value):
        self.send, self.stage = value, 0

    def hop(self):
        return HOPS[self.stage]

    def land(self, got):
        self.stage += 1
        self.send = self.send + got
        if self.stage == 3:
            for axis, bit in more_bits():
                self.send = self.send + swap(self.send, axis, bit)


def together(*values):
    return lax.optimization_barrier(values)


def phase(units=(), moves=(), fill=None, alone=(), then=None):
    groups = {}
    for unit in units:
        groups.setdefault((unit.hop(), unit.send.dtype), []).append(unit)
    groups = list(groups.values()) + [[unit] for unit in alone]
    sends = [
        group[0].send
        if len(group) == 1
        else jnp.concatenate([unit.send for unit in group], axis=1)
        for group in groups
    ]
    ready = [value for value, _ in moves] + sends[: len(groups) - len(alone)]
    flights = [swap(value, *hop) for value, hop in moves]
    flights += [swap(send, *group[0].hop()) for send, group in zip(sends, groups)]
    filled = list(fill(lambda value: after(value, *ready))) if fill else []
    more = then(filled) if then else []
    groups += [[unit] for unit in more]
    flights += [swap(unit.send, *unit.hop()) for unit in more]
    sizes = [value.size * value.dtype.itemsize for value in flights]
    soon = [k for k, size in enumerate(sizes) if size < max(sizes)]
    done = together(*[flights[k] for k in soon], *filled)
    rest = [k for k in range(len(flights)) if k not in soon]
    done = together(*done, *[flights[k] for k in rest])
    landed = [None] * len(flights)
    for k, value in zip(soon, done):
        landed[k] = value
    for k, value in zip(rest, done[len(soon) + len(filled) :]):
        landed[k] = value
    for group, got in zip(groups, landed[len(moves) :]):
        lane = 0
        for unit in group:
            width = unit.send.shape[1]
            unit.land(got if len(group) == 1 else got[:, lane : lane + width])
            lane += width
    return landed[: len(moves)], done[len(soon) : len(soon) + len(filled)], more


def place_of(hops):
    place = 0
    for axis, bit in hops:
        place = place * 2 + side_of(axis, bit)
    return place[None].astype(I32)


def relative(values, mp_index):
    size = values.shape[-1] // 4
    blocks = [values[..., k * size : (k + 1) * size] for k in range(4)]
    values = jnp.where(mp_index & 1, jnp.concatenate([blocks[k ^ 1] for k in range(4)], -1), values)
    blocks = [values[..., k * size : (k + 1) * size] for k in range(4)]
    return jnp.where(mp_index & 2, jnp.concatenate([blocks[k ^ 2] for k in range(4)], -1), values)


def flip(values, bit):
    size = values.shape[-1] // 4
    return jnp.concatenate([values[:, (k ^ bit) * size :][:, :size] for k in range(4)], axis=1)


def per_device(
    tokens,
    segment_ids,
    key_mask,
    positives,
    w_qkv,
    b_qv,
    w_out,
    b_out,
    gain_one,
    shift_one,
    w_up,
    b_up,
    w_down,
    b_down,
    gain_two,
    shift_two,
    w_col,
    b_col,
):
    own_rows = tokens[0, 0]
    count, model_dim = own_rows.shape
    pair, width = 2 * count, w_out.shape[0]
    half = count // 2
    units = w_up.shape[1]
    segs = positives.shape[1]
    dp_size = lax.axis_size("dp")
    mp_index = lax.axis_index("mp")
    dp_index = lax.axis_index("dp")
    tower = lax.axis_index("tower")
    is_query = tower == 0
    query_flag = (1 - tower)[None].astype(I32)
    mp_place = mp_index[None].astype(I32)
    rest_place = place_of(HOPS)
    tower_place = tower[None].astype(I32)
    labels = jnp.arange(segs, dtype=I32)
    row = lambda vector: vector[None, :]
    block_bf = ((count, model_dim), BF)
    block_f32 = ((count, model_dim), F32)

    def core(block):
        return swap(block, "mp", 1)

    def across(block):
        return swap(block, "mp", 2)

    x_0, x_1, x_2 = own_rows, core(own_rows), across(own_rows)
    w_three = jnp.transpose(w_qkv, (1, 0, 2))

    seg_pair = segment_ids[:, 0]
    starts = jnp.concatenate([jnp.ones((2, 1), bool), seg_pair[:, 1:] != seg_pair[:, :-1]], axis=1)
    valid_pair = jnp.logical_or(key_mask[:, 0] > 0, starts)
    codes = relative(seg_pair + 16 * valid_pair.astype(I32) + 32 * starts.astype(I32), mp_index)
    seg_rel, valid_rel = codes & 15, (codes & 16) > 0
    code_row = jnp.where(is_query, codes[0], codes[1])
    seg_row = code_row & 15
    seg_key = jnp.broadcast_to(
        jnp.where((code_row & 16) > 0, seg_row, -1)[:, None], (4 * count, LANES)
    )
    seg_query = jnp.broadcast_to(seg_row[None, :], (8, 4 * count))
    members = seg_rel[:, None, :] == labels[None, :, None]
    weights = jnp.logical_and(members, valid_rel[:, None, :]).astype(F32)
    weight_q, weight_p = weights[0], weights[1]
    pick = (code_row[None, :count] - 32 == labels[:, None] + 16).astype(F32)
    order = dp_index ^ jnp.arange(dp_size, dtype=I32)
    kinds = jnp.arange(2, dtype=I32)[:, None, None]
    targets = (
        (1 - tower) * dp_size * segs
        + jnp.arange(dp_size, dtype=I32)[None, :, None] * segs
        + positives[order][None]
    )
    targets = jnp.where(kinds == tower, targets, -1).reshape(2 * dp_size * segs)
    paired = (targets[:, None] == jnp.arange(2 * dp_size * segs, dtype=I32)).astype(F32)
    positive_row = lax.dynamic_index_in_dim(positives, dp_index, 0, keepdims=False)
    positive_row = (positive_row[:, None] == labels).astype(F32)

    half_bf = ((pair, width), BF)
    mixed_bf = ((count, width), BF)
    x_hop, core_hop, y_hop = ("mp", 2), ("mp", 1), ("tower", 1)

    def project(first, second, kept=()):
        return call(
            project_body,
            "project",
            [first, second, w_three, b_qv],
            [half_bf] * 3 + list(kept),
            semaphores=len(kept),
        )

    near_qkv = project(x_0, x_1)
    halves = [
        lax.dynamic_slice_in_dim(weight, tower * half, half, 0) for weight in (w_out, w_col)
    ]
    x_2, out_half, col_half, out_1, col_1 = together(
        x_2, *halves, core(w_out), core(w_col), near_qkv,
        seg_key, seg_query, weight_q, weight_p, pick, paired, positive_row,
    )[:5]
    x_3 = core(x_2)
    out_2, col_2 = across(out_half), across(col_half)
    far_qkv = project(x_2, x_3, [KeptOut(*block_bf)] * 2)
    x_2_kept, x_3_kept = far_qkv[3:]
    key_values = [near_qkv[1], far_qkv[1], near_qkv[2], far_qkv[2]]
    seg_query_near, seg_query_far = seg_query[:, :pair], seg_query[:, pair:]

    def attend(seg_half, query):
        return call(
            attend_body,
            "attend",
            [seg_key, seg_half, query, *key_values],
            [Out((8, pair), F32), mixed_bf, mixed_bf],
            [((4 * count, width), BF), ((width, 4 * count), BF), ((width, pair), F32)],
        )

    total_far, mixed_far_2, mixed_far_3 = attend(seg_query_far, far_qkv[0])
    mixed_far_2, mixed_far_3, out_2 = together(mixed_far_2, mixed_far_3, out_2)
    (out_2_more, mixed_2, mixed_1_2), (total_near, mixed_0, mixed_near_1, col_2), _ = phase(
        (),
        [(out_2, y_hop), (mixed_far_2, x_hop), (mixed_far_3, x_hop)],
        lambda late: [*attend(seg_query_near, late(near_qkv[0])), col_2],
    )
    (mixed_1, mixed_3, out_3, out_3_more), _, _ = phase(
        (),
        [(mixed_near_1, core_hop), (mixed_1_2, core_hop), (out_2, core_hop)]
        + [(out_2_more, core_hop)],
    )
    col_3 = core(col_2)
    mixed = [mixed_0, mixed_1, mixed_2, mixed_3]
    outs = [w_out, out_1, out_2, out_3, out_2_more, out_3_more]
    hidden, centred_one = call(
        norm_one_body,
        "norm_one",
        [tower_place, own_rows, *mixed, *outs, row(b_out), row(gain_one), row(shift_one)],
        [block_bf, block_f32],
    )

    h_0, h_1 = hidden, core(hidden)
    kept_bf = Out((count, units), BF)
    (h_2, col_2_more), (act_0, act_1, slope_0, slope_1, part_0, part_1), _ = phase(
        (),
        [(hidden, x_hop), (col_2, y_hop)],
        lambda late: call(
            ffn_body,
            "feed_forward",
            [h_0, h_1, w_up, row(b_up), w_down],
            [kept_bf] * 4 + [Out(*block_bf), block_bf],
        ),
    )
    h_3, col_3_more = core(h_2), core(col_2_more)
    part_2, part_3 = call(
        ffn_only_body, "feed_far", [h_2, h_3, w_up, row(b_up), w_down], [block_bf] * 2
    )
    near_sum = core(part_1)
    joined = add(part_2, core(part_3))
    joined, near_sum = together(joined, near_sum)
    (arrived,), (act_2, act_3, slope_2, slope_3, h_2_kept, h_3_kept, col_weight), _ = phase(
        (),
        [(joined, x_hop)],
        lambda late: [
            *call(
                ffn_keep_body,
                "feed_keep",
                [late(h_2), h_3, w_up, row(b_up)],
                [kept_bf] * 4 + [Out(*block_bf)] * 2,
            ),
            *call(
                place_col_body,
                "place_col",
                [mp_place, tower_place, w_col, late(col_1), col_2, col_3, col_2_more, col_3_more],
                [((model_dim, model_dim), BF)],
            ),
        ],
    )
    ins = [centred_one, row(gain_one), row(shift_one), part_0, near_sum, arrived]
    ins += [row(b_down), row(gain_two), row(shift_two), col_weight, row(b_col), pick]
    cls_own, send, send_half = call(
        head_body,
        "heads",
        ins,
        [((2 * segs, model_dim), BF), block_bf, ((half, model_dim), BF)],
    )

    cls_own = cls_own[:segs]
    (other, own_half, cls_far), (encoded, middle, col_pre, cls_raw), _ = phase(
        (),
        [(send, y_hop), (send_half, x_hop), (cls_own, ("dp", 1))],
        lambda late: call(
            head_keep_body,
            "heads_keep",
            [late(centred_one)] + ins[1:],
            [Out(*block_bf), Out(*block_f32), Out(*block_f32), Out((segs, model_dim), F32)],
        ),
    )
    cls_all = jnp.concatenate([cls_own, cls_far])
    (far_b, far_a, cls_far), _, _ = phase(
        (), [(own_half, y_hop), (other[:half], x_hop), (cls_all, ("dp", 2))]
    )
    cls_all = jnp.concatenate([cls_all, cls_far])
    for bit in dp_bits()[2:]:
        cls_all = jnp.concatenate([cls_all, swap(cls_all, "dp", bit)])
    (near, diag_a, diag_b, cls_near), _, _ = phase(
        (),
        [(other, core_hop), (far_a, core_hop), (far_b, core_hop), (cls_all, core_hop)],
    )
    cls_all = add(cls_all, cls_near)
    pieces = [other, near, far_a, far_b, diag_a, diag_b]
    exp_terms, others, sums = call(
        similar_body,
        "similar",
        [query_flag, send, *map(Kept, pieces), weight_p],
        [((count, 4 * count), F32), ((4 * count, model_dim), BF), ((segs, 4 * count), F32)],
        semaphores=6,
    )
    cls_all = after(cls_all, sums)
    (swapped, cls_far), _, _ = phase((), [(sums, x_hop), (cls_all, x_hop)])
    sums = sums + flip(swapped, 2)
    cls_all = add(cls_all, cls_far)
    (swapped,), _, _ = phase((), [(sums, core_hop)])
    sums = sums + flip(swapped, 1)
    (cls_other,), (grad_pre, col_bias, col_loss, pair_score), _ = phase(
        (),
        [(after(cls_all, sums), y_hop)],
        lambda late: call(
            score_body,
            "scores",
            [query_flag, late(sums), exp_terms, others, weight_q, weight_p, positive_row, col_pre],
            [block_bf, ((1, model_dim), F32), ((8, LANES), F32), ((segs, segs), F32)],
        ),
    )
    grad_cls, dense_loss = call(
        dense_body,
        "dense",
        [query_flag, jnp.concatenate([cls_all, cls_other]), paired, cls_raw],
        [((segs, model_dim), F32), ((8, LANES), F32)],
    )
    grad_two, grad_two_b, grad_two_kept, small_two = call(
        norm_two_back_body,
        "norm_two_back",
        [grad_pre, col_weight, grad_cls, pick, middle, row(gain_two)]
        + [col_bias, col_loss, dense_loss],
        [Out(*block_f32), block_bf, Out(*block_bf), ((8, model_dim), F32)],
    )

    def feed_back(first, second, slope_one, slope_two, part):
        return call(
            ffn_back_body,
            "feed_back",
            [first, second, slope_one, slope_two, w_down, w_up],
            [kept_bf] * 2 + [part, block_bf, ((1, units), F32)],
        )

    def streams(*values):
        return [Stream(value) for value in values]

    def weight_grad(left, right, cuts):
        rows = left[0].value.shape[1]
        tokens = 4 * count
        outs = [Out((rows // 2, cut), BF) for cut in cuts for _ in range(2)]
        outs[1] = ((rows // 2, cuts[0]), BF)
        return call(
            functools.partial(
                weight_grad_body,
                lefts=len(left),
                rights=[len(parts) for parts in right],
                cuts=cuts,
            ),
            "weight_grad",
            [rest_place, *left, *[part for parts in right for part in parts]],
            outs,
            [((rows, tokens), BF), ((tokens, sum(cuts)), BF)],
            limit=20,
        )

    def turned_grad(grad, left):
        return call(
            functools.partial(turned_grad_body, rows=count),
            "turned_grad",
            [rest_place, mp_place, grad, *left],
            [Out((model_dim, count), BF)] * 2 + [((model_dim, 2 * count), BF)],
            [((model_dim, count), BF)],
        )

    def near_back(late):
        backs = feed_back(grad_two_b, g_1, slope_0, slope_1, Out(*block_bf))
        return [*backs, *turned_grad(Stream(after(grad_pre, backs[3])), [Stream(encoded)])]

    g_1 = core(grad_two_b)
    (g_2,), (inner_0, inner_1, part_0, part_1, bias_near, *col_parts), _ = phase(
        (), [(grad_two_b, x_hop)], near_back
    )
    g_3 = core(g_2)
    inner_2, inner_3, part_2, part_3, bias_far = feed_back(g_2, g_3, slope_2, slope_3, block_bf)
    cut = model_dim // 2
    (near_sum, arrived), down, _ = phase(
        (),
        [(part_1, core_hop), (part_3, core_hop)],
        lambda late: weight_grad(
            streams(act_0, act_1, act_2, act_3),
            [[Stream(grad_two_kept), Stream(g_1), late(g_2), g_3]],
            [cut, cut],
        ),
    )
    down = [Unit(*down[:2]), Unit(*down[2:])]
    joined = add(part_2, arrived)
    (arrived, col_near), up, _ = phase(
        down[:1],
        [(joined, x_hop), (col_parts[2], core_hop)],
        lambda late: weight_grad(
            streams(late(h_0), h_1, h_2_kept, h_3_kept),
            [streams(inner_0, inner_1, inner_2, inner_3)],
            [cut, cut],
        ),
    )
    up = [Unit(*up[:2]), Unit(*up[2:])]
    col_joined = add(col_parts[1], col_near[:, :count])
    col_own = add(col_parts[0], col_near[:, count:])
    grad_one, grad_one_b, small_one, back_0, back_2, back_13 = call(
        norm_one_back_body,
        "norm_one_back",
        [tower_place, grad_two, part_0, near_sum, arrived, centred_one, row(gain_one), *outs],
        [Out(*block_f32), Out(*block_bf), ((8, model_dim), F32)]
        + [mixed_bf, mixed_bf, ((count, 2 * width), BF)],
        limit=12,
    )

    back_13 = core(back_13)
    back_23 = jnp.concatenate([back_2, back_13[:, width:]], axis=1)
    all_bf, all_f32 = ((4 * count, width), BF), ((4 * count, width), F32)
    back_scratch = [all_bf] * 2 + [((width, 4 * count), BF), ((width, pair), F32)]

    def back_ins(seg_half, log_total, grads, query, mixed_pair):
        return streams(seg_key, seg_half, log_total) + grads + streams(
            query, *mixed_pair, *key_values
        )

    def near_rows(late):
        backs = call(
            functools.partial(attend_back_body, lanes=(0, 0), last=False),
            "attend_back",
            back_ins(
                seg_query_near,
                total_near,
                [late(back_0), back_13],
                near_qkv[0],
                (mixed_0, mixed_near_1),
            ),
            [half_bf, all_f32, all_f32, ((8, width), F32)],
            back_scratch,
            limit=16,
        )
        return [*backs, *turned_grad(Stream(after(grad_one_b, backs[0])), streams(*mixed))]

    small = jnp.concatenate([small_two, small_one])
    (back_23, small_far), (grad_q_near, key_sum, value_sum, bias_near_q, *out_parts), _ = phase(
        [down[0], up[0]], [(back_23, x_hop), (small, x_hop)], near_rows, alone=[down[1]]
    )
    small = small + small_far
    (col_far, out_near), (grad_q_far, grad_k, grad_v, bias_far_v), _ = phase(
        [up[1], up[0], down[1], down[0]],
        [(col_joined, x_hop), (out_parts[2], core_hop)],
        lambda late: call(
            functools.partial(attend_back_body, lanes=(0, width), last=True),
            "attend_back",
            back_ins(
                seg_query_far,
                total_far,
                [late(back_23), back_23],
                far_qkv[0],
                (mixed_far_2, mixed_far_3),
            )
            + [key_sum, value_sum],
            [half_bf, all_bf, all_bf, ((8, width), F32)],
            back_scratch + [all_f32, all_f32],
            limit=16,
        ),
    )
    out_joined = add(out_parts[1], out_near[:, :count])
    out_own = add(out_parts[0], out_near[:, count:])

    def own_grads(late):
        qkv = weight_grad(
            streams(late(x_0), x_1, x_2_kept, x_3_kept),
            [streams(grad_q_near, grad_q_far), streams(grad_k), streams(grad_v)],
            [2 * width, width],
        )
        grad_x = call(
            input_grad_body,
            "input_grad",
            streams(after(grad_q_near, qkv[1]), grad_q_far, grad_k, grad_v, w_three),
            [Out(*block_bf)] * 2 + [((pair, model_dim), BF)],
        )
        return [*qkv, *grad_x]

    (out_far, small_near), (_, _, keep_2, send_2, part_0, part_2, part_31), rest = phase(
        [up[1], up[0], down[1], down[0]],
        [(out_joined, x_hop), (small, core_hop)],
        own_grads,
        then=lambda filled: [Unit(*filled[:2])],
    )
    bias_v = (bias_far_v + bias_near_q)[:2].reshape(1, 2 * width)
    small = Small(
        jnp.concatenate(
            [
                small + small_near,
                bias_near + bias_far,
                jnp.concatenate([bias_v, jnp.zeros((1, model_dim - 2 * width), F32)], axis=1),
            ]
        )
    )
    out_t = add(out_own, out_far)
    col_t = add(col_own, col_far)
    rows = model_dim // 2
    rest.append(
        Unit(
            *(
                jnp.concatenate([value, out_t[side], col_t[side]], axis=1)
                for value, side in ((keep_2, slice(0, rows)), (send_2, slice(rows, None)))
            )
        )
    )
    (part_31,), _, _ = phase(
        [rest[1], rest[0], down[0], up[1], up[0], down[1], small], [(part_31, core_hop)]
    )
    joined = add(part_2, part_31[:count])
    (arrived,), _, _ = phase(
        [down[0], rest[1], up[0], down[1], rest[0], up[1], small], [(joined, x_hop)]
    )
    grad_input = (
        grad_one
        + part_0.astype(F32)
        + part_31[count:].astype(F32)
        + arrived.astype(F32)
    )
    d_tokens = grad_input.astype(BF).reshape(1, 1, count, model_dim)
    _, (d_tokens,), _ = phase(
        [up[0], down[1], up[1], rest[1], rest[0], small], fill=lambda late: [d_tokens]
    )

    def place_wide(late, first, second):
        halves = [late(first.halves[0]), first.halves[1], *second.halves]
        shape = (model_dim, 2 * halves[0].shape[1])
        return call(
            functools.partial(place_wide_body, size=model_dim // 8),
            "place_wide",
            [rest_place, *streams(*halves)],
            [KeptOut(shape, F32)],
            [(shape, F32)],
            semaphores=8,
        )

    _, (grad_down,), _ = phase(
        [up[1], rest[0], rest[1]], fill=lambda late: place_wide(late, *down)
    )
    _, (grad_up,), _ = phase([rest[0], rest[1]], fill=lambda late: place_wide(late, *up))
    _, (grad_qkv,), _ = phase(
        [rest[1]],
        fill=lambda late: call(
            functools.partial(place_qk_body, size=model_dim // 8),
            "place_qk",
            [rest_place, *streams(late(rest[0].halves[0]), rest[0].halves[1])],
            [KeptOut((3, model_dim, width), F32)],
            [((2, model_dim, width), F32)],
            semaphores=16,
        ),
    )
    grad_qkv, grad_out, grad_col = call(
        functools.partial(place_last_body, size=model_dim // 8),
        "place_last",
        [rest_place, *streams(*rest[1].halves), Kept(grad_qkv)],
        [KeptOut((3, model_dim, width), F32)] + [Out((width, model_dim), F32)] * 2,
        [((model_dim, width), F32)],
        semaphores=8,
        alias={3: 0},
    )
    small = small.send
    loss = small[4, 0] * (1.0 / (segs * 2 * lax.axis_size("mp")))
    return (
        encoded.reshape(1, 1, count, model_dim),
        loss,
        pair_score.reshape(1, segs, segs),
        d_tokens,
        jnp.transpose(grad_qkv, (1, 0, 2)),
        small[17, : 2 * width].reshape(2, width),
        grad_out,
        small[8],
        small[9],
        small[10],
        grad_up,
        small[16],
        grad_down,
        small[1],
        small[2],
        small[3],
        grad_col,
        small[0],
    )


def solution(mesh):
    return jax.shard_map(
        per_device,
        mesh=mesh,
        in_specs=(
            P("tower", "dp", "mp", None),
            P(None, "dp", None),
            P(None, "dp", None),
            P(),
            P(None, None, "mp"),
            P(None, "mp"),
            P("mp", None),
            P(),
            P(),
            P(),
            P(None, "mp"),
            P("mp"),
            P("mp", None),
            P(),
            P(),
            P(),
            P("mp", None),
            P(),
        ),
        out_specs=(
            P("tower", "dp", "mp", None),
            P(),
            P("dp", None, None),
            P("tower", "dp", "mp", None),
            P(None, None, "mp"),
            P(None, "mp"),
            P("mp", None),
            P(),
            P(),
            P(),
            P(None, "mp"),
            P("mp"),
            P("mp", None),
            P(),
            P(),
            P(),
            P("mp", None),
            P(),
        ),
        check_vma=False,
    )
```

```python
import functools
import math

import jax
import jax.numpy as jnp
from jax import lax
from jax.experimental import pallas as pl
from jax.experimental.pallas import tpu as pltpu
from jax.sharding import PartitionSpec as P

HEAD_DIM = 64
EPS = 1e-05
NORM_EPS = 1e-06
SCALE_DENSE = 50.0
SCALE_COL = 50.0
SHARP = 20.0
HIGH = lax.Precision.HIGHEST
BF = jnp.bfloat16
F32 = jnp.float32
I32 = jnp.int32
LANES = 128
MIB = 1 << 20


def swap(block, axis, bit):
    count = lax.axis_size(axis)
    return lax.ppermute(block, axis, [(low, low ^ bit) for low in range(count)])


def after(value, *first):
    return lax.optimization_barrier((value,) + first)[0]


class Stream:
    def __init__(self, value):
        self.value = value


class Kept:
    def __init__(self, value):
        self.value = value


class Out:
    def __init__(self, shape, dtype):
        self.spec = (shape, dtype)


class KeptOut:
    def __init__(self, shape, dtype):
        self.spec = (shape, dtype)


class Arriving:
    def __init__(self, buffer, copy):
        self.buffer, self.copy, self.shape = buffer, copy, buffer.shape

    def wait(self):
        if self.copy is not None:
            self.copy.wait()
            self.copy = None

    def __getitem__(self, index):
        self.wait()
        return self.buffer[index]


class Leaving:
    def __init__(self, buffer, copy):
        self.buffer, self.copy, self.shape, self.dtype = buffer, copy, buffer.shape, buffer.dtype
        self.started = False

    def __setitem__(self, index, value):
        self.buffer[index] = value

    def __getitem__(self, index):
        return self.buffer[index]

    def flush(self):
        self.started = True
        self.copy.start()


MICROS = dict(
    project=1.0, norm_two_back=2.0, norm_two_keep=0.1, attend=3.7, norm_one=1.5, feed_forward=3.0, feed_far=1.3, feed_keep=2.5,
    place_col=1.0, heads=2.0, heads_keep=2.2, similar=1.8, dense=0.8, scores=3.0, feed_back=2.5, feed_back_far=1.3, feed_back_keep=0.1,
    weight_grad=0.1, turned_grad=0.1, norm_one_back=0.1, attend_back=0.1, input_grad=0.1,
    place_wide=0.1, place_qkv=0.1, place_last=0.1,
)


def call(body, name, ins, outs, scratch=(), semaphores=0, limit=8, alias=None):
    streams = [v.value for v in ins if isinstance(v, Stream)]
    leaving = [v.spec for v in outs if isinstance(v, Out)]
    values = [
        pltpu.with_memory_space_constraint(v.value, pltpu.HBM)
        if isinstance(v, (Stream, Kept))
        else v
        for v in ins
    ]

    def spec_of(v):
        if isinstance(v, (Stream, Kept, Out, KeptOut)):
            return pl.BlockSpec(memory_space=pltpu.HBM)
        if not isinstance(v, tuple) and v.ndim == 1 and v.dtype == I32:
            return pl.BlockSpec(memory_space=pltpu.SMEM)
        return pl.BlockSpec(memory_space=pltpu.VMEM)

    specs = [v.spec if isinstance(v, (Out, KeptOut)) else v for v in outs]
    sems = len(streams) + len(leaving) + semaphores

    def kernel(*refs):
        refs = list(refs)
        in_refs, refs = refs[: len(ins)], refs[len(ins) :]
        out_refs, refs = refs[: len(outs)], refs[len(outs) :]
        in_buffers, refs = refs[: len(streams)], refs[len(streams) :]
        out_buffers, refs = refs[: len(leaving)], refs[len(leaving) :]
        own, tail = refs[: len(scratch)], refs[len(scratch) :]
        place = 0
        args = []
        for v, ref in zip(ins, in_refs):
            if isinstance(v, Stream):
                copy = pltpu.make_async_copy(ref, in_buffers[place], tail[0].at[place])
                copy.start()
                ref = Arriving(in_buffers[place], copy)
                place += 1
            args.append(ref)
        results = []
        for v, ref in zip(outs, out_refs):
            if isinstance(v, Out):
                buffer = out_buffers[place - len(streams)]
                ref = Leaving(buffer, pltpu.make_async_copy(buffer, ref, tail[0].at[place]))
                place += 1
            results.append(ref)
        more = [tail[0].at[place + k] for k in range(semaphores)]
        body(*args, *results, *own, *more)
        for ref in args:
            if isinstance(ref, Arriving):
                ref.wait()
        sent = [ref for ref in results if isinstance(ref, Leaving)]
        for ref in sent:
            if not ref.started:
                ref.flush()
        for ref in sent:
            ref.copy.wait()

    shapes = [(v.shape, v.dtype) for v in streams] + leaving + list(scratch)
    scratch_shapes = [pltpu.VMEM(shape, dtype) for shape, dtype in shapes]
    if sems:
        scratch_shapes.append(pltpu.SemaphoreType.DMA((sems,)))
    return pl.pallas_call(
        kernel,
        in_specs=[spec_of(v) for v in ins],
        out_specs=[spec_of(v) for v in outs],
        out_shape=[
            (pltpu.HBM if isinstance(v, (Out, KeptOut)) else jax.ShapeDtypeStruct)(*spec)
            for v, spec in zip(outs, specs)
        ],
        scratch_shapes=scratch_shapes,
        compiler_params=pltpu.CompilerParams(vmem_limit_bytes=limit * MIB),
        cost_estimate=pl.CostEstimate(
            flops=int(MICROS[name] * 1e9), bytes_accessed=int(MICROS[name] * 1e6), transcendentals=0
        ),
        input_output_aliases=alias or {},
        name=name,
    )(*values)


def nn(left, right, precision=None):
    return lax.dot_general(
        left, right, (((1,), (0,)), ((), ())), precision=precision, preferred_element_type=F32
    )


def nt(left, right, precision=None):
    return lax.dot_general(
        left, right, (((1,), (1,)), ((), ())), precision=precision, preferred_element_type=F32
    )


def tn(left, right, precision=None):
    return lax.dot_general(
        left, right, (((0,), (0,)), ((), ())), precision=precision, preferred_element_type=F32
    )


def total(values):
    return jnp.sum(values, axis=0, keepdims=True)


def centre(values):
    return values - jnp.mean(values, axis=-1, keepdims=True)


def spread_of(centred):
    return lax.rsqrt(jnp.mean(centred * centred, axis=-1, keepdims=True) + EPS)


def norm_back(grad, normed, scale, gain):
    scaled = grad * gain
    mean_one = jnp.mean(scaled, axis=-1, keepdims=True)
    mean_two = jnp.mean(scaled * normed, axis=-1, keepdims=True)
    return scale * (scaled - mean_one - normed * mean_two)


def unit_rows(values):
    scale = lax.rsqrt(jnp.sum(values * values, axis=-1, keepdims=True) + NORM_EPS)
    return values * scale, scale


def unit_back(grad, unit, scale):
    return scale * (grad - unit * jnp.sum(grad * unit, axis=-1, keepdims=True))


def flagged(flag, shape):
    return (jnp.zeros(shape, I32) + flag) > 0


def project_body(first, second, weight, bias, query, key, value, *kept):
    count = first.shape[0]
    copies = []
    if kept:
        *kept, sem_one, sem_two = kept
        for source, out, sem in zip((first, second), kept, (sem_one, sem_two)):
            copy_out(copies, source, out, sem)
    for place, source in enumerate((first, second)):
        rows = slice(place * count, (place + 1) * count)
        block = source[...]
        query[rows, :] = (nn(block, weight[0]) + bias[0:1, :]).astype(BF)
        key[rows, :] = nn(block, weight[1]).astype(BF)
        value[rows, :] = (nn(block, weight[2]) + bias[1:2, :]).astype(BF)
    for copy in copies:
        copy.wait()


def head_masks(rows, heads):
    lanes = lax.broadcasted_iota(I32, rows.shape, 1) // HEAD_DIM
    return [jnp.where(lanes == head, rows, jnp.zeros_like(rows)) for head in range(heads)]


def allowed_pairs(seg_key, seg_query):
    return jnp.concatenate([seg_key] * (seg_query.shape[1] // LANES), axis=1) == seg_query


def attend_body(
    seg_key, seg_query, query, key_near, key_far, val_near, val_far,
    log_total, context_one, context_two, keys, values_t, context_t,
):
    half = key_near.shape[0]
    heads = query.shape[1] // HEAD_DIM
    keys[:half, :], keys[half:, :] = key_near[...], key_far[...]
    values_t[:, :half], values_t[:, half:] = val_near[...].T, val_far[...].T
    allowed = allowed_pairs(seg_key[...], seg_query[0:1, :])
    queries = head_masks(query[...] * BF(0.125), heads)

    def scores(head):
        return jnp.where(allowed, nt(keys[...], queries[head]), -1e30)

    current = scores(0)
    for head in range(heads):
        later = scores(head + 1) if head + 1 < heads else None
        rows = slice(head * HEAD_DIM, (head + 1) * HEAD_DIM)
        top = jnp.max(current, axis=0, keepdims=True)
        exp_terms = jnp.exp(current - top)
        norm = total(exp_terms)
        context_t[rows, :] = nn(values_t[rows, :], exp_terms.astype(BF)) * (1.0 / norm)
        log_total[head : head + 1, :] = top + jnp.log(norm)
        current = later
    log_total[heads:, :] = jnp.zeros((8 - heads, half), F32)
    log_total.flush()
    count = context_one.shape[0]
    context_one[...] = context_t[:, :count].T.astype(BF)
    context_two[...] = context_t[:, count:].T.astype(BF)


def attend_back_body(
    seg_key, seg_query, log_total, grad_one, grad_two, query, context_one, context_two,
    key_near, key_far, val_near, val_far, *refs, lanes, last,
):
    if last:
        key_before, value_before, gq, gk, gv, bias, keys, values, keys_t, grad_t = refs[:10]
        key_sum, value_sum, bias_before = refs[10], refs[11], None
    else:
        gq, key_sum, value_sum, bias, keys, values, keys_t, grad_t = refs
    half = key_near.shape[0]
    width = query.shape[1]
    heads = width // HEAD_DIM
    picked = (
        lax.broadcasted_iota(I32, (8, width), 1) // HEAD_DIM
        == lax.broadcasted_iota(I32, (8, width), 0)
    ).astype(F32)
    keys[:half, :], keys[half:, :] = key_near[...], key_far[...]
    values[:half, :], values[half:, :] = val_near[...], val_far[...]
    keys_t[...] = keys[...].T
    grad_context = jnp.concatenate(
        [grad[:, lane : lane + width] for grad, lane in zip((grad_one, grad_two), lanes)], axis=0
    )
    mixed = jnp.concatenate([context_one[...], context_two[...]], axis=0)
    allowed = allowed_pairs(seg_key[...], seg_query[0:1, :])
    dots = nt(picked, grad_context.astype(F32) * mixed.astype(F32), HIGH)
    queries = head_masks(query[...] * BF(0.125), heads)
    grad_heads = head_masks(grad_context, heads)

    def start(head):
        return nt(keys[...], queries[head]), nt(values[...], grad_heads[head])

    current = start(0)
    for head in range(heads):
        later = start(head + 1) if head + 1 < heads else None
        rows = slice(head * HEAD_DIM, (head + 1) * HEAD_DIM)
        raw, grad_probs = current
        probs = jnp.where(allowed, jnp.exp(raw - log_total[head : head + 1, :]), 0.0)
        grad_scores = (probs * (grad_probs - dots[head : head + 1, :])).astype(BF)
        add_v = nn(probs.astype(BF), grad_heads[head])
        add_k = nn(grad_scores, queries[head])
        if head:
            value_sum[...] += add_v
            key_sum[...] += add_k
        elif last:
            value_sum[...] = value_before[...] + add_v
            key_sum[...] = key_before[...] + add_k
        else:
            value_sum[...], key_sum[...] = add_v, add_k
        grad_t[rows, :] = nn(keys_t[rows, :], grad_scores)
        current = later
    grad_query = (grad_t[...].T * 0.125).astype(BF)
    gq[...] = grad_query
    bias[...] = jnp.zeros_like(bias)
    bias[0:1, :] = total(grad_query.astype(F32))
    if last:
        gk[...] = key_sum[...].astype(BF)
        grad_value = value_sum[...].astype(BF)
        gv[...] = grad_value
        bias[1:2, :] = total(grad_value.astype(F32))


def norm_one_body(
    tower, rows, mixed_0, mixed_1, mixed_2, mixed_3, w_0, w_1, w_2, w_3, w_2_more, w_3_more,
    b_out, gain, shift, hidden, centred,
):
    summed = rows[...].astype(F32) + b_out[...]
    summed = summed + nn(mixed_0[...], w_0[...]) + nn(mixed_1[...], w_1[...])
    here, there = lane_halves(tower, w_2)
    for mixed, weight, more in ((mixed_2, w_2, w_2_more), (mixed_3, w_3, w_3_more)):
        summed = summed + nn(mixed[:, here], weight[...]) + nn(mixed[:, there], more[...])
    middle = centre(summed)
    hidden[...] = (middle * spread_of(middle) * gain[...] + shift[...]).astype(BF)
    centred[...] = middle


def lane_halves(tower, part):
    size = part.shape[0]
    return (
        pl.ds(pl.multiple_of(tower[0] * size, size), size),
        pl.ds(pl.multiple_of((1 - tower[0]) * size, size), size),
    )


def gelu_pair(inner):
    cdf = 0.5 + 0.5 * lax.erf(inner * math.sqrt(0.5))
    density = jnp.exp(-0.5 * inner * inner) * (1.0 / math.sqrt(2.0 * math.pi))
    return (inner * cdf).astype(BF), (cdf + inner * density).astype(BF)


def ffn_body(
    first, second, w_up, b_up, w_down,
    active_one, active_two, slope_one, slope_two, part_one, part_two,
):
    inners = [nn(first[...], w_up[...]) + b_up[...]]
    inners.append(nn(second[...], w_up[...]) + b_up[...])
    places = ((active_one, slope_one, part_one), (active_two, slope_two, part_two))
    for inner, (active, slope, part) in zip(inners, places):
        act, active_slope = gelu_pair(inner)
        active[...] = act
        active.flush()
        slope[...] = active_slope
        slope.flush()
        part[...] = nn(act, w_down[...]).astype(BF)


def ffn_only_body(rows, w_up, b_up, w_down, part):
    inner = nn(rows[...], w_up[...]) + b_up[...]
    act = (inner * (0.5 + 0.5 * lax.erf(inner * math.sqrt(0.5)))).astype(BF)
    part[...] = nn(act, w_down[...]).astype(BF)


def ffn_keep_body(
    first, second, w_up, b_up,
    active_one, active_two, slope_one, slope_two, copy_one, copy_two,
):
    copy_one[...], copy_two[...] = first[...], second[...]
    copy_one.flush()
    copy_two.flush()
    for rows, active, slope in ((first, active_one, slope_one), (second, active_two, slope_two)):
        active[...], slope[...] = gelu_pair(nn(rows[...], w_up[...]) + b_up[...])
        active.flush()
        slope.flush()


def head_rows(centred, gain_one, shift_one, part, near, far, b_down, gain, shift):
    hidden = centred[...] * spread_of(centred[...]) * gain_one[...] + shift_one[...]
    summed = part[...].astype(F32) + near[...].astype(F32) + far[...].astype(F32)
    middle = centre(hidden + summed + b_down[...])
    return middle, middle * spread_of(middle) * gain[...] + shift[...]


def head_body(
    centred, gain_one, shift_one, part, near, far, b_down, gain, shift,
    col_weight, b_col, pick, cls_own, send, send_half,
):
    _, final = head_rows(centred, gain_one, shift_one, part, near, far, b_down, gain, shift)
    col, _ = unit_rows(nn(final.astype(BF), col_weight[...]) + b_col[...])
    cls, _ = unit_rows(nn(pick[...], final, HIGH))
    count = send_half.shape[0]
    col = col.astype(BF)
    cls_own[...] = jnp.concatenate([cls, jnp.zeros_like(cls)], axis=0).astype(BF)
    send[...] = col
    send_half[...] = col[count:]


def head_keep_body(
    centred, gain_one, shift_one, part, near, far, b_down, gain, shift,
    col_weight, b_col, pick, encoded, middle, col_pre, cls_raw,
):
    kept, final = head_rows(centred, gain_one, shift_one, part, near, far, b_down, gain, shift)
    middle[...] = kept
    middle.flush()
    encoded[...] = final.astype(BF)
    encoded.flush()
    col_pre[...] = nn(final.astype(BF), col_weight[...]) + b_col[...]
    col_pre.flush()
    cls_raw[...] = nn(pick[...], final, HIGH)


def similar_body(is_query, own, *refs):
    pieces, (weight_p, exp_terms, others, sums) = refs[:6], refs[6:]
    count = own.shape[0]
    row = 0
    for piece in pieces:
        rows = slice(row, row + piece.shape[0])
        others[rows, :] = piece[...]
        exp_terms[:, rows] = jnp.exp(SHARP * nt(own[...], piece[...]))
        row += piece.shape[0]
    weight = weight_p[...].astype(BF)
    terms = exp_terms[...]
    high = terms.astype(BF)
    low = (terms - high.astype(F32)).astype(BF)
    sums_q = nt(weight, high) + nt(weight, low)
    sums_p = nn(weight[:, :count], high) + nn(weight[:, :count], low)
    sums_q = jnp.concatenate([sums_q, jnp.zeros((sums_q.shape[0], 3 * count), F32)], axis=1)
    sums[...] = jnp.where(flagged(is_query[0], sums_p.shape), sums_q, sums_p)


def dense_body(is_query, vectors, targets, cls_raw, grad_cls, loss):
    block = vectors[...]
    shape = (block.shape[0], block.shape[0])
    segs = cls_raw.shape[0]
    kind_rows = block.shape[0] // 2
    query_kind = 1 - is_query[0]
    row_kind = lax.broadcasted_iota(I32, shape, 0) // kind_rows
    col_kind = lax.broadcasted_iota(I32, shape, 1) // kind_rows
    paired = jnp.logical_and(row_kind == query_kind, col_kind != query_kind)
    logits = jnp.where(paired, nt(block, block) * SCALE_DENSE, -1e30)
    onehot = targets[...]
    top = jnp.max(logits, axis=1, keepdims=True)
    exp_terms = jnp.where(paired, jnp.exp(logits - top), 0.0)
    norm = jnp.sum(exp_terms, axis=1, keepdims=True)
    norm = jnp.where(norm > 0.0, norm, 1.0)
    grad = ((exp_terms / norm - onehot) * (1.0 / segs)).astype(BF)
    grad = jnp.where(paired, grad, jnp.zeros_like(grad))
    hit = jnp.sum(jnp.where(paired, logits * onehot, 0.0), axis=1, keepdims=True)
    losses = top + jnp.log(norm) - hit
    rows = lax.broadcasted_iota(I32, losses.shape, 0) - query_kind * kind_rows
    mine = jnp.logical_and(rows >= 0, rows < segs)
    loss[...] = jnp.zeros_like(loss) + jnp.sum(jnp.where(mine, losses, 0.0))
    grad_rows = nn(grad[: 2 * segs], block)[:segs]
    grad_cols = tn(grad[:, : 2 * segs], block)[:segs]
    own = jnp.where(flagged(is_query[0], grad_rows.shape), grad_rows, grad_cols) * SCALE_DENSE
    grad_cls[...] = unit_back(own, *unit_rows(cls_raw[...]))


def score_body(
    is_query, sums, exp_terms, others, weight_q, weight_p, target, col_pre,
    grad_pre, scores,
):
    count = exp_terms.shape[0]
    segs = weight_q.shape[0]
    seg_sums = sums[...]
    w_q, w_p = weight_q[...], weight_p[...]
    size = jnp.sum(w_q, axis=1, keepdims=True)
    nearest = jnp.log(seg_sums) * (1.0 / SHARP)
    pair = nt(w_q, nearest, HIGH) / size
    scores[...] = pair
    logits = pair * SCALE_COL
    onehot = target[...]
    top = jnp.max(logits, axis=1, keepdims=True)
    terms = jnp.exp(logits - top)
    norm = jnp.sum(terms, axis=1, keepdims=True)
    grad_pair = (terms / norm - onehot) * (SCALE_COL / segs) / size
    grad_sums = tn(grad_pair, w_q, HIGH) / (SHARP * seg_sums)
    left = jnp.where(
        flagged(is_query[0], (segs, count)), grad_sums[:, :count], w_p[:, :count]
    )
    right = jnp.where(flagged(is_query[0], w_p.shape), w_p, grad_sums)
    grad_similar = (tn(left, right, HIGH) * (exp_terms[...] * SHARP)).astype(BF)
    grad_vec = nn(grad_similar, others[...])
    pre = unit_back(grad_vec, *unit_rows(col_pre[...])).astype(BF)
    grad_pre[...] = pre


def norm_two_back_rows(grad_pre, col_weight, grad_cls, pick, middle, gain):
    grad_final = nt(grad_pre[...], col_weight[...]) + tn(pick[...], grad_cls[...], HIGH)
    spread = spread_of(middle[...])
    unit = middle[...] * spread
    return norm_back(grad_final, unit, spread, gain[...]), grad_final, unit


def norm_two_back_body(grad_pre, col_weight, grad_cls, pick, middle, gain, grad_b):
    back, _, _ = norm_two_back_rows(grad_pre, col_weight, grad_cls, pick, middle, gain)
    grad_b[...] = back.astype(BF)


def norm_two_keep_body(
    grad_pre, col_weight, grad_cls, pick, middle, gain, scores, target, dense_loss,
    grad_two, grad_kept, small,
):
    back, grad_final, unit = norm_two_back_rows(
        grad_pre, col_weight, grad_cls, pick, middle, gain
    )
    grad_kept[...] = back.astype(BF)
    grad_kept.flush()
    grad_two[...] = back
    grad_two.flush()
    logits = scores[...] * SCALE_COL
    top = jnp.max(logits, axis=1, keepdims=True)
    norm = jnp.sum(jnp.exp(logits - top), axis=1, keepdims=True)
    losses = top + jnp.log(norm) - jnp.sum(logits * target[...], axis=1, keepdims=True)
    small[0:1, :] = total(grad_pre[...].astype(F32))
    small[1:2, :] = total(back)
    small[2:3, :] = total(grad_final * unit)
    small[3:4, :] = total(grad_final)
    small[4:5, :] = jnp.zeros((1, unit.shape[1]), F32) + (jnp.sum(losses) + dense_loss[0:1, 0:1])
    small[5:8, :] = jnp.zeros((3, unit.shape[1]), F32)


def ffn_back_body(
    first, second, slope_one, slope_two, w_down, w_up,
    inner_one, inner_two, part_one, part_two, bias,
):
    bias_sum = jnp.zeros((1, slope_one.shape[1]), F32)
    raws = [nt(second[...], w_down[...]), nt(first[...], w_down[...])]
    for raw, slope, inner in zip(raws, (slope_two, slope_one), (inner_two, inner_one)):
        grad = (raw * slope[...].astype(F32)).astype(BF)
        inner[...] = grad
        inner.flush()
        bias_sum = bias_sum + total(grad.astype(F32))
    part_two[...] = nt(inner_two[...], w_up[...]).astype(BF)
    part_one[...] = nt(inner_one[...], w_up[...]).astype(BF)
    bias[...] = bias_sum


def ffn_back_only_body(rows, slope, w_down, w_up, part):
    inner = (nt(rows[...], w_down[...]) * slope[...].astype(F32)).astype(BF)
    part[...] = nt(inner, w_up[...]).astype(BF)


def ffn_back_keep_body(first, second, slope_one, slope_two, w_down, inner_one, inner_two, bias):
    bias_sum = jnp.zeros((1, slope_one.shape[1]), F32)
    for rows, slope, inner in ((first, slope_one, inner_one), (second, slope_two, inner_two)):
        grad = (nt(rows[...], w_down[...]) * slope[...].astype(F32)).astype(BF)
        inner[...] = grad
        inner.flush()
        bias_sum = bias_sum + total(grad.astype(F32))
    bias[...] = bias_sum


def norm_one_back_body(
    tower, grad_two, part, near, far, centred, gain, w_0, w_1, w_2, w_3, w_2_more, w_3_more,
    grad_one, grad_b, small, mixed_0, mixed_2, mixed_13,
):
    grad = (
        grad_two[...]
        + part[...].astype(F32)
        + near[...].astype(F32)
        + far[...].astype(F32)
    )
    spread = spread_of(centred[...])
    unit = centred[...] * spread
    back = norm_back(grad, unit, spread, gain[...])
    grad_one[...] = back
    grad_one.flush()
    rounded = back.astype(BF)
    grad_b[...] = rounded
    grad_b.flush()
    width = mixed_0.shape[1]
    size = w_2.shape[0]
    for weight, more, mixed, lane in (
        (w_3, w_3_more, mixed_13, width), (w_2, w_2_more, mixed_2, 0)
    ):
        for part, side in ((weight, tower[0]), (more, 1 - tower[0])):
            lanes = pl.ds(pl.multiple_of(side * size + lane, size), size)
            mixed[:, lanes] = nt(rounded, part[...]).astype(BF)
    mixed_13[:, :width] = nt(rounded, w_1[...]).astype(BF)
    mixed_0[...] = nt(rounded, w_0[...]).astype(BF)
    small[0:1, :] = total(back)
    small[1:2, :] = total(grad * unit)
    small[2:3, :] = total(grad)
    small[3:8, :] = jnp.zeros((5, unit.shape[1]), F32)


def input_grad_body(
    query_near, query_far, grad_key, grad_value, weight, part_0, part_2, part_31
):
    count = part_0.shape[0]
    places = ((3, part_31, 0), (1, part_31, count), (2, part_2, 0), (0, part_0, 0))
    for block, out, row in places:
        own = slice(block % 2 * count, (block % 2 + 1) * count)
        rows = slice(block * count, (block + 1) * count)
        out[row : row + count, :] = (
            nt((query_near, query_far)[block // 2][own, :], weight[0])
            + nt(grad_key[rows, :], weight[1])
            + nt(grad_value[rows, :], weight[2])
        ).astype(BF)


def order_rows(place, source, out, size):
    for block in range(source.shape[1] // size):
        start = pl.multiple_of((jnp.int32(block) ^ place) * size, size)
        out[block * size : (block + 1) * size, :] = source[:, pl.ds(start, size)].T


def weight_grad_body(place, *refs, lefts, rights, cuts, first):
    left = refs[:lefts]
    right = refs[lefts : lefts + sum(rights)]
    outs, (ordered, joined) = refs[lefts + sum(rights) : -2], refs[-2:]
    token = 0
    for part in left:
        tokens = slice(token, token + part.shape[0])
        order_rows(place[0], part, ordered.at[:, tokens], LANES)
        token += part.shape[0]
    at = 0
    lane = 0
    for group in rights:
        token = 0
        for part in right[at : at + group]:
            rows = part.shape[0]
            lanes = min(part.shape[1], joined.shape[1])
            joined[token : token + rows, lane : lane + lanes] = part[:, first : first + lanes]
            token += rows
        at += group
        lane += lanes
    half = ordered.shape[0] // 2
    lane = 0
    for cut, (keep, send) in zip(cuts, zip(outs[::2], outs[1::2])):
        lanes = slice(lane, lane + cut)
        for rows, out in ((slice(half, 2 * half), send), (slice(0, half), keep)):
            out[...] = nn(ordered[rows, :], joined[:, lanes]).astype(BF)
            if isinstance(out, Leaving):
                out.flush()
        lane += cut


def turned_grad_body(place, mp_place, grad, *refs, rows):
    left, (part_0, part_2, part_31, ordered) = refs[:-4], refs[-4:]
    order_rows(place[0], grad, ordered, LANES)
    outs = ((0, part_0, 0), (2, part_2, 0), (3, part_31, 0), (1, part_31, rows))
    for block, out, lane in outs:
        if len(left) == 1:
            start = pl.multiple_of((jnp.int32(block) ^ mp_place[0]) * rows, rows)
            right = left[0][:, pl.ds(start, rows)]
        else:
            right = left[block][...]
        out[:, lane : lane + rows] = nn(ordered[...], right).astype(BF)
        if isinstance(out, Leaving):
            out.flush()


def place_col_body(mp_place, tower, w_0, w_1, w_2, w_3, w_2_more, w_3_more, out):
    count = w_0.shape[0]
    here, there = lane_halves(tower, w_2)
    for block, parts in enumerate(((w_0,), (w_1,), (w_2, w_2_more), (w_3, w_3_more))):
        start = pl.multiple_of((jnp.int32(block) ^ mp_place[0]) * count, count)
        if len(parts) == 1:
            out[pl.ds(start, count), :] = parts[0][...]
        else:
            size = parts[0].shape[0]
            out[pl.ds(pl.multiple_of(start + tower[0] * size, size), size), :] = parts[0][...]
            out[pl.ds(pl.multiple_of(start + (1 - tower[0]) * size, size), size), :] = parts[1][...]


def copy_out(copies, source, target, sem):
    copies.append(pltpu.make_async_copy(source, target, sem))
    copies[-1].start()


def place_wide_body(place, *refs, size):
    *parts, out, buffer = refs[: -8]
    sems = refs[-8:]
    copies = []
    cut = parts[0].shape[1]
    for block in range(8):
        here = pl.ds(block * size, size)
        start = pl.multiple_of((jnp.int32(block) ^ place[0]) * size, size)
        row = block % 4 * size
        for column in range(len(parts) // 2):
            part = parts[2 * column + block // 4]
            lanes = slice(column * cut, (column + 1) * cut)
            buffer[here, lanes] = part[row : row + size, :].astype(F32)
        copy_out(copies, buffer.at[here], out.at[pl.ds(start, size)], sems[block])
    for copy in copies:
        copy.wait()


def place_qkv_body(place, one, one_more, qkv, buffer, *sems, size):
    copies = []
    width = qkv.shape[2]
    for block in range(8):
        here = pl.ds(block * size, size)
        start = pl.multiple_of((jnp.int32(block) ^ place[0]) * size, size)
        rows = slice(block % 4 * size, (block % 4 + 1) * size)
        part = (one, one_more)[block // 4]
        for kind in range(3):
            lanes = slice(kind * width, (kind + 1) * width)
            buffer[kind, here, :] = part[rows, lanes].astype(F32)
            copy_out(
                copies,
                buffer.at[kind, here],
                qkv.at[kind, pl.ds(start, size)],
                sems[3 * block + kind],
            )
    for copy in copies:
        copy.wait()


def place_last_body(place, one, one_more, out, col, *, size):
    width = out.shape[0]
    for block in range(8):
        start = pl.multiple_of((jnp.int32(block) ^ place[0]) * size, size)
        rows = slice(block % 4 * size, (block % 4 + 1) * size)
        part = (one, one_more)[block // 4]
        out[:, pl.ds(start, size)] = part[rows, :width].astype(F32).T
        col[:, pl.ds(start, size)] = part[rows, width:].astype(F32).T


def dp_bits():
    return [1 << k for k in range(int(math.log2(lax.axis_size("dp"))))]


def add(*values):
    return sum(value.astype(F32) for value in values).astype(BF)


def side_of(axis, bit):
    return jnp.minimum(lax.axis_index(axis) & bit, 1)


def join(value, other, axis, bit):
    return jnp.where(
        side_of(axis, bit) == 0,
        jnp.concatenate([value, other]),
        jnp.concatenate([other, value]),
    )


def more_bits():
    return [("dp", bit) for bit in dp_bits()[2:]]


def sum_more(value):
    for axis, bit in more_bits():
        half = value.shape[0] // 2
        side = side_of(axis, bit)
        sent = lax.dynamic_slice_in_dim(value, (1 - side) * half, half, 0)
        kept = lax.dynamic_slice_in_dim(value, side * half, half, 0)
        value = add(kept, swap(sent, axis, bit))
    for axis, bit in more_bits()[::-1]:
        value = join(value, swap(value, axis, bit), axis, bit)
    return value


HOPS = (("tower", 1), ("dp", 1), ("dp", 2))


class Unit:
    def __init__(self, keep, send):
        self.value, self.send, self.stage = keep, send, 0

    def hop(self):
        return HOPS[min(self.stage, 5 - self.stage)]

    def land(self, got):
        self.stage += 1
        if self.stage <= 3:
            value = self.value.astype(F32) + got.astype(F32)
            if self.stage < 3:
                half = value.shape[0] // 2
                self.value, self.send = value[:half], value[half:].astype(BF)
            else:
                self.send = sum_more(value.astype(BF))
        elif self.stage < 6:
            self.send = jnp.concatenate([self.send, got])
        else:
            self.halves = (self.send, got)


class Small:
    def __init__(self, value):
        self.send, self.stage = value, 0

    def hop(self):
        return HOPS[self.stage]

    def land(self, got):
        self.stage += 1
        self.send = self.send + got
        if self.stage == 3:
            for axis, bit in more_bits():
                self.send = self.send + swap(self.send, axis, bit)


def together(*values):
    return lax.optimization_barrier(values)


def phase(units=(), moves=(), fill=None, then=None, land=()):
    groups = {}
    for unit in units:
        groups.setdefault((unit.hop(), unit.send.dtype), []).append(unit)
    groups = list(groups.values())
    sends = [
        group[0].send
        if len(group) == 1
        else jnp.concatenate([unit.send for unit in group], axis=1)
        for group in groups
    ]
    if moves:
        sends = [after(send, moves[0][0]) for send in sends]
    ready = [value for value, _ in moves] + sends
    flights = [swap(value, *hop) for value, hop in moves]
    flights += [swap(send, *group[0].hop()) for send, group in zip(sends, groups)]
    groups += [[unit] for unit in land]
    flights += [unit.flight for unit in land]
    filled = list(fill(lambda value: after(value, *ready))) if fill else []
    if then:
        started = then(filled)
        started.flight = swap(started.send, *started.hop())
    sizes = [value.size * value.dtype.itemsize for value in flights]
    soon = [k for k, size in enumerate(sizes) if size < max(sizes)]
    done = together(*[flights[k] for k in soon], *filled)
    rest = [k for k in range(len(flights)) if k not in soon]
    done = together(*done, *[flights[k] for k in rest])
    landed = [None] * len(flights)
    for k, value in zip(soon, done):
        landed[k] = value
    for k, value in zip(rest, done[len(soon) + len(filled) :]):
        landed[k] = value
    for group, got in zip(groups, landed[len(moves) :]):
        lane = 0
        for unit in group:
            width = unit.send.shape[1]
            unit.land(got if len(group) == 1 else got[:, lane : lane + width])
            lane += width
    arrived, filled = landed[: len(moves)], done[len(soon) : len(soon) + len(filled)]
    return (arrived, filled, started) if then else (arrived, filled)


def place_of(hops):
    place = 0
    for axis, bit in hops:
        place = place * 2 + side_of(axis, bit)
    return place[None].astype(I32)


def relative(values, mp_index):
    size = values.shape[-1] // 4
    blocks = [values[..., k * size : (k + 1) * size] for k in range(4)]
    values = jnp.where(mp_index & 1, jnp.concatenate([blocks[k ^ 1] for k in range(4)], -1), values)
    blocks = [values[..., k * size : (k + 1) * size] for k in range(4)]
    return jnp.where(mp_index & 2, jnp.concatenate([blocks[k ^ 2] for k in range(4)], -1), values)


def flip(values, bit):
    size = values.shape[-1] // 4
    return jnp.concatenate([values[:, (k ^ bit) * size :][:, :size] for k in range(4)], axis=1)


def per_device(
    tokens,
    segment_ids,
    key_mask,
    positives,
    w_qkv,
    b_qv,
    w_out,
    b_out,
    gain_one,
    shift_one,
    w_up,
    b_up,
    w_down,
    b_down,
    gain_two,
    shift_two,
    w_col,
    b_col,
):
    own_rows = tokens[0, 0]
    count, model_dim = own_rows.shape
    pair, width = 2 * count, w_out.shape[0]
    half = count // 2
    units = w_up.shape[1]
    segs = positives.shape[1]
    dp_size = lax.axis_size("dp")
    mp_index = lax.axis_index("mp")
    dp_index = lax.axis_index("dp")
    tower = lax.axis_index("tower")
    is_query = tower == 0
    query_flag = (1 - tower)[None].astype(I32)
    mp_place = mp_index[None].astype(I32)
    rest_place = place_of(HOPS)
    tower_place = tower[None].astype(I32)
    labels = jnp.arange(segs, dtype=I32)
    row = lambda vector: vector[None, :]
    block_bf = ((count, model_dim), BF)
    block_f32 = ((count, model_dim), F32)

    def core(block):
        return swap(block, "mp", 1)

    def across(block):
        return swap(block, "mp", 2)

    x_0, x_1, x_2 = own_rows, core(own_rows), across(own_rows)
    w_three = jnp.transpose(w_qkv, (1, 0, 2))

    seg_pair = segment_ids[:, 0]
    starts = jnp.concatenate([jnp.ones((2, 1), bool), seg_pair[:, 1:] != seg_pair[:, :-1]], axis=1)
    valid_pair = jnp.logical_or(key_mask[:, 0] > 0, starts)
    codes = relative(seg_pair + 16 * valid_pair.astype(I32) + 32 * starts.astype(I32), mp_index)
    seg_rel, valid_rel = codes & 15, (codes & 16) > 0
    code_row = jnp.where(is_query, codes[0], codes[1])
    seg_row = code_row & 15
    seg_key = jnp.broadcast_to(
        jnp.where((code_row & 16) > 0, seg_row, -1)[:, None], (4 * count, LANES)
    )
    seg_query = jnp.broadcast_to(seg_row[None, :], (8, 4 * count))
    members = seg_rel[:, None, :] == labels[None, :, None]
    weights = jnp.logical_and(members, valid_rel[:, None, :]).astype(F32)
    weight_q, weight_p = weights[0], weights[1]
    pick = (code_row[None, :count] - 32 == labels[:, None] + 16).astype(F32)
    order = dp_index ^ jnp.arange(dp_size, dtype=I32)
    kinds = jnp.arange(2, dtype=I32)[:, None, None]
    targets = (
        (1 - tower) * dp_size * segs
        + jnp.arange(dp_size, dtype=I32)[None, :, None] * segs
        + positives[order][None]
    )
    targets = jnp.where(kinds == tower, targets, -1).reshape(2 * dp_size * segs)
    paired = (targets[:, None] == jnp.arange(2 * dp_size * segs, dtype=I32)).astype(F32)
    positive_row = lax.dynamic_index_in_dim(positives, dp_index, 0, keepdims=False)
    positive_row = (positive_row[:, None] == labels).astype(F32)

    half_bf = ((pair, width), BF)
    mixed_bf = ((count, width), BF)
    x_hop, core_hop, y_hop = ("mp", 2), ("mp", 1), ("tower", 1)

    def project(first, second, kept=()):
        return call(
            project_body,
            "project",
            [first, second, w_three, b_qv],
            [half_bf] * 3 + list(kept),
            semaphores=len(kept),
        )

    near_qkv = project(x_0, x_1)
    halves = [
        lax.dynamic_slice_in_dim(weight, tower * half, half, 0) for weight in (w_out, w_col)
    ]
    x_2, out_half, col_half, out_1, col_1 = together(
        x_2, *halves, core(w_out), core(w_col), near_qkv,
        seg_key, seg_query, weight_q, weight_p, pick, paired, positive_row,
    )[:5]
    x_3 = core(x_2)
    out_2, col_2 = across(out_half), across(col_half)
    far_qkv = project(x_2, x_3, [KeptOut(*block_bf)] * 2)
    x_2_kept, x_3_kept = far_qkv[3:]
    key_values = [near_qkv[1], far_qkv[1], near_qkv[2], far_qkv[2]]
    seg_query_near, seg_query_far = seg_query[:, :pair], seg_query[:, pair:]

    def attend(seg_half, query):
        return call(
            attend_body,
            "attend",
            [seg_key, seg_half, query, *key_values],
            [Out((8, pair), F32), mixed_bf, mixed_bf],
            [((4 * count, width), BF), ((width, 4 * count), BF), ((width, pair), F32)],
        )

    total_far, mixed_far_2, mixed_far_3 = attend(seg_query_far, far_qkv[0])
    mixed_far_2, mixed_far_3, out_2 = together(mixed_far_2, mixed_far_3, out_2)
    (out_2_more, mixed_2, mixed_1_2), (total_near, mixed_0, mixed_near_1, col_2) = phase(
        (),
        [(out_2, y_hop), (mixed_far_2, x_hop), (mixed_far_3, x_hop)],
        lambda late: [*attend(seg_query_near, late(near_qkv[0])), col_2],
    )
    (mixed_1, mixed_3, out_3, out_3_more), _ = phase(
        (),
        [(mixed_near_1, core_hop), (mixed_1_2, core_hop), (out_2, core_hop)]
        + [(out_2_more, core_hop)],
    )
    col_3 = core(col_2)
    mixed = [mixed_0, mixed_1, mixed_2, mixed_3]
    outs = [w_out, out_1, out_2, out_3, out_2_more, out_3_more]
    hidden, centred_one = call(
        norm_one_body,
        "norm_one",
        [tower_place, own_rows, *mixed, *outs, row(b_out), row(gain_one), row(shift_one)],
        [block_bf, block_f32],
    )

    h_0, h_1 = hidden, core(hidden)
    kept_bf = Out((count, units), BF)
    (h_2, col_2_more), (act_0, act_1, slope_0, slope_1, part_0, part_1) = phase(
        (),
        [(hidden, x_hop), (col_2, y_hop)],
        lambda late: call(
            ffn_body,
            "feed_forward",
            [h_0, h_1, w_up, row(b_up), w_down],
            [kept_bf] * 4 + [Out(*block_bf), block_bf],
        ),
    )
    h_3, col_3_more = core(h_2), core(col_2_more)

    def feed_far(rows):
        return call(
            ffn_only_body, "feed_far", [rows, w_up, row(b_up), w_down], [block_bf]
        )[0]

    part_2 = feed_far(h_2)
    part_3 = feed_far(after(h_3, part_2))
    near_sum = core(part_1)
    joined = add(part_2, core(part_3))
    joined, near_sum = together(joined, near_sum)
    (arrived,), (act_2, act_3, slope_2, slope_3, h_2_kept, h_3_kept, col_weight) = phase(
        (),
        [(joined, x_hop)],
        lambda late: [
            *call(
                ffn_keep_body,
                "feed_keep",
                [late(h_2), h_3, w_up, row(b_up)],
                [kept_bf] * 4 + [Out(*block_bf)] * 2,
            ),
            *call(
                place_col_body,
                "place_col",
                [mp_place, tower_place, w_col, late(col_1), col_2, col_3, col_2_more, col_3_more],
                [((model_dim, model_dim), BF)],
            ),
        ],
    )
    ins = [centred_one, row(gain_one), row(shift_one), part_0, near_sum, arrived]
    ins += [row(b_down), row(gain_two), row(shift_two), col_weight, row(b_col), pick]
    cls_own, send, send_half = call(
        head_body,
        "heads",
        ins,
        [((2 * segs, model_dim), BF), block_bf, ((half, model_dim), BF)],
    )

    cls_own = cls_own[:segs]
    (other, own_half, cls_far), (encoded, middle, col_pre, cls_raw) = phase(
        (),
        [(send, y_hop), (send_half, x_hop), (cls_own, ("dp", 1))],
        lambda late: call(
            head_keep_body,
            "heads_keep",
            [late(centred_one)] + ins[1:],
            [Out(*block_bf), Out(*block_f32), Out(*block_f32), Out((segs, model_dim), F32)],
        ),
    )
    cls_all = jnp.concatenate([cls_own, cls_far])
    (far_b, far_a, cls_far), _ = phase(
        (), [(own_half, y_hop), (other[:half], x_hop), (cls_all, ("dp", 2))]
    )
    cls_all = jnp.concatenate([cls_all, cls_far])
    for bit in dp_bits()[2:]:
        cls_all = jnp.concatenate([cls_all, swap(cls_all, "dp", bit)])
    (near, diag_a, diag_b, cls_near), _ = phase(
        (),
        [(other, core_hop), (far_a, core_hop), (far_b, core_hop), (cls_all, core_hop)],
    )
    cls_all = add(cls_all, cls_near)
    pieces = [other, near, far_a, far_b, diag_a, diag_b]
    exp_terms, others, sums = call(
        similar_body,
        "similar",
        [query_flag, send, *pieces, weight_p],
        [((count, 4 * count), F32), ((4 * count, model_dim), BF), ((segs, 4 * count), F32)],
    )
    cls_all = after(cls_all, sums)
    (swapped, cls_far), _ = phase((), [(sums, x_hop), (cls_all, x_hop)])
    sums = sums + flip(swapped, 2)
    cls_all = add(cls_all, cls_far)
    (swapped,), _ = phase((), [(sums, core_hop)])
    sums = sums + flip(swapped, 1)
    (cls_other,), (grad_pre, pair_score) = phase(
        (),
        [(after(cls_all, sums), y_hop)],
        lambda late: call(
            score_body,
            "scores",
            [query_flag, late(sums), exp_terms, others, weight_q, weight_p, positive_row, col_pre],
            [block_bf, ((segs, segs), F32)],
        ),
    )
    grad_cls, dense_loss = call(
        dense_body,
        "dense",
        [query_flag, jnp.concatenate([cls_all, cls_other]), paired, cls_raw],
        [((segs, model_dim), F32), ((8, LANES), F32)],
    )
    ins = [grad_pre, col_weight, grad_cls, pick, middle, row(gain_two)]
    (grad_two_b,) = call(norm_two_back_body, "norm_two_back", ins, [block_bf])

    def streams(*values):
        return [Stream(value) for value in values]

    def feed_back(first, second, slope_one, slope_two, part):
        return call(
            ffn_back_body,
            "feed_back",
            [first, second, *streams(slope_one, slope_two), w_down, w_up],
            [kept_bf] * 2 + [part, block_bf, Out((1, units), F32)],
            limit=12,
        )

    def weight_grad(left, right, cuts, first=0):
        rows = getattr(left[0], "value", left[0]).shape[1]
        tokens = 4 * count
        outs = [Out((rows // 2, cut), BF) for cut in cuts for _ in range(2)]
        outs[1] = ((rows // 2, cuts[0]), BF)
        return call(
            functools.partial(
                weight_grad_body,
                lefts=len(left),
                rights=[len(parts) for parts in right],
                cuts=cuts,
                first=first,
            ),
            "weight_grad",
            [rest_place, *left, *[part for parts in right for part in parts]],
            outs,
            [((rows, tokens), BF), ((tokens, sum(cuts)), BF)],
            limit=20,
        )

    def turned_grad(grad, left):
        return call(
            functools.partial(turned_grad_body, rows=count),
            "turned_grad",
            [rest_place, mp_place, grad, *left],
            [Out((model_dim, count), BF)] * 2 + [((model_dim, 2 * count), BF)],
            [((model_dim, count), BF)],
        )

    def near_back(late):
        backs = feed_back(grad_two_b, g_1, slope_0, slope_1, Out(*block_bf))
        kept = call(
            norm_two_keep_body,
            "norm_two_keep",
            [after(grad_pre, backs[3])] + ins[1:] + [pair_score, positive_row, dense_loss],
            [Out(*block_f32), Out(*block_bf), Out((8, model_dim), F32)],
        )
        turned = turned_grad(Stream(after(grad_pre, kept[2])), [Stream(encoded)])
        return [*backs, *kept, *turned]

    g_1 = core(grad_two_b)
    (g_2,), (inner_0, inner_1, part_0, part_1, bias_near, *kept) = phase(
        (), [(grad_two_b, x_hop)], near_back
    )
    grad_two, grad_two_kept, small_two, col_own, col_joined, col_near = kept
    g_3 = core(g_2)

    def feed_back_far(rows, slope):
        return call(
            ffn_back_only_body, "feed_back_far", [rows, slope, w_down, w_up], [block_bf]
        )[0]

    part_2 = feed_back_far(g_2, slope_2)
    part_3 = feed_back_far(after(g_3, part_2), slope_3)
    cut = model_dim // 2

    def down_grad(late, start):
        return weight_grad(
            streams(act_0, act_1, act_2, act_3),
            [[Stream(grad_two_kept), Stream(g_1), late(g_2), g_3]],
            [cut],
            start,
        )

    (near_sum, arrived), down = phase(
        (), [(part_1, core_hop), (part_3, core_hop)], lambda late: down_grad(late, 0)
    )
    down = [Unit(*down)]
    joined = add(part_2, arrived)

    def unit_grads(late):
        more = down_grad(late, cut)
        inner_2, inner_3, bias_far = call(
            ffn_back_keep_body,
            "feed_back_keep",
            [after(g_2, more[1]), g_3, slope_2, slope_3, w_down],
            [kept_bf] * 2 + [Out((1, units), F32)],
        )
        up = weight_grad(
            streams(after(h_0, bias_far), h_1, h_2_kept, h_3_kept),
            [streams(inner_0, inner_1, inner_2, inner_3)],
            [cut, cut],
        )
        return [*more, *up, bias_far]

    (arrived,), (_, _, *up, bias_far), more = phase(
        down, [(joined, x_hop)], unit_grads, then=lambda filled: Unit(*filled[:2])
    )
    down.append(more)
    up = [Unit(*up[:2]), Unit(*up[2:])]
    grad_one, grad_one_b, small_one, back_0, back_2, back_13 = call(
        norm_one_back_body,
        "norm_one_back",
        [tower_place, grad_two, part_0, near_sum, arrived, centred_one, row(gain_one), *outs],
        [Out(*block_f32), Out(*block_bf), ((8, model_dim), F32)]
        + [mixed_bf, mixed_bf, ((count, 2 * width), BF)],
        limit=12,
    )

    (back_13,), _ = phase((), [(back_13, core_hop)], land=[down[1]])
    back_23 = jnp.concatenate([back_2, back_13[:, width:]], axis=1)
    all_bf, all_f32 = ((4 * count, width), BF), ((4 * count, width), F32)
    back_scratch = [all_bf] * 2 + [((width, 4 * count), BF), ((width, pair), F32)]

    def back_ins(seg_half, log_total, grads, query, mixed_pair):
        return [seg_key, seg_half, log_total, *grads, query, *mixed_pair, *key_values]

    def near_rows(late):
        backs = call(
            functools.partial(attend_back_body, lanes=(0, 0), last=False),
            "attend_back",
            back_ins(
                seg_query_near,
                total_near,
                [late(back_0), back_13],
                near_qkv[0],
                (mixed_0, mixed_near_1),
            ),
            [half_bf, all_f32, all_f32, ((8, width), F32)],
            back_scratch,
            limit=16,
        )
        return [*backs, *turned_grad(Stream(after(grad_one_b, backs[0])), streams(*mixed))]

    (back_23, col_near), (grad_q_near, key_sum, value_sum, bias_near_q, *out_parts) = phase(
        [*down, up[0]], [(back_23, x_hop), (col_near, core_hop)], near_rows
    )
    col_joined = add(col_joined, col_near[:, :count])
    col_own = add(col_own, col_near[:, count:])

    def far_rows(late):
        backs = call(
            functools.partial(attend_back_body, lanes=(0, width), last=True),
            "attend_back",
            back_ins(
                seg_query_far,
                total_far,
                [late(back_23), back_23],
                far_qkv[0],
                (mixed_far_2, mixed_far_3),
            )
            + [key_sum, value_sum],
            [half_bf, all_bf, all_bf, ((8, width), F32)],
            back_scratch + [all_f32, all_f32],
            limit=16,
        )
        grads = weight_grad(
            [after(x_0, backs[1]), x_1, x_2_kept, x_3_kept],
            [[grad_q_near, backs[0]], [backs[1]], [backs[2]]],
            [3 * width],
        )
        return [*backs, *grads]

    (out_near, col_far), (grad_q_far, grad_k, grad_v, bias_far_v, *grads) = phase(
        [up[1], up[0], *down], [(out_parts[2], core_hop), (col_joined, x_hop)], far_rows
    )
    qkv = Unit(*grads)
    out_joined = add(out_parts[1], out_near[:, :count])
    out_own = add(out_parts[0], out_near[:, count:])
    small = jnp.concatenate([small_two, small_one])
    (out_far, small_far), (part_0, part_2, part_31) = phase(
        [qkv, up[1], up[0], *down],
        [(out_joined, x_hop), (small, x_hop)],
        lambda late: call(
            input_grad_body,
            "input_grad",
            streams(late(grad_q_near), grad_q_far, grad_k, grad_v, w_three),
            [Out(*block_bf)] * 2 + [((pair, model_dim), BF)],
        ),
    )
    small = small + small_far
    turned = jnp.concatenate([add(out_own, out_far), add(col_own, col_far)], axis=1)
    rows = model_dim // 2
    rest = Unit(turned[:rows], turned[rows:])
    (part_31, small_near), _ = phase(
        [rest, qkv, *down, up[1], up[0]], [(part_31, core_hop), (small, core_hop)]
    )
    bias_v = (bias_far_v + bias_near_q)[:2].reshape(1, 2 * width)
    small = Small(
        jnp.concatenate(
            [
                small + small_near,
                bias_near + bias_far,
                jnp.concatenate([bias_v, jnp.zeros((1, model_dim - 2 * width), F32)], axis=1),
            ]
        )
    )
    joined = add(part_2, part_31[:count])
    phase([*down, rest, up[0], qkv, up[1]])
    phase([up[0], up[1], rest, qkv, small])
    (arrived,), _ = phase([up[1], qkv, rest, small], [(joined, x_hop)])
    grad_input = (
        grad_one
        + part_0.astype(F32)
        + part_31[count:].astype(F32)
        + arrived.astype(F32)
    )
    d_tokens = grad_input.astype(BF).reshape(1, 1, count, model_dim)

    def place_wide(late, *parts):
        halves = [half for unit in parts for half in unit.halves]
        shape = (model_dim, model_dim)
        return call(
            functools.partial(place_wide_body, size=model_dim // 8),
            "place_wide",
            [rest_place, *streams(late(halves[0]), *halves[1:])],
            [KeptOut(shape, F32)],
            [(shape, F32)],
            semaphores=8,
        )

    _, (grad_down, d_tokens) = phase(
        [qkv, rest, small], fill=lambda late: [*place_wide(late, *down), d_tokens]
    )
    _, (grad_up, grad_qkv) = phase(
        [rest],
        fill=lambda late: [
            *place_wide(late, *up),
            *call(
                functools.partial(place_qkv_body, size=model_dim // 8),
                "place_qkv",
                [rest_place, *streams(late(qkv.halves[0]), qkv.halves[1])],
                [KeptOut((3, model_dim, width), F32)],
                [((3, model_dim, width), F32)],
                semaphores=24,
            ),
        ],
    )
    grad_out, grad_col = call(
        functools.partial(place_last_body, size=model_dim // 8),
        "place_last",
        [rest_place, *rest.halves],
        [Out((width, model_dim), F32)] * 2,
    )
    small = small.send
    loss = small[4, 0] * (1.0 / (segs * 2 * lax.axis_size("mp")))
    return (
        encoded.reshape(1, 1, count, model_dim),
        loss,
        pair_score.reshape(1, segs, segs),
        d_tokens,
        jnp.transpose(grad_qkv, (1, 0, 2)),
        small[17, : 2 * width].reshape(2, width),
        grad_out,
        small[8],
        small[9],
        small[10],
        grad_up,
        small[16],
        grad_down,
        small[1],
        small[2],
        small[3],
        grad_col,
        small[0],
    )


def solution(mesh):
    return jax.shard_map(
        per_device,
        mesh=mesh,
        in_specs=(
            P("tower", "dp", "mp", None),
            P(None, "dp", None),
            P(None, "dp", None),
            P(),
            P(None, None, "mp"),
            P(None, "mp"),
            P("mp", None),
            P(),
            P(),
            P(),
            P(None, "mp"),
            P("mp"),
            P("mp", None),
            P(),
            P(),
            P(),
            P("mp", None),
            P(),
        ),
        out_specs=(
            P("tower", "dp", "mp", None),
            P(),
            P("dp", None, None),
            P("tower", "dp", "mp", None),
            P(None, None, "mp"),
            P(None, "mp"),
            P("mp", None),
            P(),
            P(),
            P(),
            P(None, "mp"),
            P("mp"),
            P("mp", None),
            P(),
            P(),
            P(),
            P("mp", None),
            P(),
        ),
        check_vma=False,
    )
```

```python
import functools
import math

import jax
import jax.numpy as jnp
from jax import lax
from jax.experimental import pallas as pl
from jax.experimental.pallas import tpu as pltpu
from jax.sharding import PartitionSpec as P

HEAD_DIM = 64
EPS = 1e-05
NORM_EPS = 1e-06
SCALE_DENSE = 50.0
SCALE_COL = 50.0
SHARP = 20.0
HIGH = lax.Precision.HIGHEST
BF = jnp.bfloat16
F32 = jnp.float32
I32 = jnp.int32
LANES = 128
MIB = 1 << 20


def swap(block, axis, bit):
    count = lax.axis_size(axis)
    return lax.ppermute(block, axis, [(low, low ^ bit) for low in range(count)])


def after(value, *first):
    return lax.optimization_barrier((value,) + first)[0]


class Stream:
    def __init__(self, value):
        self.value = value


class Kept:
    def __init__(self, value):
        self.value = value


class Out:
    def __init__(self, shape, dtype):
        self.spec = (shape, dtype)


class KeptOut:
    def __init__(self, shape, dtype):
        self.spec = (shape, dtype)


class Arriving:
    def __init__(self, buffer, copy):
        self.buffer, self.copy, self.shape = buffer, copy, buffer.shape

    def wait(self):
        if self.copy is not None:
            self.copy.wait()
            self.copy = None

    def __getitem__(self, index):
        self.wait()
        return self.buffer[index]


class Leaving:
    def __init__(self, buffer, copy):
        self.buffer, self.copy, self.shape, self.dtype = buffer, copy, buffer.shape, buffer.dtype
        self.started = False

    def __setitem__(self, index, value):
        self.buffer[index] = value

    def __getitem__(self, index):
        return self.buffer[index]

    def flush(self):
        self.started = True
        self.copy.start()


MICROS = dict(
    project=1.0, norm_two_back=2.0, norm_two_keep=0.1, attend=3.7, norm_one=1.5, feed_forward=3.0, feed_far=1.3, feed_keep=2.5,
    place_col=1.0, heads=2.0, heads_keep=2.2, similar=1.8, dense=0.8, scores=3.0, feed_back=2.5, feed_back_far=1.3, feed_back_keep=0.1,
    weight_grad=0.1, turned_grad=0.1, norm_one_back=0.1, attend_back=0.1, input_grad=0.1,
    place_wide=0.1, place_qkv=0.1, place_last=0.1,
)


def call(body, name, ins, outs, scratch=(), semaphores=0, limit=8, alias=None):
    streams = [v.value for v in ins if isinstance(v, Stream)]
    leaving = [v.spec for v in outs if isinstance(v, Out)]
    values = [
        pltpu.with_memory_space_constraint(v.value, pltpu.HBM)
        if isinstance(v, (Stream, Kept))
        else v
        for v in ins
    ]

    def spec_of(v):
        if isinstance(v, (Stream, Kept, Out, KeptOut)):
            return pl.BlockSpec(memory_space=pltpu.HBM)
        if not isinstance(v, tuple) and v.ndim == 1 and v.dtype == I32:
            return pl.BlockSpec(memory_space=pltpu.SMEM)
        return pl.BlockSpec(memory_space=pltpu.VMEM)

    specs = [v.spec if isinstance(v, (Out, KeptOut)) else v for v in outs]
    sems = len(streams) + len(leaving) + semaphores

    def kernel(*refs):
        refs = list(refs)
        in_refs, refs = refs[: len(ins)], refs[len(ins) :]
        out_refs, refs = refs[: len(outs)], refs[len(outs) :]
        in_buffers, refs = refs[: len(streams)], refs[len(streams) :]
        out_buffers, refs = refs[: len(leaving)], refs[len(leaving) :]
        own, tail = refs[: len(scratch)], refs[len(scratch) :]
        place = 0
        args = []
        for v, ref in zip(ins, in_refs):
            if isinstance(v, Stream):
                copy = pltpu.make_async_copy(ref, in_buffers[place], tail[0].at[place])
                copy.start()
                ref = Arriving(in_buffers[place], copy)
                place += 1
            args.append(ref)
        results = []
        for v, ref in zip(outs, out_refs):
            if isinstance(v, Out):
                buffer = out_buffers[place - len(streams)]
                ref = Leaving(buffer, pltpu.make_async_copy(buffer, ref, tail[0].at[place]))
                place += 1
            results.append(ref)
        more = [tail[0].at[place + k] for k in range(semaphores)]
        body(*args, *results, *own, *more)
        for ref in args:
            if isinstance(ref, Arriving):
                ref.wait()
        sent = [ref for ref in results if isinstance(ref, Leaving)]
        for ref in sent:
            if not ref.started:
                ref.flush()
        for ref in sent:
            ref.copy.wait()

    shapes = [(v.shape, v.dtype) for v in streams] + leaving + list(scratch)
    scratch_shapes = [pltpu.VMEM(shape, dtype) for shape, dtype in shapes]
    if sems:
        scratch_shapes.append(pltpu.SemaphoreType.DMA((sems,)))
    return pl.pallas_call(
        kernel,
        in_specs=[spec_of(v) for v in ins],
        out_specs=[spec_of(v) for v in outs],
        out_shape=[
            (pltpu.HBM if isinstance(v, (Out, KeptOut)) else jax.ShapeDtypeStruct)(*spec)
            for v, spec in zip(outs, specs)
        ],
        scratch_shapes=scratch_shapes,
        compiler_params=pltpu.CompilerParams(vmem_limit_bytes=limit * MIB),
        cost_estimate=pl.CostEstimate(
            flops=int(MICROS[name] * 1e9), bytes_accessed=int(MICROS[name] * 1e6), transcendentals=0
        ),
        input_output_aliases=alias or {},
        name=name,
    )(*values)


def nn(left, right, precision=None):
    return lax.dot_general(
        left, right, (((1,), (0,)), ((), ())), precision=precision, preferred_element_type=F32
    )


def nt(left, right, precision=None):
    return lax.dot_general(
        left, right, (((1,), (1,)), ((), ())), precision=precision, preferred_element_type=F32
    )


def tn(left, right, precision=None):
    return lax.dot_general(
        left, right, (((0,), (0,)), ((), ())), precision=precision, preferred_element_type=F32
    )


def total(values):
    return jnp.sum(values, axis=0, keepdims=True)


def centre(values):
    return values - jnp.mean(values, axis=-1, keepdims=True)


def spread_of(centred):
    return lax.rsqrt(jnp.mean(centred * centred, axis=-1, keepdims=True) + EPS)


def norm_back(grad, normed, scale, gain):
    scaled = grad * gain
    mean_one = jnp.mean(scaled, axis=-1, keepdims=True)
    mean_two = jnp.mean(scaled * normed, axis=-1, keepdims=True)
    return scale * (scaled - mean_one - normed * mean_two)


def unit_rows(values):
    scale = lax.rsqrt(jnp.sum(values * values, axis=-1, keepdims=True) + NORM_EPS)
    return values * scale, scale


def unit_back(grad, unit, scale):
    return scale * (grad - unit * jnp.sum(grad * unit, axis=-1, keepdims=True))


def flagged(flag, shape):
    return (jnp.zeros(shape, I32) + flag) > 0


def project_body(first, second, weight, bias, query, key, value, *kept):
    count = first.shape[0]
    copies = []
    if kept:
        *kept, sem_one, sem_two = kept
        for source, out, sem in zip((first, second), kept, (sem_one, sem_two)):
            copy_out(copies, source, out, sem)
    for place, source in enumerate((first, second)):
        rows = slice(place * count, (place + 1) * count)
        block = source[...]
        query[rows, :] = (nn(block, weight[0]) + bias[0:1, :]).astype(BF)
        key[rows, :] = nn(block, weight[1]).astype(BF)
        value[rows, :] = (nn(block, weight[2]) + bias[1:2, :]).astype(BF)
    for copy in copies:
        copy.wait()


def head_masks(rows, heads):
    lanes = lax.broadcasted_iota(I32, rows.shape, 1) // HEAD_DIM
    return [jnp.where(lanes == head, rows, jnp.zeros_like(rows)) for head in range(heads)]


def allowed_pairs(seg_key, seg_query):
    return jnp.concatenate([seg_key] * (seg_query.shape[1] // LANES), axis=1) == seg_query


def attend_body(
    seg_key, seg_query, query, key_near, key_far, val_near, val_far,
    log_total, context_one, context_two, keys, values_t, context_t,
):
    half = key_near.shape[0]
    heads = query.shape[1] // HEAD_DIM
    keys[:half, :], keys[half:, :] = key_near[...], key_far[...]
    values_t[:, :half], values_t[:, half:] = val_near[...].T, val_far[...].T
    allowed = allowed_pairs(seg_key[...], seg_query[0:1, :])
    queries = head_masks(query[...] * BF(0.125), heads)

    def scores(head):
        return jnp.where(allowed, nt(keys[...], queries[head]), -1e30)

    current = scores(0)
    for head in range(heads):
        later = scores(head + 1) if head + 1 < heads else None
        rows = slice(head * HEAD_DIM, (head + 1) * HEAD_DIM)
        top = jnp.max(current, axis=0, keepdims=True)
        exp_terms = jnp.exp(current - top)
        norm = total(exp_terms)
        context_t[rows, :] = nn(values_t[rows, :], exp_terms.astype(BF)) * (1.0 / norm)
        log_total[head : head + 1, :] = top + jnp.log(norm)
        current = later
    log_total[heads:, :] = jnp.zeros((8 - heads, half), F32)
    log_total.flush()
    count = context_one.shape[0]
    context_one[...] = context_t[:, :count].T.astype(BF)
    context_two[...] = context_t[:, count:].T.astype(BF)


def attend_back_body(
    seg_key, seg_query, log_total, grad_one, grad_two, query, context_one, context_two,
    key_near, key_far, val_near, val_far, *refs, lanes, last,
):
    if last:
        key_before, value_before, gq, gk, gv, bias, keys, values, keys_t, grad_t = refs[:10]
        key_sum, value_sum, bias_before = refs[10], refs[11], None
    else:
        gq, key_sum, value_sum, bias, keys, values, keys_t, grad_t = refs
    half = key_near.shape[0]
    width = query.shape[1]
    heads = width // HEAD_DIM
    picked = (
        lax.broadcasted_iota(I32, (8, width), 1) // HEAD_DIM
        == lax.broadcasted_iota(I32, (8, width), 0)
    ).astype(F32)
    keys[:half, :], keys[half:, :] = key_near[...], key_far[...]
    values[:half, :], values[half:, :] = val_near[...], val_far[...]
    keys_t[...] = keys[...].T
    grad_context = jnp.concatenate(
        [grad[:, lane : lane + width] for grad, lane in zip((grad_one, grad_two), lanes)], axis=0
    )
    mixed = jnp.concatenate([context_one[...], context_two[...]], axis=0)
    allowed = allowed_pairs(seg_key[...], seg_query[0:1, :])
    dots = nt(picked, grad_context.astype(F32) * mixed.astype(F32), HIGH)
    queries = head_masks(query[...] * BF(0.125), heads)
    grad_heads = head_masks(grad_context, heads)

    def start(head):
        return nt(keys[...], queries[head]), nt(values[...], grad_heads[head])

    current = start(0)
    for head in range(heads):
        later = start(head + 1) if head + 1 < heads else None
        rows = slice(head * HEAD_DIM, (head + 1) * HEAD_DIM)
        raw, grad_probs = current
        probs = jnp.where(allowed, jnp.exp(raw - log_total[head : head + 1, :]), 0.0)
        grad_scores = (probs * (grad_probs - dots[head : head + 1, :])).astype(BF)
        add_v = nn(probs.astype(BF), grad_heads[head])
        add_k = nn(grad_scores, queries[head])
        if head:
            value_sum[...] += add_v
            key_sum[...] += add_k
        elif last:
            value_sum[...] = value_before[...] + add_v
            key_sum[...] = key_before[...] + add_k
        else:
            value_sum[...], key_sum[...] = add_v, add_k
        grad_t[rows, :] = nn(keys_t[rows, :], grad_scores)
        current = later
    grad_query = (grad_t[...].T * 0.125).astype(BF)
    gq[...] = grad_query
    bias[...] = jnp.zeros_like(bias)
    bias[0:1, :] = total(grad_query.astype(F32))
    if last:
        gk[...] = key_sum[...].astype(BF)
        grad_value = value_sum[...].astype(BF)
        gv[...] = grad_value
        bias[1:2, :] = total(grad_value.astype(F32))


def norm_one_body(
    tower, rows, mixed_0, mixed_1, mixed_2, mixed_3, w_0, w_1, w_2, w_3, w_2_more, w_3_more,
    b_out, gain, shift, hidden, centred,
):
    summed = rows[...].astype(F32) + b_out[...]
    summed = summed + nn(mixed_0[...], w_0[...]) + nn(mixed_1[...], w_1[...])
    here, there = lane_halves(tower, w_2)
    for mixed, weight, more in ((mixed_2, w_2, w_2_more), (mixed_3, w_3, w_3_more)):
        summed = summed + nn(mixed[:, here], weight[...]) + nn(mixed[:, there], more[...])
    middle = centre(summed)
    hidden[...] = (middle * spread_of(middle) * gain[...] + shift[...]).astype(BF)
    centred[...] = middle


def lane_halves(tower, part):
    size = part.shape[0]
    return (
        pl.ds(pl.multiple_of(tower[0] * size, size), size),
        pl.ds(pl.multiple_of((1 - tower[0]) * size, size), size),
    )


def gelu_pair(inner):
    cdf = 0.5 + 0.5 * lax.erf(inner * math.sqrt(0.5))
    density = jnp.exp(-0.5 * inner * inner) * (1.0 / math.sqrt(2.0 * math.pi))
    return (inner * cdf).astype(BF), (cdf + inner * density).astype(BF)


def ffn_body(
    first, second, w_up, b_up, w_down,
    active_one, active_two, slope_one, slope_two, part_one, part_two,
):
    inners = [nn(first[...], w_up[...]) + b_up[...]]
    inners.append(nn(second[...], w_up[...]) + b_up[...])
    places = ((active_one, slope_one, part_one), (active_two, slope_two, part_two))
    for inner, (active, slope, part) in zip(inners, places):
        act, active_slope = gelu_pair(inner)
        active[...] = act
        active.flush()
        slope[...] = active_slope
        slope.flush()
        part[...] = nn(act, w_down[...]).astype(BF)


def ffn_only_body(rows, w_up, b_up, w_down, part):
    inner = nn(rows[...], w_up[...]) + b_up[...]
    act = (inner * (0.5 + 0.5 * lax.erf(inner * math.sqrt(0.5)))).astype(BF)
    part[...] = nn(act, w_down[...]).astype(BF)


def ffn_keep_body(
    first, second, w_up, b_up,
    active_one, active_two, slope_one, slope_two, copy_one, copy_two,
):
    copy_one[...], copy_two[...] = first[...], second[...]
    copy_one.flush()
    copy_two.flush()
    for rows, active, slope in ((first, active_one, slope_one), (second, active_two, slope_two)):
        active[...], slope[...] = gelu_pair(nn(rows[...], w_up[...]) + b_up[...])
        active.flush()
        slope.flush()


def head_rows(centred, gain_one, shift_one, part, near, far, b_down, gain, shift):
    hidden = centred[...] * spread_of(centred[...]) * gain_one[...] + shift_one[...]
    summed = part[...].astype(F32) + near[...].astype(F32) + far[...].astype(F32)
    middle = centre(hidden + summed + b_down[...])
    return middle, middle * spread_of(middle) * gain[...] + shift[...]


def head_body(
    centred, gain_one, shift_one, part, near, far, b_down, gain, shift,
    col_weight, b_col, pick, cls_own, send, send_half,
):
    _, final = head_rows(centred, gain_one, shift_one, part, near, far, b_down, gain, shift)
    col, _ = unit_rows(nn(final.astype(BF), col_weight[...]) + b_col[...])
    cls, _ = unit_rows(nn(pick[...], final, HIGH))
    count = send_half.shape[0]
    col = col.astype(BF)
    cls_own[...] = jnp.concatenate([cls, jnp.zeros_like(cls)], axis=0).astype(BF)
    send[...] = col
    send_half[...] = col[count:]


def head_keep_body(
    centred, gain_one, shift_one, part, near, far, b_down, gain, shift,
    col_weight, b_col, pick, encoded, middle, col_pre, cls_raw,
):
    kept, final = head_rows(centred, gain_one, shift_one, part, near, far, b_down, gain, shift)
    middle[...] = kept
    middle.flush()
    encoded[...] = final.astype(BF)
    encoded.flush()
    col_pre[...] = nn(final.astype(BF), col_weight[...]) + b_col[...]
    col_pre.flush()
    cls_raw[...] = nn(pick[...], final, HIGH)


def similar_body(is_query, own, *refs):
    pieces, (weight_p, exp_terms, others, sums) = refs[:6], refs[6:]
    count = own.shape[0]
    row = 0
    for piece in pieces:
        rows = slice(row, row + piece.shape[0])
        others[rows, :] = piece[...]
        exp_terms[:, rows] = jnp.exp(SHARP * nt(own[...], piece[...]))
        row += piece.shape[0]
    weight = weight_p[...].astype(BF)
    terms = exp_terms[...]
    high = terms.astype(BF)
    low = (terms - high.astype(F32)).astype(BF)
    sums_q = nt(weight, high) + nt(weight, low)
    sums_p = nn(weight[:, :count], high) + nn(weight[:, :count], low)
    sums_q = jnp.concatenate([sums_q, jnp.zeros((sums_q.shape[0], 3 * count), F32)], axis=1)
    sums[...] = jnp.where(flagged(is_query[0], sums_p.shape), sums_q, sums_p)


def dense_body(is_query, vectors, targets, cls_raw, grad_cls, loss):
    block = vectors[...]
    shape = (block.shape[0], block.shape[0])
    segs = cls_raw.shape[0]
    kind_rows = block.shape[0] // 2
    query_kind = 1 - is_query[0]
    row_kind = lax.broadcasted_iota(I32, shape, 0) // kind_rows
    col_kind = lax.broadcasted_iota(I32, shape, 1) // kind_rows
    paired = jnp.logical_and(row_kind == query_kind, col_kind != query_kind)
    logits = jnp.where(paired, nt(block, block) * SCALE_DENSE, -1e30)
    onehot = targets[...]
    top = jnp.max(logits, axis=1, keepdims=True)
    exp_terms = jnp.where(paired, jnp.exp(logits - top), 0.0)
    norm = jnp.sum(exp_terms, axis=1, keepdims=True)
    norm = jnp.where(norm > 0.0, norm, 1.0)
    grad = ((exp_terms / norm - onehot) * (1.0 / segs)).astype(BF)
    grad = jnp.where(paired, grad, jnp.zeros_like(grad))
    hit = jnp.sum(jnp.where(paired, logits * onehot, 0.0), axis=1, keepdims=True)
    losses = top + jnp.log(norm) - hit
    rows = lax.broadcasted_iota(I32, losses.shape, 0) - query_kind * kind_rows
    mine = jnp.logical_and(rows >= 0, rows < segs)
    loss[...] = jnp.zeros_like(loss) + jnp.sum(jnp.where(mine, losses, 0.0))
    grad_rows = nn(grad[: 2 * segs], block)[:segs]
    grad_cols = tn(grad[:, : 2 * segs], block)[:segs]
    own = jnp.where(flagged(is_query[0], grad_rows.shape), grad_rows, grad_cols) * SCALE_DENSE
    grad_cls[...] = unit_back(own, *unit_rows(cls_raw[...]))


def score_body(
    is_query, sums, exp_terms, others, weight_q, weight_p, target, col_pre,
    grad_pre, scores,
):
    count = exp_terms.shape[0]
    segs = weight_q.shape[0]
    seg_sums = sums[...]
    w_q, w_p = weight_q[...], weight_p[...]
    size = jnp.sum(w_q, axis=1, keepdims=True)
    nearest = jnp.log(seg_sums) * (1.0 / SHARP)
    pair = nt(w_q, nearest, HIGH) / size
    scores[...] = pair
    logits = pair * SCALE_COL
    onehot = target[...]
    top = jnp.max(logits, axis=1, keepdims=True)
    terms = jnp.exp(logits - top)
    norm = jnp.sum(terms, axis=1, keepdims=True)
    grad_pair = (terms / norm - onehot) * (SCALE_COL / segs) / size
    grad_sums = tn(grad_pair, w_q, HIGH) / (SHARP * seg_sums)
    left = jnp.where(
        flagged(is_query[0], (segs, count)), grad_sums[:, :count], w_p[:, :count]
    )
    right = jnp.where(flagged(is_query[0], w_p.shape), w_p, grad_sums)
    grad_similar = (tn(left, right, HIGH) * (exp_terms[...] * SHARP)).astype(BF)
    grad_vec = nn(grad_similar, others[...])
    pre = unit_back(grad_vec, *unit_rows(col_pre[...])).astype(BF)
    grad_pre[...] = pre


def norm_two_back_rows(grad_pre, col_weight, grad_cls, pick, middle, gain):
    grad_final = nt(grad_pre[...], col_weight[...]) + tn(pick[...], grad_cls[...], HIGH)
    spread = spread_of(middle[...])
    unit = middle[...] * spread
    return norm_back(grad_final, unit, spread, gain[...]), grad_final, unit


def norm_two_back_body(grad_pre, col_weight, grad_cls, pick, middle, gain, grad_b):
    back, _, _ = norm_two_back_rows(grad_pre, col_weight, grad_cls, pick, middle, gain)
    grad_b[...] = back.astype(BF)


def norm_two_keep_body(
    grad_pre, col_weight, grad_cls, pick, middle, gain, scores, target, dense_loss,
    grad_two, grad_kept, small,
):
    back, grad_final, unit = norm_two_back_rows(
        grad_pre, col_weight, grad_cls, pick, middle, gain
    )
    grad_kept[...] = back.astype(BF)
    grad_kept.flush()
    grad_two[...] = back
    grad_two.flush()
    logits = scores[...] * SCALE_COL
    top = jnp.max(logits, axis=1, keepdims=True)
    norm = jnp.sum(jnp.exp(logits - top), axis=1, keepdims=True)
    losses = top + jnp.log(norm) - jnp.sum(logits * target[...], axis=1, keepdims=True)
    small[0:1, :] = total(grad_pre[...].astype(F32))
    small[1:2, :] = total(back)
    small[2:3, :] = total(grad_final * unit)
    small[3:4, :] = total(grad_final)
    small[4:5, :] = jnp.zeros((1, unit.shape[1]), F32) + (jnp.sum(losses) + dense_loss[0:1, 0:1])
    small[5:8, :] = jnp.zeros((3, unit.shape[1]), F32)


def ffn_back_body(
    first, second, slope_one, slope_two, w_down, w_up,
    inner_one, inner_two, part_one, part_two, bias,
):
    bias_sum = jnp.zeros((1, slope_one.shape[1]), F32)
    raws = [nt(second[...], w_down[...]), nt(first[...], w_down[...])]
    for raw, slope, inner in zip(raws, (slope_two, slope_one), (inner_two, inner_one)):
        grad = (raw * slope[...].astype(F32)).astype(BF)
        inner[...] = grad
        inner.flush()
        bias_sum = bias_sum + total(grad.astype(F32))
    part_two[...] = nt(inner_two[...], w_up[...]).astype(BF)
    part_one[...] = nt(inner_one[...], w_up[...]).astype(BF)
    bias[...] = bias_sum


def ffn_back_only_body(rows, slope, w_down, w_up, part):
    inner = (nt(rows[...], w_down[...]) * slope[...].astype(F32)).astype(BF)
    part[...] = nt(inner, w_up[...]).astype(BF)


def ffn_back_keep_body(first, second, slope_one, slope_two, w_down, inner_one, inner_two, bias):
    bias_sum = jnp.zeros((1, slope_one.shape[1]), F32)
    for rows, slope, inner in ((first, slope_one, inner_one), (second, slope_two, inner_two)):
        grad = (nt(rows[...], w_down[...]) * slope[...].astype(F32)).astype(BF)
        inner[...] = grad
        inner.flush()
        bias_sum = bias_sum + total(grad.astype(F32))
    bias[...] = bias_sum


def norm_one_back_body(
    tower, grad_two, part, near, far, centred, gain, w_0, w_1, w_2, w_3, w_2_more, w_3_more,
    grad_one, grad_b, small, mixed_0, mixed_2, mixed_13,
):
    grad = (
        grad_two[...]
        + part[...].astype(F32)
        + near[...].astype(F32)
        + far[...].astype(F32)
    )
    spread = spread_of(centred[...])
    unit = centred[...] * spread
    back = norm_back(grad, unit, spread, gain[...])
    grad_one[...] = back
    grad_one.flush()
    rounded = back.astype(BF)
    grad_b[...] = rounded
    grad_b.flush()
    width = mixed_0.shape[1]
    size = w_2.shape[0]
    for weight, more, mixed, lane in (
        (w_3, w_3_more, mixed_13, width), (w_2, w_2_more, mixed_2, 0)
    ):
        for part, side in ((weight, tower[0]), (more, 1 - tower[0])):
            lanes = pl.ds(pl.multiple_of(side * size + lane, size), size)
            mixed[:, lanes] = nt(rounded, part[...]).astype(BF)
    mixed_13[:, :width] = nt(rounded, w_1[...]).astype(BF)
    mixed_0[...] = nt(rounded, w_0[...]).astype(BF)
    small[0:1, :] = total(back)
    small[1:2, :] = total(grad * unit)
    small[2:3, :] = total(grad)
    small[3:8, :] = jnp.zeros((5, unit.shape[1]), F32)


def input_grad_body(
    query_near, query_far, grad_key, grad_value, weight, part_0, part_2, part_31
):
    count = part_0.shape[0]
    places = ((3, part_31, 0), (1, part_31, count), (2, part_2, 0), (0, part_0, 0))
    for block, out, row in places:
        own = slice(block % 2 * count, (block % 2 + 1) * count)
        rows = slice(block * count, (block + 1) * count)
        out[row : row + count, :] = (
            nt((query_near, query_far)[block // 2][own, :], weight[0])
            + nt(grad_key[rows, :], weight[1])
            + nt(grad_value[rows, :], weight[2])
        ).astype(BF)


def order_rows(place, source, out, size):
    for block in range(source.shape[1] // size):
        start = pl.multiple_of((jnp.int32(block) ^ place) * size, size)
        out[block * size : (block + 1) * size, :] = source[:, pl.ds(start, size)].T


def weight_grad_body(place, *refs, lefts, rights, cuts, first):
    left = refs[:lefts]
    right = refs[lefts : lefts + sum(rights)]
    outs, (ordered, joined) = refs[lefts + sum(rights) : -2], refs[-2:]
    token = 0
    for part in left:
        tokens = slice(token, token + part.shape[0])
        order_rows(place[0], part, ordered.at[:, tokens], LANES)
        token += part.shape[0]
    at = 0
    lane = 0
    for group in rights:
        token = 0
        for part in right[at : at + group]:
            rows = part.shape[0]
            lanes = min(part.shape[1], joined.shape[1])
            joined[token : token + rows, lane : lane + lanes] = part[:, first : first + lanes]
            token += rows
        at += group
        lane += lanes
    half = ordered.shape[0] // 2
    lane = 0
    for cut, (keep, send) in zip(cuts, zip(outs[::2], outs[1::2])):
        lanes = slice(lane, lane + cut)
        for rows, out in ((slice(half, 2 * half), send), (slice(0, half), keep)):
            out[...] = nn(ordered[rows, :], joined[:, lanes]).astype(BF)
            if isinstance(out, Leaving):
                out.flush()
        lane += cut


def turned_grad_body(place, mp_place, grad, *refs, rows):
    left, (part_0, part_2, part_31, ordered) = refs[:-4], refs[-4:]
    order_rows(place[0], grad, ordered, LANES)
    outs = ((0, part_0, 0), (2, part_2, 0), (3, part_31, 0), (1, part_31, rows))
    for block, out, lane in outs:
        if len(left) == 1:
            start = pl.multiple_of((jnp.int32(block) ^ mp_place[0]) * rows, rows)
            right = left[0][:, pl.ds(start, rows)]
        else:
            right = left[block][...]
        out[:, lane : lane + rows] = nn(ordered[...], right).astype(BF)
        if isinstance(out, Leaving):
            out.flush()


def place_col_body(mp_place, tower, w_0, w_1, w_2, w_3, w_2_more, w_3_more, out):
    count = w_0.shape[0]
    here, there = lane_halves(tower, w_2)
    for block, parts in enumerate(((w_0,), (w_1,), (w_2, w_2_more), (w_3, w_3_more))):
        start = pl.multiple_of((jnp.int32(block) ^ mp_place[0]) * count, count)
        if len(parts) == 1:
            out[pl.ds(start, count), :] = parts[0][...]
        else:
            size = parts[0].shape[0]
            out[pl.ds(pl.multiple_of(start + tower[0] * size, size), size), :] = parts[0][...]
            out[pl.ds(pl.multiple_of(start + (1 - tower[0]) * size, size), size), :] = parts[1][...]


def copy_out(copies, source, target, sem):
    copies.append(pltpu.make_async_copy(source, target, sem))
    copies[-1].start()


def place_wide_body(place, *refs, size):
    *parts, out, buffer = refs[: -8]
    sems = refs[-8:]
    copies = []
    cut = parts[0].shape[1]
    for block in range(8):
        here = pl.ds(block * size, size)
        start = pl.multiple_of((jnp.int32(block) ^ place[0]) * size, size)
        row = block % 4 * size
        for column in range(len(parts) // 2):
            part = parts[2 * column + block // 4]
            lanes = slice(column * cut, (column + 1) * cut)
            buffer[here, lanes] = part[row : row + size, :].astype(F32)
        copy_out(copies, buffer.at[here], out.at[pl.ds(start, size)], sems[block])
    for copy in copies:
        copy.wait()


def place_qkv_body(place, one, one_more, qkv, buffer, *sems, size):
    copies = []
    width = qkv.shape[2]
    for block in range(8):
        here = pl.ds(block * size, size)
        start = pl.multiple_of((jnp.int32(block) ^ place[0]) * size, size)
        rows = slice(block % 4 * size, (block % 4 + 1) * size)
        part = (one, one_more)[block // 4]
        for kind in range(3):
            lanes = slice(kind * width, (kind + 1) * width)
            buffer[kind, here, :] = part[rows, lanes].astype(F32)
            copy_out(
                copies,
                buffer.at[kind, here],
                qkv.at[kind, pl.ds(start, size)],
                sems[3 * block + kind],
            )
    for copy in copies:
        copy.wait()


def place_last_body(place, one, one_more, out, col, *, size):
    width = out.shape[0]
    for block in range(8):
        start = pl.multiple_of((jnp.int32(block) ^ place[0]) * size, size)
        rows = slice(block % 4 * size, (block % 4 + 1) * size)
        part = (one, one_more)[block // 4]
        out[:, pl.ds(start, size)] = part[rows, :width].astype(F32).T
        col[:, pl.ds(start, size)] = part[rows, width:].astype(F32).T


def dp_bits():
    return [1 << k for k in range(int(math.log2(lax.axis_size("dp"))))]


def add(*values):
    return sum(value.astype(F32) for value in values).astype(BF)


def side_of(axis, bit):
    return jnp.minimum(lax.axis_index(axis) & bit, 1)


def join(value, other, axis, bit):
    return jnp.where(
        side_of(axis, bit) == 0,
        jnp.concatenate([value, other]),
        jnp.concatenate([other, value]),
    )


def more_bits():
    return [("dp", bit) for bit in dp_bits()[2:]]


def sum_more(value):
    for axis, bit in more_bits():
        half = value.shape[0] // 2
        side = side_of(axis, bit)
        sent = lax.dynamic_slice_in_dim(value, (1 - side) * half, half, 0)
        kept = lax.dynamic_slice_in_dim(value, side * half, half, 0)
        value = add(kept, swap(sent, axis, bit))
    for axis, bit in more_bits()[::-1]:
        value = join(value, swap(value, axis, bit), axis, bit)
    return value


HOPS = (("tower", 1), ("dp", 1), ("dp", 2))


class Unit:
    def __init__(self, keep, send):
        self.value, self.send, self.stage = keep, send, 0

    def hop(self):
        return HOPS[min(self.stage, 5 - self.stage)]

    def land(self, got):
        self.stage += 1
        if self.stage <= 3:
            value = self.value.astype(F32) + got.astype(F32)
            if self.stage < 3:
                half = value.shape[0] // 2
                self.value, self.send = value[:half], value[half:].astype(BF)
            else:
                self.send = sum_more(value.astype(BF))
        elif self.stage < 6:
            self.send = jnp.concatenate([self.send, got])
        else:
            self.halves = (self.send, got)


class Small:
    def __init__(self, value):
        self.send, self.stage = value, 0

    def hop(self):
        return HOPS[self.stage]

    def land(self, got):
        self.stage += 1
        self.send = self.send + got
        if self.stage == 3:
            for axis, bit in more_bits():
                self.send = self.send + swap(self.send, axis, bit)


def together(*values):
    return lax.optimization_barrier(values)


def launch(units):
    groups = {}
    for unit in units:
        groups.setdefault((unit.hop(), unit.send.dtype), []).append(unit)
    started = []
    for (hop, _), group in groups.items():
        send = group[0].send
        if len(group) > 1:
            send = jnp.concatenate([unit.send for unit in group], axis=1)
        started.append((group, send, swap(send, *hop)))
    return started


def land(started, *others):
    flights = [flight for _, _, flight in started]
    sizes = [value.size * value.dtype.itemsize for value in flights]
    soon = [k for k, size in enumerate(sizes) if size < max(sizes)]
    late = [k for k in range(len(flights)) if k not in soon]
    done = together(*[flights[k] for k in soon], *others)
    done = together(*done, *[flights[k] for k in late])
    others = done[len(soon) : len(soon) + len(others)]
    landed = done[: len(soon)] + done[len(soon) + len(others) :]
    arrived = []
    for k, got in sorted(zip(soon + late, landed), key=lambda pair: pair[0]):
        group = started[k][0]
        if group is None:
            arrived.append(got)
            continue
        lane = 0
        for unit in group:
            width = unit.send.shape[1]
            unit.land(got if len(group) == 1 else got[:, lane : lane + width])
            lane += width
    return arrived, list(others)


def move(value, hop):
    return (None, value, swap(value, *hop))


def phase(units=(), moves=(), fill=None, then=None, more=()):
    if moves:
        for unit in units:
            unit.send = after(unit.send, moves[0][0])
    started = [move(value, hop) for value, hop in moves] + launch(units)
    ready = [send for _, send, _ in started]
    filled = list(fill(lambda value: after(value, *ready))) if fill else []
    extra = launch([then(filled)]) if then else []
    arrived, filled = land(started + list(more), *filled)
    return (arrived, filled, extra) if then else (arrived, filled)


def place_of(hops):
    place = 0
    for axis, bit in hops:
        place = place * 2 + side_of(axis, bit)
    return place[None].astype(I32)


def relative(values, mp_index):
    size = values.shape[-1] // 4
    blocks = [values[..., k * size : (k + 1) * size] for k in range(4)]
    values = jnp.where(mp_index & 1, jnp.concatenate([blocks[k ^ 1] for k in range(4)], -1), values)
    blocks = [values[..., k * size : (k + 1) * size] for k in range(4)]
    return jnp.where(mp_index & 2, jnp.concatenate([blocks[k ^ 2] for k in range(4)], -1), values)


def flip(values, bit):
    size = values.shape[-1] // 4
    return jnp.concatenate([values[:, (k ^ bit) * size :][:, :size] for k in range(4)], axis=1)


def per_device(
    tokens,
    segment_ids,
    key_mask,
    positives,
    w_qkv,
    b_qv,
    w_out,
    b_out,
    gain_one,
    shift_one,
    w_up,
    b_up,
    w_down,
    b_down,
    gain_two,
    shift_two,
    w_col,
    b_col,
):
    own_rows = tokens[0, 0]
    count, model_dim = own_rows.shape
    pair, width = 2 * count, w_out.shape[0]
    half = count // 2
    units = w_up.shape[1]
    segs = positives.shape[1]
    dp_size = lax.axis_size("dp")
    mp_index = lax.axis_index("mp")
    dp_index = lax.axis_index("dp")
    tower = lax.axis_index("tower")
    is_query = tower == 0
    query_flag = (1 - tower)[None].astype(I32)
    mp_place = mp_index[None].astype(I32)
    rest_place = place_of(HOPS)
    tower_place = tower[None].astype(I32)
    labels = jnp.arange(segs, dtype=I32)
    row = lambda vector: vector[None, :]
    block_bf = ((count, model_dim), BF)
    block_f32 = ((count, model_dim), F32)

    def core(block):
        return swap(block, "mp", 1)

    def across(block):
        return swap(block, "mp", 2)

    x_0, x_1, x_2 = own_rows, core(own_rows), across(own_rows)
    w_three = jnp.transpose(w_qkv, (1, 0, 2))

    seg_pair = segment_ids[:, 0]
    starts = jnp.concatenate([jnp.ones((2, 1), bool), seg_pair[:, 1:] != seg_pair[:, :-1]], axis=1)
    valid_pair = jnp.logical_or(key_mask[:, 0] > 0, starts)
    codes = relative(seg_pair + 16 * valid_pair.astype(I32) + 32 * starts.astype(I32), mp_index)
    seg_rel, valid_rel = codes & 15, (codes & 16) > 0
    code_row = jnp.where(is_query, codes[0], codes[1])
    seg_row = code_row & 15
    seg_key = jnp.broadcast_to(
        jnp.where((code_row & 16) > 0, seg_row, -1)[:, None], (4 * count, LANES)
    )
    seg_query = jnp.broadcast_to(seg_row[None, :], (8, 4 * count))
    members = seg_rel[:, None, :] == labels[None, :, None]
    weights = jnp.logical_and(members, valid_rel[:, None, :]).astype(F32)
    weight_q, weight_p = weights[0], weights[1]
    pick = (code_row[None, :count] - 32 == labels[:, None] + 16).astype(F32)
    order = dp_index ^ jnp.arange(dp_size, dtype=I32)
    kinds = jnp.arange(2, dtype=I32)[:, None, None]
    targets = (
        (1 - tower) * dp_size * segs
        + jnp.arange(dp_size, dtype=I32)[None, :, None] * segs
        + positives[order][None]
    )
    targets = jnp.where(kinds == tower, targets, -1).reshape(2 * dp_size * segs)
    paired = (targets[:, None] == jnp.arange(2 * dp_size * segs, dtype=I32)).astype(F32)
    positive_row = lax.dynamic_index_in_dim(positives, dp_index, 0, keepdims=False)
    positive_row = (positive_row[:, None] == labels).astype(F32)

    half_bf = ((pair, width), BF)
    mixed_bf = ((count, width), BF)
    x_hop, core_hop, y_hop = ("mp", 2), ("mp", 1), ("tower", 1)

    def project(first, second, kept=()):
        return call(
            project_body,
            "project",
            [first, second, w_three, b_qv],
            [half_bf] * 3 + list(kept),
            semaphores=len(kept),
        )

    near_qkv = project(x_0, x_1)
    halves = [
        lax.dynamic_slice_in_dim(weight, tower * half, half, 0) for weight in (w_out, w_col)
    ]
    x_2, out_half, col_half, out_1, col_1 = together(
        x_2, *halves, core(w_out), core(w_col), near_qkv,
        seg_key, seg_query, weight_q, weight_p, pick, paired, positive_row,
    )[:5]
    x_3 = core(x_2)
    out_2, col_2 = across(out_half), across(col_half)
    far_qkv = project(x_2, x_3, [KeptOut(*block_bf)] * 2)
    x_2_kept, x_3_kept = far_qkv[3:]
    key_values = [near_qkv[1], far_qkv[1], near_qkv[2], far_qkv[2]]
    seg_query_near, seg_query_far = seg_query[:, :pair], seg_query[:, pair:]

    def attend(seg_half, query):
        return call(
            attend_body,
            "attend",
            [seg_key, seg_half, query, *key_values],
            [Out((8, pair), F32), mixed_bf, mixed_bf],
            [((4 * count, width), BF), ((width, 4 * count), BF), ((width, pair), F32)],
        )

    total_far, mixed_far_2, mixed_far_3 = attend(seg_query_far, far_qkv[0])
    mixed_far_2, mixed_far_3, out_2 = together(mixed_far_2, mixed_far_3, out_2)
    (out_2_more, mixed_2, mixed_1_2), (total_near, mixed_0, mixed_near_1, col_2) = phase(
        (),
        [(out_2, y_hop), (mixed_far_2, x_hop), (mixed_far_3, x_hop)],
        lambda late: [*attend(seg_query_near, late(near_qkv[0])), col_2],
    )
    (mixed_1, mixed_3, out_3, out_3_more), _ = phase(
        (),
        [(mixed_near_1, core_hop), (mixed_1_2, core_hop), (out_2, core_hop)]
        + [(out_2_more, core_hop)],
    )
    col_3 = core(col_2)
    mixed = [mixed_0, mixed_1, mixed_2, mixed_3]
    outs = [w_out, out_1, out_2, out_3, out_2_more, out_3_more]
    hidden, centred_one = call(
        norm_one_body,
        "norm_one",
        [tower_place, own_rows, *mixed, *outs, row(b_out), row(gain_one), row(shift_one)],
        [block_bf, block_f32],
    )

    h_0, h_1 = hidden, core(hidden)
    kept_bf = Out((count, units), BF)
    (h_2, col_2_more), (act_0, act_1, slope_0, slope_1, part_0, part_1) = phase(
        (),
        [(hidden, x_hop), (col_2, y_hop)],
        lambda late: call(
            ffn_body,
            "feed_forward",
            [h_0, h_1, w_up, row(b_up), w_down],
            [kept_bf] * 4 + [Out(*block_bf), block_bf],
        ),
    )
    h_3, col_3_more = core(h_2), core(col_2_more)

    def feed_far(rows):
        return call(
            ffn_only_body, "feed_far", [rows, w_up, row(b_up), w_down], [block_bf]
        )[0]

    part_2 = feed_far(h_2)
    part_3 = feed_far(after(h_3, part_2))
    near_sum = core(part_1)
    joined = add(part_2, core(part_3))
    joined, near_sum = together(joined, near_sum)
    (arrived,), (act_2, act_3, slope_2, slope_3, h_2_kept, h_3_kept, col_weight) = phase(
        (),
        [(joined, x_hop)],
        lambda late: [
            *call(
                ffn_keep_body,
                "feed_keep",
                [late(h_2), h_3, w_up, row(b_up)],
                [kept_bf] * 4 + [Out(*block_bf)] * 2,
            ),
            *call(
                place_col_body,
                "place_col",
                [mp_place, tower_place, w_col, late(col_1), col_2, col_3, col_2_more, col_3_more],
                [((model_dim, model_dim), BF)],
            ),
        ],
    )
    ins = [centred_one, row(gain_one), row(shift_one), part_0, near_sum, arrived]
    ins += [row(b_down), row(gain_two), row(shift_two), col_weight, row(b_col), pick]
    cls_own, send, send_half = call(
        head_body,
        "heads",
        ins,
        [((2 * segs, model_dim), BF), block_bf, ((half, model_dim), BF)],
    )

    cls_own = cls_own[:segs]
    (other, own_half, cls_far), (encoded, middle, col_pre, cls_raw) = phase(
        (),
        [(send, y_hop), (send_half, x_hop), (cls_own, ("dp", 1))],
        lambda late: call(
            head_keep_body,
            "heads_keep",
            [late(centred_one)] + ins[1:],
            [Out(*block_bf), Out(*block_f32), Out(*block_f32), Out((segs, model_dim), F32)],
        ),
    )
    cls_all = jnp.concatenate([cls_own, cls_far])
    (far_b, far_a, cls_far), _ = phase(
        (), [(own_half, y_hop), (other[:half], x_hop), (cls_all, ("dp", 2))]
    )
    cls_all = jnp.concatenate([cls_all, cls_far])
    for bit in dp_bits()[2:]:
        cls_all = jnp.concatenate([cls_all, swap(cls_all, "dp", bit)])
    (near, diag_a, diag_b, cls_near), _ = phase(
        (),
        [(other, core_hop), (far_a, core_hop), (far_b, core_hop), (cls_all, core_hop)],
    )
    cls_all = add(cls_all, cls_near)
    pieces = [other, near, far_a, far_b, diag_a, diag_b]
    exp_terms, others, sums = call(
        similar_body,
        "similar",
        [query_flag, send, *pieces, weight_p],
        [((count, 4 * count), F32), ((4 * count, model_dim), BF), ((segs, 4 * count), F32)],
    )
    cls_all = after(cls_all, sums)
    (swapped, cls_far), _ = phase((), [(sums, x_hop), (cls_all, x_hop)])
    sums = sums + flip(swapped, 2)
    cls_all = add(cls_all, cls_far)
    (swapped,), _ = phase((), [(sums, core_hop)])
    sums = sums + flip(swapped, 1)
    (cls_other,), (grad_pre, pair_score) = phase(
        (),
        [(after(cls_all, sums), y_hop)],
        lambda late: call(
            score_body,
            "scores",
            [query_flag, late(sums), exp_terms, others, weight_q, weight_p, positive_row, col_pre],
            [block_bf, ((segs, segs), F32)],
        ),
    )
    grad_cls, dense_loss = call(
        dense_body,
        "dense",
        [query_flag, jnp.concatenate([cls_all, cls_other]), paired, cls_raw],
        [((segs, model_dim), F32), ((8, LANES), F32)],
    )
    ins = [grad_pre, col_weight, grad_cls, pick, middle, row(gain_two)]
    (grad_two_b,) = call(norm_two_back_body, "norm_two_back", ins, [block_bf])

    def streams(*values):
        return [Stream(value) for value in values]

    def feed_back(first, second, slope_one, slope_two, part):
        return call(
            ffn_back_body,
            "feed_back",
            [first, second, *streams(slope_one, slope_two), w_down, w_up],
            [kept_bf] * 2 + [part, block_bf, Out((1, units), F32)],
            limit=12,
        )

    def weight_grad(left, right, cuts, first=0):
        rows = getattr(left[0], "value", left[0]).shape[1]
        tokens = 4 * count
        outs = [Out((rows // 2, cut), BF) for cut in cuts for _ in range(2)]
        outs[1] = ((rows // 2, cuts[0]), BF)
        return call(
            functools.partial(
                weight_grad_body,
                lefts=len(left),
                rights=[len(parts) for parts in right],
                cuts=cuts,
                first=first,
            ),
            "weight_grad",
            [rest_place, *left, *[part for parts in right for part in parts]],
            outs,
            [((rows, tokens), BF), ((tokens, sum(cuts)), BF)],
            limit=20,
        )

    def turned_grad(grad, left):
        return call(
            functools.partial(turned_grad_body, rows=count),
            "turned_grad",
            [rest_place, mp_place, grad, *left],
            [Out((model_dim, count), BF)] * 2 + [((model_dim, 2 * count), BF)],
            [((model_dim, count), BF)],
        )

    def near_back(late):
        backs = feed_back(grad_two_b, g_1, slope_0, slope_1, Out(*block_bf))
        kept = call(
            norm_two_keep_body,
            "norm_two_keep",
            [after(grad_pre, backs[3])] + ins[1:] + [pair_score, positive_row, dense_loss],
            [Out(*block_f32), Out(*block_bf), Out((8, model_dim), F32)],
        )
        turned = turned_grad(Stream(after(grad_pre, kept[2])), [Stream(encoded)])
        return [*backs, *kept, *turned]

    g_1 = core(grad_two_b)
    (g_2,), (inner_0, inner_1, part_0, part_1, bias_near, *kept) = phase(
        (), [(grad_two_b, x_hop)], near_back
    )
    grad_two, grad_two_kept, small_two, col_own, col_joined, col_near = kept
    g_3 = core(g_2)

    def feed_back_far(rows, slope):
        return call(
            ffn_back_only_body, "feed_back_far", [rows, slope, w_down, w_up], [block_bf]
        )[0]

    part_2 = feed_back_far(g_2, slope_2)
    part_3 = feed_back_far(after(g_3, part_2), slope_3)
    cut = model_dim // 2

    def down_grad(late, start):
        return weight_grad(
            streams(act_0, act_1, act_2, act_3),
            [[Stream(grad_two_kept), Stream(g_1), late(g_2), g_3]],
            [cut],
            start,
        )

    (near_sum, arrived), down = phase(
        (), [(part_1, core_hop), (part_3, core_hop)], lambda late: down_grad(late, 0)
    )
    down = [Unit(*down)]
    joined = add(part_2, arrived)

    def unit_grads(late):
        more = down_grad(late, cut)
        inner_2, inner_3, bias_far = call(
            ffn_back_keep_body,
            "feed_back_keep",
            [after(g_2, more[1]), g_3, slope_2, slope_3, w_down],
            [kept_bf] * 2 + [Out((1, units), F32)],
        )
        up = weight_grad(
            streams(after(h_0, bias_far), h_1, h_2_kept, h_3_kept),
            [streams(inner_0, inner_1, inner_2, inner_3)],
            [cut, cut],
        )
        return [*more, *up, bias_far]

    (arrived,), (_, _, *up, bias_far), more = phase(
        down, [(joined, x_hop)], unit_grads, then=lambda filled: Unit(*filled[:2])
    )
    down.append(more[0][0][0])
    up = [Unit(*up[:2]), Unit(*up[2:])]
    grad_one, grad_one_b, small_one, back_0, back_2, back_13 = call(
        norm_one_back_body,
        "norm_one_back",
        [tower_place, grad_two, part_0, near_sum, arrived, centred_one, row(gain_one), *outs],
        [Out(*block_f32), Out(*block_bf), ((8, model_dim), F32)]
        + [mixed_bf, mixed_bf, ((count, 2 * width), BF)],
        limit=12,
    )

    (back_13,), _ = phase((), [(back_13, core_hop)])
    back_23 = jnp.concatenate([back_2, back_13[:, width:]], axis=1)
    all_bf, all_f32 = ((4 * count, width), BF), ((4 * count, width), F32)
    back_scratch = [all_bf] * 2 + [((width, 4 * count), BF), ((width, pair), F32)]

    def back_ins(seg_half, log_total, grads, query, mixed_pair):
        return [seg_key, seg_half, log_total, *grads, query, *mixed_pair, *key_values]

    back_hop = move(back_23, x_hop)
    grad_q_near, key_sum, value_sum, bias_near_q = call(
        functools.partial(attend_back_body, lanes=(0, 0), last=False),
        "attend_back",
        back_ins(
            seg_query_near,
            total_near,
            [after(back_0, back_23), back_13],
            near_qkv[0],
            (mixed_0, mixed_near_1),
        ),
        [half_bf, all_f32, all_f32, ((8, width), F32)],
        back_scratch,
        limit=16,
    )
    _, (grad_q_near,) = land(more, grad_q_near)
    up[0].send = after(up[0].send, down[1].send)
    started = launch([*down, up[0]])
    out_own, out_joined, out_near = turned_grad(
        Stream(after(grad_one_b, *[send for _, send, _ in started])), streams(*mixed)
    )
    (back_23, col_near), (out_near,) = land([back_hop, move(col_near, core_hop)], out_near)
    grad_q_far, grad_k, grad_v, bias_far_v = call(
        functools.partial(attend_back_body, lanes=(0, width), last=True),
        "attend_back",
        back_ins(
            seg_query_far,
            total_far,
            [after(back_23, out_near), back_23],
            far_qkv[0],
            (mixed_far_2, mixed_far_3),
        )
        + [key_sum, value_sum],
        [half_bf, all_bf, all_bf, ((8, width), F32)],
        back_scratch + [all_f32, all_f32],
        limit=16,
    )
    _, (grad_v,) = land(started, grad_v)
    col_joined = add(col_joined, col_near[:, :count])
    col_own = add(col_own, col_near[:, count:])
    up[1].send = after(up[1].send, down[0].send)
    started = [move(out_near, core_hop), move(col_joined, x_hop)]
    started += launch([up[1], up[0], *down])
    qkv = Unit(
        *weight_grad(
            [after(x_0, grad_v, *[send for _, send, _ in started]), x_1, x_2_kept, x_3_kept],
            [[grad_q_near, grad_q_far], [grad_k], [grad_v]],
            [3 * width],
        )
    )
    sent = launch([qkv])
    part_0, part_2, part_31 = call(
        input_grad_body,
        "input_grad",
        streams(after(grad_q_near, qkv.send), grad_q_far, grad_k, grad_v, w_three),
        [Out(*block_bf)] * 2 + [((pair, model_dim), BF)],
    )
    (out_near, col_far), (part_31,) = land(started, part_31)
    out_joined = add(out_joined, out_near[:, :count])
    out_own = add(out_own, out_near[:, count:])
    small = jnp.concatenate([small_two, small_one])
    (out_far, small_far), _ = phase(
        [up[1], up[0], *down], [(out_joined, x_hop), (small, x_hop)], more=sent
    )
    small = small + small_far
    turned = jnp.concatenate([add(out_own, out_far), add(col_own, col_far)], axis=1)
    rows = model_dim // 2
    rest = Unit(turned[:rows], turned[rows:])
    (part_31, small_near), _ = phase(
        [rest, qkv, *down, up[1], up[0]], [(part_31, core_hop), (small, core_hop)]
    )
    bias_v = (bias_far_v + bias_near_q)[:2].reshape(1, 2 * width)
    small = Small(
        jnp.concatenate(
            [
                small + small_near,
                bias_near + bias_far,
                jnp.concatenate([bias_v, jnp.zeros((1, model_dim - 2 * width), F32)], axis=1),
            ]
        )
    )
    joined = add(part_2, part_31[:count])
    phase([*down, rest, up[0], qkv, up[1]])
    phase([up[0], up[1], rest, qkv, small])
    (arrived,), _ = phase([up[1], qkv, rest, small], [(joined, x_hop)])
    grad_input = (
        grad_one
        + part_0.astype(F32)
        + part_31[count:].astype(F32)
        + arrived.astype(F32)
    )
    d_tokens = grad_input.astype(BF).reshape(1, 1, count, model_dim)

    def place_wide(late, *parts):
        halves = [half for unit in parts for half in unit.halves]
        shape = (model_dim, model_dim)
        return call(
            functools.partial(place_wide_body, size=model_dim // 8),
            "place_wide",
            [rest_place, late(halves[0]), *halves[1:]],
            [KeptOut(shape, F32)],
            [(shape, F32)],
            semaphores=8,
        )

    _, (grad_down, d_tokens) = phase(
        [qkv, rest, small], fill=lambda late: [*place_wide(late, *down), d_tokens]
    )
    _, (grad_up, grad_qkv) = phase(
        [rest],
        fill=lambda late: [
            *place_wide(late, *up),
            *call(
                functools.partial(place_qkv_body, size=model_dim // 8),
                "place_qkv",
                [rest_place, late(qkv.halves[0]), qkv.halves[1]],
                [KeptOut((3, model_dim, width), F32)],
                [((3, model_dim, width), F32)],
                semaphores=24,
            ),
        ],
    )
    grad_out, grad_col = call(
        functools.partial(place_last_body, size=model_dim // 8),
        "place_last",
        [rest_place, *rest.halves],
        [Out((width, model_dim), F32)] * 2,
    )
    small = small.send
    loss = small[4, 0] * (1.0 / (segs * 2 * lax.axis_size("mp")))
    return (
        encoded.reshape(1, 1, count, model_dim),
        loss,
        pair_score.reshape(1, segs, segs),
        d_tokens,
        jnp.transpose(grad_qkv, (1, 0, 2)),
        small[17, : 2 * width].reshape(2, width),
        grad_out,
        small[8],
        small[9],
        small[10],
        grad_up,
        small[16],
        grad_down,
        small[1],
        small[2],
        small[3],
        grad_col,
        small[0],
    )


def solution(mesh):
    return jax.shard_map(
        per_device,
        mesh=mesh,
        in_specs=(
            P("tower", "dp", "mp", None),
            P(None, "dp", None),
            P(None, "dp", None),
            P(),
            P(None, None, "mp"),
            P(None, "mp"),
            P("mp", None),
            P(),
            P(),
            P(),
            P(None, "mp"),
            P("mp"),
            P("mp", None),
            P(),
            P(),
            P(),
            P("mp", None),
            P(),
        ),
        out_specs=(
            P("tower", "dp", "mp", None),
            P(),
            P("dp", None, None),
            P("tower", "dp", "mp", None),
            P(None, None, "mp"),
            P(None, "mp"),
            P("mp", None),
            P(),
            P(),
            P(),
            P(None, "mp"),
            P("mp"),
            P("mp", None),
            P(),
            P(),
            P(),
            P("mp", None),
            P(),
        ),
        check_vma=False,
    )
```

```python
import functools
import math

import jax
import jax.numpy as jnp
from jax import lax
from jax.experimental import pallas as pl
from jax.experimental.pallas import tpu as pltpu
from jax.sharding import PartitionSpec as P

HEAD_DIM = 64
EPS = 1e-05
NORM_EPS = 1e-06
SCALE_DENSE = 50.0
SCALE_COL = 50.0
SHARP = 20.0
HIGH = lax.Precision.HIGHEST
BF = jnp.bfloat16
F32 = jnp.float32
I32 = jnp.int32
LANES = 128
MIB = 1 << 20


def swap(block, axis, bit):
    count = lax.axis_size(axis)
    return lax.ppermute(block, axis, [(low, low ^ bit) for low in range(count)])


def after(value, *first):
    return lax.optimization_barrier((value,) + first)[0]


class Stream:
    def __init__(self, value):
        self.value = value


class Kept:
    def __init__(self, value):
        self.value = value


class Out:
    def __init__(self, shape, dtype):
        self.spec = (shape, dtype)


class KeptOut:
    def __init__(self, shape, dtype):
        self.spec = (shape, dtype)


class Arriving:
    def __init__(self, buffer, copy):
        self.buffer, self.copy, self.shape = buffer, copy, buffer.shape

    def wait(self):
        if self.copy is not None:
            self.copy.wait()
            self.copy = None

    def __getitem__(self, index):
        self.wait()
        return self.buffer[index]


class Leaving:
    def __init__(self, buffer, copy):
        self.buffer, self.copy, self.shape, self.dtype = buffer, copy, buffer.shape, buffer.dtype
        self.started = False

    def __setitem__(self, index, value):
        self.buffer[index] = value

    def __getitem__(self, index):
        return self.buffer[index]

    def flush(self):
        self.started = True
        self.copy.start()


MICROS = dict(
    project=1.0, norm_two_back=2.0, norm_two_keep=0.1, attend=3.7, norm_one=1.5, feed_forward=3.0, feed_far=1.3, feed_keep=2.5,
    place_col=1.0, heads=2.0, heads_keep=2.2, similar=1.8, dense=0.8, scores=3.0, feed_back=2.5, feed_back_far=1.3, feed_back_keep=0.1,
    weight_grad=0.1, turned_grad=0.1, norm_one_back=0.1, attend_back=0.1, input_grad=0.1,
    place_wide=0.1, place_qkv=0.1, place_last=0.1,
)


def call(body, name, ins, outs, scratch=(), semaphores=0, limit=8, alias=None):
    streams = [v.value for v in ins if isinstance(v, Stream)]
    leaving = [v.spec for v in outs if isinstance(v, Out)]
    values = [
        pltpu.with_memory_space_constraint(v.value, pltpu.HBM)
        if isinstance(v, (Stream, Kept))
        else v
        for v in ins
    ]

    def spec_of(v):
        if isinstance(v, (Stream, Kept, Out, KeptOut)):
            return pl.BlockSpec(memory_space=pltpu.HBM)
        if not isinstance(v, tuple) and v.ndim == 1 and v.dtype == I32:
            return pl.BlockSpec(memory_space=pltpu.SMEM)
        return pl.BlockSpec(memory_space=pltpu.VMEM)

    specs = [v.spec if isinstance(v, (Out, KeptOut)) else v for v in outs]
    sems = len(streams) + len(leaving) + semaphores

    def kernel(*refs):
        refs = list(refs)
        in_refs, refs = refs[: len(ins)], refs[len(ins) :]
        out_refs, refs = refs[: len(outs)], refs[len(outs) :]
        in_buffers, refs = refs[: len(streams)], refs[len(streams) :]
        out_buffers, refs = refs[: len(leaving)], refs[len(leaving) :]
        own, tail = refs[: len(scratch)], refs[len(scratch) :]
        place = 0
        args = []
        for v, ref in zip(ins, in_refs):
            if isinstance(v, Stream):
                copy = pltpu.make_async_copy(ref, in_buffers[place], tail[0].at[place])
                copy.start()
                ref = Arriving(in_buffers[place], copy)
                place += 1
            args.append(ref)
        results = []
        for v, ref in zip(outs, out_refs):
            if isinstance(v, Out):
                buffer = out_buffers[place - len(streams)]
                ref = Leaving(buffer, pltpu.make_async_copy(buffer, ref, tail[0].at[place]))
                place += 1
            results.append(ref)
        more = [tail[0].at[place + k] for k in range(semaphores)]
        body(*args, *results, *own, *more)
        for ref in args:
            if isinstance(ref, Arriving):
                ref.wait()
        sent = [ref for ref in results if isinstance(ref, Leaving)]
        for ref in sent:
            if not ref.started:
                ref.flush()
        for ref in sent:
            ref.copy.wait()

    shapes = [(v.shape, v.dtype) for v in streams] + leaving + list(scratch)
    scratch_shapes = [pltpu.VMEM(shape, dtype) for shape, dtype in shapes]
    if sems:
        scratch_shapes.append(pltpu.SemaphoreType.DMA((sems,)))
    return pl.pallas_call(
        kernel,
        in_specs=[spec_of(v) for v in ins],
        out_specs=[spec_of(v) for v in outs],
        out_shape=[
            (pltpu.HBM if isinstance(v, (Out, KeptOut)) else jax.ShapeDtypeStruct)(*spec)
            for v, spec in zip(outs, specs)
        ],
        scratch_shapes=scratch_shapes,
        compiler_params=pltpu.CompilerParams(vmem_limit_bytes=limit * MIB),
        cost_estimate=pl.CostEstimate(
            flops=int(MICROS[name] * 1e9), bytes_accessed=int(MICROS[name] * 1e6), transcendentals=0
        ),
        input_output_aliases=alias or {},
        name=name,
    )(*values)


def nn(left, right, precision=None):
    return lax.dot_general(
        left, right, (((1,), (0,)), ((), ())), precision=precision, preferred_element_type=F32
    )


def nt(left, right, precision=None):
    return lax.dot_general(
        left, right, (((1,), (1,)), ((), ())), precision=precision, preferred_element_type=F32
    )


def tn(left, right, precision=None):
    return lax.dot_general(
        left, right, (((0,), (0,)), ((), ())), precision=precision, preferred_element_type=F32
    )


def total(values):
    return jnp.sum(values, axis=0, keepdims=True)


def centre(values):
    return values - jnp.mean(values, axis=-1, keepdims=True)


def spread_of(centred):
    return lax.rsqrt(jnp.mean(centred * centred, axis=-1, keepdims=True) + EPS)


def norm_back(grad, normed, scale, gain):
    scaled = grad * gain
    mean_one = jnp.mean(scaled, axis=-1, keepdims=True)
    mean_two = jnp.mean(scaled * normed, axis=-1, keepdims=True)
    return scale * (scaled - mean_one - normed * mean_two)


def unit_rows(values):
    scale = lax.rsqrt(jnp.sum(values * values, axis=-1, keepdims=True) + NORM_EPS)
    return values * scale, scale


def unit_back(grad, unit, scale):
    return scale * (grad - unit * jnp.sum(grad * unit, axis=-1, keepdims=True))


def flagged(flag, shape):
    return (jnp.zeros(shape, I32) + flag) > 0


def project_body(first, second, weight, bias, query, key, value, *kept):
    count = first.shape[0]
    copies = []
    if kept:
        *kept, sem_one, sem_two = kept
        for source, out, sem in zip((first, second), kept, (sem_one, sem_two)):
            copy_out(copies, source, out, sem)
    for place, source in enumerate((first, second)):
        rows = slice(place * count, (place + 1) * count)
        block = source[...]
        query[rows, :] = (nn(block, weight[0]) + bias[0:1, :]).astype(BF)
        key[rows, :] = nn(block, weight[1]).astype(BF)
        value[rows, :] = (nn(block, weight[2]) + bias[1:2, :]).astype(BF)
    for copy in copies:
        copy.wait()


def head_masks(rows, heads):
    lanes = lax.broadcasted_iota(I32, rows.shape, 1) // HEAD_DIM
    return [jnp.where(lanes == head, rows, jnp.zeros_like(rows)) for head in range(heads)]


def allowed_pairs(seg_key, seg_query):
    return jnp.concatenate([seg_key] * (seg_query.shape[1] // LANES), axis=1) == seg_query


def attend_body(
    seg_key, seg_query, query, key_near, key_far, val_near, val_far,
    log_total, context_one, context_two, keys, values_t, context_t,
):
    half = key_near.shape[0]
    heads = query.shape[1] // HEAD_DIM
    keys[:half, :], keys[half:, :] = key_near[...], key_far[...]
    values_t[:, :half], values_t[:, half:] = val_near[...].T, val_far[...].T
    allowed = allowed_pairs(seg_key[...], seg_query[0:1, :])
    queries = head_masks(query[...] * BF(0.125), heads)

    def scores(head):
        return jnp.where(allowed, nt(keys[...], queries[head]), -1e30)

    current = scores(0)
    for head in range(heads):
        later = scores(head + 1) if head + 1 < heads else None
        rows = slice(head * HEAD_DIM, (head + 1) * HEAD_DIM)
        top = jnp.max(current, axis=0, keepdims=True)
        exp_terms = jnp.exp(current - top)
        norm = total(exp_terms)
        context_t[rows, :] = nn(values_t[rows, :], exp_terms.astype(BF)) * (1.0 / norm)
        log_total[head : head + 1, :] = top + jnp.log(norm)
        current = later
    log_total[heads:, :] = jnp.zeros((8 - heads, half), F32)
    log_total.flush()
    count = context_one.shape[0]
    context_one[...] = context_t[:, :count].T.astype(BF)
    context_two[...] = context_t[:, count:].T.astype(BF)


def attend_back_body(
    seg_key, seg_query, log_total, grad_one, grad_two, query, context_one, context_two,
    key_near, key_far, val_near, val_far, *refs, lanes, last,
):
    if last:
        key_before, value_before, gq, gk, gv, bias, keys, values, keys_t, grad_t = refs[:10]
        key_sum, value_sum, bias_before = refs[10], refs[11], None
    else:
        gq, key_sum, value_sum, bias, keys, values, keys_t, grad_t = refs
    half = key_near.shape[0]
    width = query.shape[1]
    heads = width // HEAD_DIM
    picked = (
        lax.broadcasted_iota(I32, (8, width), 1) // HEAD_DIM
        == lax.broadcasted_iota(I32, (8, width), 0)
    ).astype(F32)
    keys[:half, :], keys[half:, :] = key_near[...], key_far[...]
    values[:half, :], values[half:, :] = val_near[...], val_far[...]
    keys_t[...] = keys[...].T
    grad_context = jnp.concatenate(
        [grad[:, lane : lane + width] for grad, lane in zip((grad_one, grad_two), lanes)], axis=0
    )
    mixed = jnp.concatenate([context_one[...], context_two[...]], axis=0)
    allowed = allowed_pairs(seg_key[...], seg_query[0:1, :])
    dots = nt(picked, grad_context.astype(F32) * mixed.astype(F32), HIGH)
    queries = head_masks(query[...] * BF(0.125), heads)
    grad_heads = head_masks(grad_context, heads)

    def start(head):
        return nt(keys[...], queries[head]), nt(values[...], grad_heads[head])

    current = start(0)
    for head in range(heads):
        later = start(head + 1) if head + 1 < heads else None
        rows = slice(head * HEAD_DIM, (head + 1) * HEAD_DIM)
        raw, grad_probs = current
        probs = jnp.where(allowed, jnp.exp(raw - log_total[head : head + 1, :]), 0.0)
        grad_scores = (probs * (grad_probs - dots[head : head + 1, :])).astype(BF)
        add_v = nn(probs.astype(BF), grad_heads[head])
        add_k = nn(grad_scores, queries[head])
        if head:
            value_sum[...] += add_v
            key_sum[...] += add_k
        elif last:
            value_sum[...] = value_before[...] + add_v
            key_sum[...] = key_before[...] + add_k
        else:
            value_sum[...], key_sum[...] = add_v, add_k
        grad_t[rows, :] = nn(keys_t[rows, :], grad_scores)
        current = later
    grad_query = (grad_t[...].T * 0.125).astype(BF)
    gq[...] = grad_query
    bias[...] = jnp.zeros_like(bias)
    bias[0:1, :] = total(grad_query.astype(F32))
    if last:
        gk[...] = key_sum[...].astype(BF)
        grad_value = value_sum[...].astype(BF)
        gv[...] = grad_value
        bias[1:2, :] = total(grad_value.astype(F32))


def norm_one_body(
    tower, rows, mixed_0, mixed_1, mixed_2, mixed_3, w_0, w_1, w_2, w_3, w_2_more, w_3_more,
    b_out, gain, shift, hidden, centred,
):
    summed = rows[...].astype(F32) + b_out[...]
    summed = summed + nn(mixed_0[...], w_0[...]) + nn(mixed_1[...], w_1[...])
    here, there = lane_halves(tower, w_2)
    for mixed, weight, more in ((mixed_2, w_2, w_2_more), (mixed_3, w_3, w_3_more)):
        summed = summed + nn(mixed[:, here], weight[...]) + nn(mixed[:, there], more[...])
    middle = centre(summed)
    hidden[...] = (middle * spread_of(middle) * gain[...] + shift[...]).astype(BF)
    centred[...] = middle


def lane_halves(tower, part):
    size = part.shape[0]
    return (
        pl.ds(pl.multiple_of(tower[0] * size, size), size),
        pl.ds(pl.multiple_of((1 - tower[0]) * size, size), size),
    )


def gelu_pair(inner):
    cdf = 0.5 + 0.5 * lax.erf(inner * math.sqrt(0.5))
    density = jnp.exp(-0.5 * inner * inner) * (1.0 / math.sqrt(2.0 * math.pi))
    return (inner * cdf).astype(BF), (cdf + inner * density).astype(BF)


def ffn_body(
    first, second, w_up, b_up, w_down,
    active_one, active_two, slope_one, slope_two, part_one, part_two,
):
    inners = [nn(first[...], w_up[...]) + b_up[...]]
    inners.append(nn(second[...], w_up[...]) + b_up[...])
    places = ((active_one, slope_one, part_one), (active_two, slope_two, part_two))
    for inner, (active, slope, part) in zip(inners, places):
        act, active_slope = gelu_pair(inner)
        active[...] = act
        active.flush()
        slope[...] = active_slope
        slope.flush()
        part[...] = nn(act, w_down[...]).astype(BF)


def ffn_only_body(rows, w_up, b_up, w_down, part):
    inner = nn(rows[...], w_up[...]) + b_up[...]
    act = (inner * (0.5 + 0.5 * lax.erf(inner * math.sqrt(0.5)))).astype(BF)
    part[...] = nn(act, w_down[...]).astype(BF)


def ffn_keep_body(
    first, second, w_up, b_up,
    active_one, active_two, slope_one, slope_two, copy_one, copy_two,
):
    copy_one[...], copy_two[...] = first[...], second[...]
    copy_one.flush()
    copy_two.flush()
    for rows, active, slope in ((first, active_one, slope_one), (second, active_two, slope_two)):
        active[...], slope[...] = gelu_pair(nn(rows[...], w_up[...]) + b_up[...])
        active.flush()
        slope.flush()


def head_rows(centred, gain_one, shift_one, part, near, far, b_down, gain, shift):
    hidden = centred[...] * spread_of(centred[...]) * gain_one[...] + shift_one[...]
    summed = part[...].astype(F32) + near[...].astype(F32) + far[...].astype(F32)
    middle = centre(hidden + summed + b_down[...])
    return middle, middle * spread_of(middle) * gain[...] + shift[...]


def head_body(
    centred, gain_one, shift_one, part, near, far, b_down, gain, shift,
    col_weight, b_col, pick, cls_own, send, send_half,
):
    _, final = head_rows(centred, gain_one, shift_one, part, near, far, b_down, gain, shift)
    col, _ = unit_rows(nn(final.astype(BF), col_weight[...]) + b_col[...])
    cls, _ = unit_rows(nn(pick[...], final, HIGH))
    count = send_half.shape[0]
    col = col.astype(BF)
    cls_own[...] = jnp.concatenate([cls, jnp.zeros_like(cls)], axis=0).astype(BF)
    send[...] = col
    send_half[...] = col[count:]


def head_keep_body(
    centred, gain_one, shift_one, part, near, far, b_down, gain, shift,
    col_weight, b_col, pick, encoded, middle, col_pre, cls_raw,
):
    kept, final = head_rows(centred, gain_one, shift_one, part, near, far, b_down, gain, shift)
    middle[...] = kept
    middle.flush()
    encoded[...] = final.astype(BF)
    encoded.flush()
    col_pre[...] = nn(final.astype(BF), col_weight[...]) + b_col[...]
    col_pre.flush()
    cls_raw[...] = nn(pick[...], final, HIGH)


def similar_body(is_query, own, *refs):
    pieces, (weight_p, exp_terms, others, sums) = refs[:6], refs[6:]
    count = own.shape[0]
    row = 0
    for piece in pieces:
        rows = slice(row, row + piece.shape[0])
        others[rows, :] = piece[...]
        exp_terms[:, rows] = jnp.exp(SHARP * nt(own[...], piece[...]))
        row += piece.shape[0]
    weight = weight_p[...].astype(BF)
    terms = exp_terms[...]
    high = terms.astype(BF)
    low = (terms - high.astype(F32)).astype(BF)
    sums_q = nt(weight, high) + nt(weight, low)
    sums_p = nn(weight[:, :count], high) + nn(weight[:, :count], low)
    sums_q = jnp.concatenate([sums_q, jnp.zeros((sums_q.shape[0], 3 * count), F32)], axis=1)
    sums[...] = jnp.where(flagged(is_query[0], sums_p.shape), sums_q, sums_p)


def dense_body(is_query, vectors, targets, cls_raw, grad_cls, loss):
    block = vectors[...]
    shape = (block.shape[0], block.shape[0])
    segs = cls_raw.shape[0]
    kind_rows = block.shape[0] // 2
    query_kind = 1 - is_query[0]
    row_kind = lax.broadcasted_iota(I32, shape, 0) // kind_rows
    col_kind = lax.broadcasted_iota(I32, shape, 1) // kind_rows
    paired = jnp.logical_and(row_kind == query_kind, col_kind != query_kind)
    logits = jnp.where(paired, nt(block, block) * SCALE_DENSE, -1e30)
    onehot = targets[...]
    top = jnp.max(logits, axis=1, keepdims=True)
    exp_terms = jnp.where(paired, jnp.exp(logits - top), 0.0)
    norm = jnp.sum(exp_terms, axis=1, keepdims=True)
    norm = jnp.where(norm > 0.0, norm, 1.0)
    grad = ((exp_terms / norm - onehot) * (1.0 / segs)).astype(BF)
    grad = jnp.where(paired, grad, jnp.zeros_like(grad))
    hit = jnp.sum(jnp.where(paired, logits * onehot, 0.0), axis=1, keepdims=True)
    losses = top + jnp.log(norm) - hit
    rows = lax.broadcasted_iota(I32, losses.shape, 0) - query_kind * kind_rows
    mine = jnp.logical_and(rows >= 0, rows < segs)
    loss[...] = jnp.zeros_like(loss) + jnp.sum(jnp.where(mine, losses, 0.0))
    grad_rows = nn(grad[: 2 * segs], block)[:segs]
    grad_cols = tn(grad[:, : 2 * segs], block)[:segs]
    own = jnp.where(flagged(is_query[0], grad_rows.shape), grad_rows, grad_cols) * SCALE_DENSE
    grad_cls[...] = unit_back(own, *unit_rows(cls_raw[...]))


def score_body(
    is_query, sums, exp_terms, others, weight_q, weight_p, target, col_pre,
    grad_pre, scores,
):
    count = exp_terms.shape[0]
    segs = weight_q.shape[0]
    seg_sums = sums[...]
    w_q, w_p = weight_q[...], weight_p[...]
    size = jnp.sum(w_q, axis=1, keepdims=True)
    nearest = jnp.log(seg_sums) * (1.0 / SHARP)
    pair = nt(w_q, nearest, HIGH) / size
    scores[...] = pair
    logits = pair * SCALE_COL
    onehot = target[...]
    top = jnp.max(logits, axis=1, keepdims=True)
    terms = jnp.exp(logits - top)
    norm = jnp.sum(terms, axis=1, keepdims=True)
    grad_pair = (terms / norm - onehot) * (SCALE_COL / segs) / size
    grad_sums = tn(grad_pair, w_q, HIGH) / (SHARP * seg_sums)
    left = jnp.where(
        flagged(is_query[0], (segs, count)), grad_sums[:, :count], w_p[:, :count]
    )
    right = jnp.where(flagged(is_query[0], w_p.shape), w_p, grad_sums)
    grad_similar = (tn(left, right, HIGH) * (exp_terms[...] * SHARP)).astype(BF)
    grad_vec = nn(grad_similar, others[...])
    pre = unit_back(grad_vec, *unit_rows(col_pre[...])).astype(BF)
    grad_pre[...] = pre


def norm_two_back_rows(grad_pre, col_weight, grad_cls, pick, middle, gain):
    grad_final = nt(grad_pre[...], col_weight[...]) + tn(pick[...], grad_cls[...], HIGH)
    spread = spread_of(middle[...])
    unit = middle[...] * spread
    return norm_back(grad_final, unit, spread, gain[...]), grad_final, unit


def norm_two_back_body(grad_pre, col_weight, grad_cls, pick, middle, gain, grad_b):
    back, _, _ = norm_two_back_rows(grad_pre, col_weight, grad_cls, pick, middle, gain)
    grad_b[...] = back.astype(BF)


def norm_two_keep_body(
    grad_pre, col_weight, grad_cls, pick, middle, gain, scores, target, dense_loss,
    grad_two, grad_kept, small,
):
    back, grad_final, unit = norm_two_back_rows(
        grad_pre, col_weight, grad_cls, pick, middle, gain
    )
    grad_kept[...] = back.astype(BF)
    grad_kept.flush()
    grad_two[...] = back
    grad_two.flush()
    logits = scores[...] * SCALE_COL
    top = jnp.max(logits, axis=1, keepdims=True)
    norm = jnp.sum(jnp.exp(logits - top), axis=1, keepdims=True)
    losses = top + jnp.log(norm) - jnp.sum(logits * target[...], axis=1, keepdims=True)
    small[0:1, :] = total(grad_pre[...].astype(F32))
    small[1:2, :] = total(back)
    small[2:3, :] = total(grad_final * unit)
    small[3:4, :] = total(grad_final)
    small[4:5, :] = jnp.zeros((1, unit.shape[1]), F32) + (jnp.sum(losses) + dense_loss[0:1, 0:1])
    small[5:8, :] = jnp.zeros((3, unit.shape[1]), F32)


def ffn_back_body(
    first, second, slope_one, slope_two, w_down, w_up,
    inner_one, inner_two, part_one, part_two, bias,
):
    bias_sum = jnp.zeros((1, slope_one.shape[1]), F32)
    raws = [nt(second[...], w_down[...]), nt(first[...], w_down[...])]
    for raw, slope, inner in zip(raws, (slope_two, slope_one), (inner_two, inner_one)):
        grad = (raw * slope[...].astype(F32)).astype(BF)
        inner[...] = grad
        inner.flush()
        bias_sum = bias_sum + total(grad.astype(F32))
    part_two[...] = nt(inner_two[...], w_up[...]).astype(BF)
    part_one[...] = nt(inner_one[...], w_up[...]).astype(BF)
    bias[...] = bias_sum


def ffn_back_only_body(rows, slope, w_down, w_up, part):
    inner = (nt(rows[...], w_down[...]) * slope[...].astype(F32)).astype(BF)
    part[...] = nt(inner, w_up[...]).astype(BF)


def ffn_back_keep_body(first, second, slope_one, slope_two, w_down, inner_one, inner_two, bias):
    bias_sum = jnp.zeros((1, slope_one.shape[1]), F32)
    for rows, slope, inner in ((first, slope_one, inner_one), (second, slope_two, inner_two)):
        grad = (nt(rows[...], w_down[...]) * slope[...].astype(F32)).astype(BF)
        inner[...] = grad
        inner.flush()
        bias_sum = bias_sum + total(grad.astype(F32))
    bias[...] = bias_sum


def norm_one_back_body(
    tower, grad_two, part, near, far, centred, gain, w_0, w_1, w_2, w_3, w_2_more, w_3_more,
    grad_one, grad_b, small, mixed_0, mixed_2, mixed_13,
):
    grad = (
        grad_two[...]
        + part[...].astype(F32)
        + near[...].astype(F32)
        + far[...].astype(F32)
    )
    spread = spread_of(centred[...])
    unit = centred[...] * spread
    back = norm_back(grad, unit, spread, gain[...])
    grad_one[...] = back
    grad_one.flush()
    rounded = back.astype(BF)
    grad_b[...] = rounded
    grad_b.flush()
    width = mixed_0.shape[1]
    size = w_2.shape[0]
    for weight, more, mixed, lane in (
        (w_3, w_3_more, mixed_13, width), (w_2, w_2_more, mixed_2, 0)
    ):
        for part, side in ((weight, tower[0]), (more, 1 - tower[0])):
            lanes = pl.ds(pl.multiple_of(side * size + lane, size), size)
            mixed[:, lanes] = nt(rounded, part[...]).astype(BF)
    mixed_13[:, :width] = nt(rounded, w_1[...]).astype(BF)
    mixed_0[...] = nt(rounded, w_0[...]).astype(BF)
    small[0:1, :] = total(back)
    small[1:2, :] = total(grad * unit)
    small[2:3, :] = total(grad)
    small[3:8, :] = jnp.zeros((5, unit.shape[1]), F32)


def input_grad_body(
    query_near, query_far, grad_key, grad_value, weight, part_0, part_2, part_31
):
    count = part_0.shape[0]
    places = ((3, part_31, 0), (1, part_31, count), (2, part_2, 0), (0, part_0, 0))
    for block, out, row in places:
        own = slice(block % 2 * count, (block % 2 + 1) * count)
        rows = slice(block * count, (block + 1) * count)
        out[row : row + count, :] = (
            nt((query_near, query_far)[block // 2][own, :], weight[0])
            + nt(grad_key[rows, :], weight[1])
            + nt(grad_value[rows, :], weight[2])
        ).astype(BF)


def order_rows(place, source, out, size):
    for block in range(source.shape[1] // size):
        start = pl.multiple_of((jnp.int32(block) ^ place) * size, size)
        out[block * size : (block + 1) * size, :] = source[:, pl.ds(start, size)].T


def weight_grad_body(place, *refs, lefts, rights, cuts, first):
    left = refs[:lefts]
    right = refs[lefts : lefts + sum(rights)]
    outs, (ordered, joined) = refs[lefts + sum(rights) : -2], refs[-2:]
    token = 0
    for part in left:
        tokens = slice(token, token + part.shape[0])
        order_rows(place[0], part, ordered.at[:, tokens], LANES)
        token += part.shape[0]
    at = 0
    lane = 0
    for group in rights:
        token = 0
        for part in right[at : at + group]:
            rows = part.shape[0]
            lanes = min(part.shape[1], joined.shape[1])
            joined[token : token + rows, lane : lane + lanes] = part[:, first : first + lanes]
            token += rows
        at += group
        lane += lanes
    half = ordered.shape[0] // 2
    lane = 0
    for cut, (keep, send) in zip(cuts, zip(outs[::2], outs[1::2])):
        lanes = slice(lane, lane + cut)
        for rows, out in ((slice(half, 2 * half), send), (slice(0, half), keep)):
            out[...] = nn(ordered[rows, :], joined[:, lanes]).astype(BF)
            if isinstance(out, Leaving):
                out.flush()
        lane += cut


def turned_grad_body(place, mp_place, grad, *refs, rows):
    left, (part_0, part_2, part_31, ordered) = refs[:-4], refs[-4:]
    order_rows(place[0], grad, ordered, LANES)
    outs = ((0, part_0, 0), (2, part_2, 0), (3, part_31, 0), (1, part_31, rows))
    for block, out, lane in outs:
        if len(left) == 1:
            start = pl.multiple_of((jnp.int32(block) ^ mp_place[0]) * rows, rows)
            right = left[0][:, pl.ds(start, rows)]
        else:
            right = left[block][...]
        out[:, lane : lane + rows] = nn(ordered[...], right).astype(BF)
        if isinstance(out, Leaving):
            out.flush()


def place_col_body(mp_place, tower, w_0, w_1, w_2, w_3, w_2_more, w_3_more, out):
    count = w_0.shape[0]
    here, there = lane_halves(tower, w_2)
    for block, parts in enumerate(((w_0,), (w_1,), (w_2, w_2_more), (w_3, w_3_more))):
        start = pl.multiple_of((jnp.int32(block) ^ mp_place[0]) * count, count)
        if len(parts) == 1:
            out[pl.ds(start, count), :] = parts[0][...]
        else:
            size = parts[0].shape[0]
            out[pl.ds(pl.multiple_of(start + tower[0] * size, size), size), :] = parts[0][...]
            out[pl.ds(pl.multiple_of(start + (1 - tower[0]) * size, size), size), :] = parts[1][...]


def copy_out(copies, source, target, sem):
    copies.append(pltpu.make_async_copy(source, target, sem))
    copies[-1].start()


def place_wide_body(place, *refs, size):
    *parts, out, buffer = refs[: -8]
    sems = refs[-8:]
    copies = []
    cut = parts[0].shape[1]
    for block in range(8):
        here = pl.ds(block * size, size)
        start = pl.multiple_of((jnp.int32(block) ^ place[0]) * size, size)
        row = block % 4 * size
        for column in range(len(parts) // 2):
            part = parts[2 * column + block // 4]
            lanes = slice(column * cut, (column + 1) * cut)
            buffer[here, lanes] = part[row : row + size, :].astype(F32)
        copy_out(copies, buffer.at[here], out.at[pl.ds(start, size)], sems[block])
    for copy in copies:
        copy.wait()


def place_qkv_body(place, one, one_more, qkv, buffer, *sems, size):
    copies = []
    width = qkv.shape[2]
    for block in range(8):
        here = pl.ds(block * size, size)
        start = pl.multiple_of((jnp.int32(block) ^ place[0]) * size, size)
        rows = slice(block % 4 * size, (block % 4 + 1) * size)
        part = (one, one_more)[block // 4]
        for kind in range(3):
            lanes = slice(kind * width, (kind + 1) * width)
            buffer[kind, here, :] = part[rows, lanes].astype(F32)
            copy_out(
                copies,
                buffer.at[kind, here],
                qkv.at[kind, pl.ds(start, size)],
                sems[3 * block + kind],
            )
    for copy in copies:
        copy.wait()


def place_last_body(place, one, one_more, out, col, *, size):
    width = out.shape[0]
    for target, lane in ((out, 0), (col, width)):
        for block in range(8):
            start = pl.multiple_of((jnp.int32(block) ^ place[0]) * size, size)
            rows = slice(block % 4 * size, (block % 4 + 1) * size)
            part = (one, one_more)[block // 4]
            target[:, pl.ds(start, size)] = part[rows, lane : lane + width].astype(F32).T
        target.flush()


def dp_bits():
    return [1 << k for k in range(int(math.log2(lax.axis_size("dp"))))]


def add(*values):
    return sum(value.astype(F32) for value in values).astype(BF)


def side_of(axis, bit):
    return jnp.minimum(lax.axis_index(axis) & bit, 1)


def join(value, other, axis, bit):
    return jnp.where(
        side_of(axis, bit) == 0,
        jnp.concatenate([value, other]),
        jnp.concatenate([other, value]),
    )


def more_bits():
    return [("dp", bit) for bit in dp_bits()[2:]]


def sum_more(value):
    for axis, bit in more_bits():
        half = value.shape[0] // 2
        side = side_of(axis, bit)
        sent = lax.dynamic_slice_in_dim(value, (1 - side) * half, half, 0)
        kept = lax.dynamic_slice_in_dim(value, side * half, half, 0)
        value = add(kept, swap(sent, axis, bit))
    for axis, bit in more_bits()[::-1]:
        value = join(value, swap(value, axis, bit), axis, bit)
    return value


HOPS = (("tower", 1), ("dp", 1), ("dp", 2))


class Unit:
    def __init__(self, keep, send):
        self.value, self.send, self.stage = keep, send, 0

    def hop(self):
        return HOPS[min(self.stage, 5 - self.stage)]

    def land(self, got):
        self.stage += 1
        if self.stage <= 3:
            value = self.value.astype(F32) + got.astype(F32)
            if self.stage < 3:
                half = value.shape[0] // 2
                self.value, self.send = value[:half], value[half:].astype(BF)
            else:
                self.send = sum_more(value.astype(BF))
        elif self.stage < 6:
            self.send = jnp.concatenate([self.send, got])
        else:
            self.halves = (self.send, got)


class Small:
    def __init__(self, value):
        self.send, self.stage = value, 0

    def hop(self):
        return HOPS[self.stage]

    def land(self, got):
        self.stage += 1
        self.send = self.send + got
        if self.stage == 3:
            for axis, bit in more_bits():
                self.send = self.send + swap(self.send, axis, bit)


def together(*values):
    return lax.optimization_barrier(values)


def launch(units):
    groups = {}
    for unit in units:
        groups.setdefault((unit.hop(), unit.send.dtype), []).append(unit)
    started = []
    for (hop, _), group in groups.items():
        send = group[0].send
        if len(group) > 1:
            send = jnp.concatenate([unit.send for unit in group], axis=1)
        started.append((group, send, swap(send, *hop)))
    return started


def land(started, *others):
    flights = [flight for _, _, flight in started]
    sizes = [value.size * value.dtype.itemsize for value in flights]
    soon = [k for k, size in enumerate(sizes) if size < max(sizes)]
    late = [k for k in range(len(flights)) if k not in soon]
    done = together(*[flights[k] for k in soon], *others)
    done = together(*done, *[flights[k] for k in late])
    others = done[len(soon) : len(soon) + len(others)]
    landed = done[: len(soon)] + done[len(soon) + len(others) :]
    arrived = []
    for k, got in sorted(zip(soon + late, landed), key=lambda pair: pair[0]):
        group = started[k][0]
        if group is None:
            arrived.append(got)
            continue
        lane = 0
        for unit in group:
            width = unit.send.shape[1]
            unit.land(got if len(group) == 1 else got[:, lane : lane + width])
            lane += width
    return arrived, list(others)


def move(value, hop):
    return (None, value, swap(value, *hop))


def phase(units=(), moves=(), fill=None, then=None, more=()):
    if moves:
        for unit in units:
            unit.send = after(unit.send, moves[0][0])
    started = [move(value, hop) for value, hop in moves] + launch(units)
    ready = [send for _, send, _ in started]
    filled = list(fill(lambda value: after(value, *ready))) if fill else []
    extra = launch([then(filled)]) if then else []
    arrived, filled = land(started + list(more), *filled)
    return (arrived, filled, extra) if then else (arrived, filled)


def place_of(hops):
    place = 0
    for axis, bit in hops:
        place = place * 2 + side_of(axis, bit)
    return place[None].astype(I32)


def relative(values, mp_index):
    size = values.shape[-1] // 4
    blocks = [values[..., k * size : (k + 1) * size] for k in range(4)]
    values = jnp.where(mp_index & 1, jnp.concatenate([blocks[k ^ 1] for k in range(4)], -1), values)
    blocks = [values[..., k * size : (k + 1) * size] for k in range(4)]
    return jnp.where(mp_index & 2, jnp.concatenate([blocks[k ^ 2] for k in range(4)], -1), values)


def flip(values, bit):
    size = values.shape[-1] // 4
    return jnp.concatenate([values[:, (k ^ bit) * size :][:, :size] for k in range(4)], axis=1)


def per_device(
    tokens,
    segment_ids,
    key_mask,
    positives,
    w_qkv,
    b_qv,
    w_out,
    b_out,
    gain_one,
    shift_one,
    w_up,
    b_up,
    w_down,
    b_down,
    gain_two,
    shift_two,
    w_col,
    b_col,
):
    own_rows = tokens[0, 0]
    count, model_dim = own_rows.shape
    pair, width = 2 * count, w_out.shape[0]
    half = count // 2
    units = w_up.shape[1]
    segs = positives.shape[1]
    dp_size = lax.axis_size("dp")
    mp_index = lax.axis_index("mp")
    dp_index = lax.axis_index("dp")
    tower = lax.axis_index("tower")
    is_query = tower == 0
    query_flag = (1 - tower)[None].astype(I32)
    mp_place = mp_index[None].astype(I32)
    rest_place = place_of(HOPS)
    tower_place = tower[None].astype(I32)
    labels = jnp.arange(segs, dtype=I32)
    row = lambda vector: vector[None, :]
    block_bf = ((count, model_dim), BF)
    block_f32 = ((count, model_dim), F32)

    def core(block):
        return swap(block, "mp", 1)

    def across(block):
        return swap(block, "mp", 2)

    x_0, x_1, x_2 = own_rows, core(own_rows), across(own_rows)
    w_three = jnp.transpose(w_qkv, (1, 0, 2))

    seg_pair = segment_ids[:, 0]
    starts = jnp.concatenate([jnp.ones((2, 1), bool), seg_pair[:, 1:] != seg_pair[:, :-1]], axis=1)
    valid_pair = jnp.logical_or(key_mask[:, 0] > 0, starts)
    codes = relative(seg_pair + 16 * valid_pair.astype(I32) + 32 * starts.astype(I32), mp_index)
    seg_rel, valid_rel = codes & 15, (codes & 16) > 0
    code_row = jnp.where(is_query, codes[0], codes[1])
    seg_row = code_row & 15
    seg_key = jnp.broadcast_to(
        jnp.where((code_row & 16) > 0, seg_row, -1)[:, None], (4 * count, LANES)
    )
    seg_query = jnp.broadcast_to(seg_row[None, :], (8, 4 * count))
    members = seg_rel[:, None, :] == labels[None, :, None]
    weights = jnp.logical_and(members, valid_rel[:, None, :]).astype(F32)
    weight_q, weight_p = weights[0], weights[1]
    pick = (code_row[None, :count] - 32 == labels[:, None] + 16).astype(F32)
    order = dp_index ^ jnp.arange(dp_size, dtype=I32)
    kinds = jnp.arange(2, dtype=I32)[:, None, None]
    targets = (
        (1 - tower) * dp_size * segs
        + jnp.arange(dp_size, dtype=I32)[None, :, None] * segs
        + positives[order][None]
    )
    targets = jnp.where(kinds == tower, targets, -1).reshape(2 * dp_size * segs)
    paired = (targets[:, None] == jnp.arange(2 * dp_size * segs, dtype=I32)).astype(F32)
    positive_row = lax.dynamic_index_in_dim(positives, dp_index, 0, keepdims=False)
    positive_row = (positive_row[:, None] == labels).astype(F32)

    half_bf = ((pair, width), BF)
    mixed_bf = ((count, width), BF)
    x_hop, core_hop, y_hop = ("mp", 2), ("mp", 1), ("tower", 1)

    def project(first, second, kept=()):
        return call(
            project_body,
            "project",
            [first, second, w_three, b_qv],
            [half_bf] * 3 + list(kept),
            semaphores=len(kept),
        )

    near_qkv = project(x_0, x_1)
    halves = [
        lax.dynamic_slice_in_dim(weight, tower * half, half, 0) for weight in (w_out, w_col)
    ]
    x_2, out_half, col_half, out_1, col_1 = together(
        x_2, *halves, core(w_out), core(w_col), near_qkv,
        seg_key, seg_query, weight_q, weight_p, pick, paired, positive_row,
    )[:5]
    x_3 = core(x_2)
    out_2, col_2 = across(out_half), across(col_half)
    far_qkv = project(x_2, x_3, [KeptOut(*block_bf)] * 2)
    x_2_kept, x_3_kept = far_qkv[3:]
    key_values = [near_qkv[1], far_qkv[1], near_qkv[2], far_qkv[2]]
    seg_query_near, seg_query_far = seg_query[:, :pair], seg_query[:, pair:]

    def attend(seg_half, query):
        return call(
            attend_body,
            "attend",
            [seg_key, seg_half, query, *key_values],
            [Out((8, pair), F32), mixed_bf, mixed_bf],
            [((4 * count, width), BF), ((width, 4 * count), BF), ((width, pair), F32)],
        )

    total_far, mixed_far_2, mixed_far_3 = attend(seg_query_far, far_qkv[0])
    mixed_far_2, mixed_far_3, out_2 = together(mixed_far_2, mixed_far_3, out_2)
    (out_2_more, mixed_2, mixed_1_2), (total_near, mixed_0, mixed_near_1, col_2) = phase(
        (),
        [(out_2, y_hop), (mixed_far_2, x_hop), (mixed_far_3, x_hop)],
        lambda late: [*attend(seg_query_near, late(near_qkv[0])), col_2],
    )
    (mixed_1, mixed_3, out_3, out_3_more), _ = phase(
        (),
        [(mixed_near_1, core_hop), (mixed_1_2, core_hop), (out_2, core_hop)]
        + [(out_2_more, core_hop)],
    )
    col_3 = core(col_2)
    mixed = [mixed_0, mixed_1, mixed_2, mixed_3]
    outs = [w_out, out_1, out_2, out_3, out_2_more, out_3_more]
    hidden, centred_one = call(
        norm_one_body,
        "norm_one",
        [tower_place, own_rows, *mixed, *outs, row(b_out), row(gain_one), row(shift_one)],
        [block_bf, block_f32],
    )

    h_0, h_1 = hidden, core(hidden)
    kept_bf = Out((count, units), BF)
    (h_2, col_2_more), (act_0, act_1, slope_0, slope_1, part_0, part_1) = phase(
        (),
        [(hidden, x_hop), (col_2, y_hop)],
        lambda late: call(
            ffn_body,
            "feed_forward",
            [h_0, h_1, w_up, row(b_up), w_down],
            [kept_bf] * 4 + [Out(*block_bf), block_bf],
        ),
    )
    h_3, col_3_more = core(h_2), core(col_2_more)

    def feed_far(rows):
        return call(
            ffn_only_body, "feed_far", [rows, w_up, row(b_up), w_down], [block_bf]
        )[0]

    part_2 = feed_far(h_2)
    part_3 = feed_far(after(h_3, part_2))
    near_sum = core(part_1)
    joined = add(part_2, core(part_3))
    joined, near_sum = together(joined, near_sum)
    (arrived,), (act_2, act_3, slope_2, slope_3, h_2_kept, h_3_kept, col_weight) = phase(
        (),
        [(joined, x_hop)],
        lambda late: [
            *call(
                ffn_keep_body,
                "feed_keep",
                [late(h_2), h_3, w_up, row(b_up)],
                [kept_bf] * 4 + [Out(*block_bf)] * 2,
            ),
            *call(
                place_col_body,
                "place_col",
                [mp_place, tower_place, w_col, late(col_1), col_2, col_3, col_2_more, col_3_more],
                [((model_dim, model_dim), BF)],
            ),
        ],
    )
    ins = [centred_one, row(gain_one), row(shift_one), part_0, near_sum, arrived]
    ins += [row(b_down), row(gain_two), row(shift_two), col_weight, row(b_col), pick]
    cls_own, send, send_half = call(
        head_body,
        "heads",
        ins,
        [((2 * segs, model_dim), BF), block_bf, ((half, model_dim), BF)],
    )

    cls_all = cls_own[:segs]
    started = [move(send, y_hop), move(send_half, x_hop)]
    cls_hop = move(cls_all, ("dp", 1))
    kept = call(
        head_keep_body,
        "heads_keep",
        [after(centred_one, send, send_half, cls_all)] + ins[1:],
        [Out(*block_bf), Out(*block_f32), Out(*block_f32), Out((segs, model_dim), F32)],
    )
    (cls_far,), kept = land([cls_hop], *kept)
    cls_all = jnp.concatenate([cls_all, cls_far])
    for bit in dp_bits()[1:]:
        (cls_far,), _ = land([move(cls_all, ("dp", bit))])
        cls_all = jnp.concatenate([cls_all, cls_far])
    (other, own_half), (cls_all, encoded, middle, col_pre, cls_raw) = land(
        started, cls_all, *kept
    )
    (far_b, far_a, cls_far), _ = phase(
        (), [(own_half, y_hop), (other[:half], x_hop), (cls_all, x_hop)]
    )
    cls_all = add(cls_all, cls_far)
    (near, diag_a, diag_b, cls_near), _ = phase(
        (),
        [(other, core_hop), (far_a, core_hop), (far_b, core_hop), (cls_all, core_hop)],
    )
    cls_all = add(cls_all, cls_near)
    pieces = [other, near, far_a, far_b, diag_a, diag_b]
    exp_terms, others, sums = call(
        similar_body,
        "similar",
        [query_flag, send, *pieces, weight_p],
        [((count, 4 * count), F32), ((4 * count, model_dim), BF), ((segs, 4 * count), F32)],
    )
    cls_all = after(cls_all, sums)
    (swapped, cls_other), _ = phase((), [(sums, x_hop), (cls_all, y_hop)])
    sums = sums + flip(swapped, 2)
    cls_all = jnp.concatenate([cls_all, cls_other])
    (swapped,), (grad_cls, dense_loss) = phase(
        (),
        [(sums, core_hop)],
        lambda late: call(
            dense_body,
            "dense",
            [query_flag, late(cls_all), paired, cls_raw],
            [((segs, model_dim), F32), ((8, LANES), F32)],
        ),
    )
    sums = sums + flip(swapped, 1)
    grad_pre, pair_score = call(
        score_body,
        "scores",
        [query_flag, sums, exp_terms, others, weight_q, weight_p, positive_row, col_pre],
        [block_bf, ((segs, segs), F32)],
    )
    ins = [grad_pre, col_weight, grad_cls, pick, middle, row(gain_two)]
    (grad_two_b,) = call(norm_two_back_body, "norm_two_back", ins, [block_bf])

    def streams(*values):
        return [Stream(value) for value in values]

    def feed_back(first, second, slope_one, slope_two, part):
        return call(
            ffn_back_body,
            "feed_back",
            [first, second, *streams(slope_one, slope_two), w_down, w_up],
            [kept_bf] * 2 + [part, block_bf, Out((1, units), F32)],
            limit=12,
        )

    def weight_grad(left, right, cuts, first=0):
        rows = getattr(left[0], "value", left[0]).shape[1]
        tokens = 4 * count
        outs = [Out((rows // 2, cut), BF) for cut in cuts for _ in range(2)]
        outs[1] = ((rows // 2, cuts[0]), BF)
        return call(
            functools.partial(
                weight_grad_body,
                lefts=len(left),
                rights=[len(parts) for parts in right],
                cuts=cuts,
                first=first,
            ),
            "weight_grad",
            [rest_place, *left, *[part for parts in right for part in parts]],
            outs,
            [((rows, tokens), BF), ((tokens, sum(cuts)), BF)],
            limit=20,
        )

    def turned_grad(grad, left):
        return call(
            functools.partial(turned_grad_body, rows=count),
            "turned_grad",
            [rest_place, mp_place, grad, *left],
            [Out((model_dim, count), BF)] * 2 + [((model_dim, 2 * count), BF)],
            [((model_dim, count), BF)],
        )

    def near_back(late):
        backs = feed_back(grad_two_b, g_1, slope_0, slope_1, Out(*block_bf))
        kept = call(
            norm_two_keep_body,
            "norm_two_keep",
            [after(grad_pre, backs[3])] + ins[1:] + [pair_score, positive_row, dense_loss],
            [Out(*block_f32), Out(*block_bf), Out((8, model_dim), F32)],
        )
        turned = turned_grad(Stream(after(grad_pre, kept[2])), [Stream(encoded)])
        return [*backs, *kept, *turned]

    g_1 = core(grad_two_b)
    (g_2,), (inner_0, inner_1, part_0, part_1, bias_near, *kept) = phase(
        (), [(grad_two_b, x_hop)], near_back
    )
    grad_two, grad_two_kept, small_two, col_own, col_joined, col_near = kept
    g_3 = core(g_2)

    def feed_back_far(rows, slope):
        return call(
            ffn_back_only_body, "feed_back_far", [rows, slope, w_down, w_up], [block_bf]
        )[0]

    part_2 = feed_back_far(g_2, slope_2)
    part_3 = feed_back_far(after(g_3, part_2), slope_3)
    cut = model_dim // 2

    def down_grad(late, start):
        return weight_grad(
            streams(act_0, act_1, act_2, act_3),
            [[Stream(grad_two_kept), Stream(g_1), late(g_2), g_3]],
            [cut],
            start,
        )

    (near_sum, arrived), down = phase(
        (), [(part_1, core_hop), (part_3, core_hop)], lambda late: down_grad(late, 0)
    )
    down = [Unit(*down)]
    joined = add(part_2, arrived)

    def unit_grads(late):
        more = down_grad(late, cut)
        inner_2, inner_3, bias_far = call(
            ffn_back_keep_body,
            "feed_back_keep",
            [after(g_2, more[1]), g_3, slope_2, slope_3, w_down],
            [kept_bf] * 2 + [Out((1, units), F32)],
        )
        up = weight_grad(
            [after(h_0, bias_far), h_1, *streams(h_2_kept, h_3_kept)],
            [streams(inner_0, inner_1, inner_2, inner_3)],
            [cut, cut],
        )
        return [*more, *up, bias_far]

    (arrived,), (_, _, *up, bias_far), more = phase(
        down, [(joined, x_hop)], unit_grads, then=lambda filled: Unit(*filled[:2])
    )
    down.append(more[0][0][0])
    up = [Unit(*up[:2]), Unit(*up[2:])]
    grad_one, grad_one_b, small_one, back_0, back_2, back_13 = call(
        norm_one_back_body,
        "norm_one_back",
        [tower_place, grad_two, part_0, near_sum, arrived, centred_one, row(gain_one), *outs],
        [Out(*block_f32), Out(*block_bf), ((8, model_dim), F32)]
        + [mixed_bf, mixed_bf, ((count, 2 * width), BF)],
        limit=12,
    )

    (back_13,), _ = phase((), [(back_13, core_hop)])
    back_23 = jnp.concatenate([back_2, back_13[:, width:]], axis=1)
    all_bf, all_f32 = ((4 * count, width), BF), ((4 * count, width), F32)
    back_scratch = [all_bf] * 2 + [((width, 4 * count), BF), ((width, pair), F32)]

    def back_ins(seg_half, log_total, grads, query, mixed_pair):
        return [seg_key, seg_half, log_total, *grads, query, *mixed_pair, *key_values]

    back_hop = move(back_23, x_hop)
    grad_q_near, key_sum, value_sum, bias_near_q = call(
        functools.partial(attend_back_body, lanes=(0, 0), last=False),
        "attend_back",
        back_ins(
            seg_query_near,
            total_near,
            [after(back_0, back_23), back_13],
            near_qkv[0],
            (mixed_0, mixed_near_1),
        ),
        [half_bf, all_f32, all_f32, ((8, width), F32)],
        back_scratch,
        limit=16,
    )
    _, (grad_q_near,) = land(more, grad_q_near)
    up[0].send = after(up[0].send, down[1].send)
    started = launch([*down, up[0]])
    out_own, out_joined, out_near = turned_grad(
        Stream(after(grad_one_b, *[send for _, send, _ in started])), streams(*mixed)
    )
    (back_23, col_near), (out_near,) = land([back_hop, move(col_near, core_hop)], out_near)
    grad_q_far, grad_k, grad_v, bias_far_v = call(
        functools.partial(attend_back_body, lanes=(0, width), last=True),
        "attend_back",
        back_ins(
            seg_query_far,
            total_far,
            [after(back_23, out_near), back_23],
            far_qkv[0],
            (mixed_far_2, mixed_far_3),
        )
        + [key_sum, value_sum],
        [half_bf, all_bf, all_bf, ((8, width), F32)],
        back_scratch + [all_f32, all_f32],
        limit=16,
    )
    _, (grad_v,) = land(started, grad_v)
    col_joined = add(col_joined, col_near[:, :count])
    col_own = add(col_own, col_near[:, count:])
    up[1].send = after(up[1].send, down[0].send)
    started = [move(out_near, core_hop), move(col_joined, x_hop)]
    started += launch([up[1], up[0], *down])
    qkv = Unit(
        *weight_grad(
            [after(x_0, grad_v, *[send for _, send, _ in started]), x_1, x_2_kept, x_3_kept],
            [[grad_q_near, grad_q_far], [grad_k], [grad_v]],
            [3 * width],
        )
    )
    sent = launch([qkv])
    part_0, part_2, part_31 = call(
        input_grad_body,
        "input_grad",
        streams(after(grad_q_near, qkv.send), grad_q_far, grad_k, grad_v, w_three),
        [Out(*block_bf)] * 2 + [((pair, model_dim), BF)],
    )
    (out_near, col_far), (part_31,) = land(started, part_31)
    out_joined = add(out_joined, out_near[:, :count])
    out_own = add(out_own, out_near[:, count:])
    small = jnp.concatenate([small_two, small_one])
    (out_far, small_far), _ = phase(
        [up[1], up[0], *down], [(out_joined, x_hop), (small, x_hop)], more=sent
    )
    small = small + small_far
    turned = jnp.concatenate([add(out_own, out_far), add(col_own, col_far)], axis=1)
    rows = model_dim // 2
    rest = Unit(turned[:rows], turned[rows:])
    (part_31, small_near), _ = phase(
        [rest, qkv, *down, up[1], up[0]], [(part_31, core_hop), (small, core_hop)]
    )
    bias_v = (bias_far_v + bias_near_q)[:2].reshape(1, 2 * width)
    small = Small(
        jnp.concatenate(
            [
                small + small_near,
                bias_near + bias_far,
                jnp.concatenate([bias_v, jnp.zeros((1, model_dim - 2 * width), F32)], axis=1),
            ]
        )
    )
    joined = add(part_2, part_31[:count])
    phase([*down, rest, up[0], qkv, up[1]])
    phase([up[0], up[1], rest, qkv, small])
    (arrived,), _ = phase([up[1], qkv, rest, small], [(joined, x_hop)])
    grad_input = (
        grad_one
        + part_0.astype(F32)
        + part_31[count:].astype(F32)
        + arrived.astype(F32)
    )
    d_tokens = grad_input.astype(BF).reshape(1, 1, count, model_dim)

    def place_wide(late, *parts):
        halves = [half for unit in parts for half in unit.halves]
        shape = (model_dim, model_dim)
        return call(
            functools.partial(place_wide_body, size=model_dim // 8),
            "place_wide",
            [rest_place, late(halves[0]), *halves[1:]],
            [KeptOut(shape, F32)],
            [(shape, F32)],
            semaphores=8,
        )

    _, (grad_down, d_tokens) = phase(
        [qkv, rest, small], fill=lambda late: [*place_wide(late, *down), d_tokens]
    )
    _, (grad_up, grad_qkv) = phase(
        [rest],
        fill=lambda late: [
            *place_wide(late, *up),
            *call(
                functools.partial(place_qkv_body, size=model_dim // 8),
                "place_qkv",
                [rest_place, late(qkv.halves[0]), qkv.halves[1]],
                [KeptOut((3, model_dim, width), F32)],
                [((3, model_dim, width), F32)],
                semaphores=24,
            ),
        ],
    )
    grad_out, grad_col = call(
        functools.partial(place_last_body, size=model_dim // 8),
        "place_last",
        [rest_place, *rest.halves],
        [Out((width, model_dim), F32)] * 2,
    )
    small = small.send
    loss = small[4, 0] * (1.0 / (segs * 2 * lax.axis_size("mp")))
    return (
        encoded.reshape(1, 1, count, model_dim),
        loss,
        pair_score.reshape(1, segs, segs),
        d_tokens,
        jnp.transpose(grad_qkv, (1, 0, 2)),
        small[17, : 2 * width].reshape(2, width),
        grad_out,
        small[8],
        small[9],
        small[10],
        grad_up,
        small[16],
        grad_down,
        small[1],
        small[2],
        small[3],
        grad_col,
        small[0],
    )


def solution(mesh):
    return jax.shard_map(
        per_device,
        mesh=mesh,
        in_specs=(
            P("tower", "dp", "mp", None),
            P(None, "dp", None),
            P(None, "dp", None),
            P(),
            P(None, None, "mp"),
            P(None, "mp"),
            P("mp", None),
            P(),
            P(),
            P(),
            P(None, "mp"),
            P("mp"),
            P("mp", None),
            P(),
            P(),
            P(),
            P("mp", None),
            P(),
        ),
        out_specs=(
            P("tower", "dp", "mp", None),
            P(),
            P("dp", None, None),
            P("tower", "dp", "mp", None),
            P(None, None, "mp"),
            P(None, "mp"),
            P("mp", None),
            P(),
            P(),
            P(),
            P(None, "mp"),
            P("mp"),
            P("mp", None),
            P(),
            P(),
            P(),
            P("mp", None),
            P(),
        ),
        check_vma=False,
    )
```

```python
import functools
import math

import jax
import jax.numpy as jnp
from jax import lax
from jax.experimental import pallas as pl
from jax.experimental.pallas import tpu as pltpu
from jax.sharding import PartitionSpec as P

HEAD_DIM = 64
EPS = 1e-05
NORM_EPS = 1e-06
SCALE_DENSE = 50.0
SCALE_COL = 50.0
SHARP = 20.0
HIGH = lax.Precision.HIGHEST
BF = jnp.bfloat16
F32 = jnp.float32
I32 = jnp.int32
LANES = 128
MIB = 1 << 20


def swap(block, axis, bit):
    count = lax.axis_size(axis)
    return lax.ppermute(block, axis, [(low, low ^ bit) for low in range(count)])


def after(value, *first):
    return lax.optimization_barrier((value,) + first)[0]


class Stream:
    def __init__(self, value):
        self.value = value


class Kept:
    def __init__(self, value):
        self.value = value


class Out:
    def __init__(self, shape, dtype):
        self.spec = (shape, dtype)


class KeptOut:
    def __init__(self, shape, dtype):
        self.spec = (shape, dtype)


class Arriving:
    def __init__(self, buffer, copy):
        self.buffer, self.copy, self.shape = buffer, copy, buffer.shape

    def wait(self):
        if self.copy is not None:
            self.copy.wait()
            self.copy = None

    def __getitem__(self, index):
        self.wait()
        return self.buffer[index]


class Leaving:
    def __init__(self, buffer, copy):
        self.buffer, self.copy, self.shape, self.dtype = buffer, copy, buffer.shape, buffer.dtype
        self.started = False

    def __setitem__(self, index, value):
        self.buffer[index] = value

    def __getitem__(self, index):
        return self.buffer[index]

    def flush(self):
        self.started = True
        self.copy.start()


MICROS = dict(
    project=1.0, norm_two_back=2.0, norm_two_keep=0.1, attend=3.7, norm_one=1.5, feed_forward=3.0, feed_far=1.3, feed_keep=2.5,
    place_col=1.0, heads=2.0, heads_keep=2.2, similar=1.8, dense=0.8, scores=3.0, feed_back=2.5, feed_back_far=1.3, feed_back_keep=0.1,
    weight_grad=0.1, turned_grad=0.1, norm_one_back=0.1, attend_back=0.1, input_grad=0.1,
    place_wide=0.1, place_qkv=0.1, place_last=0.1,
)


def call(body, name, ins, outs, scratch=(), semaphores=0, limit=8, alias=None):
    streams = [v.value for v in ins if isinstance(v, Stream)]
    leaving = [v.spec for v in outs if isinstance(v, Out)]
    values = [
        pltpu.with_memory_space_constraint(v.value, pltpu.HBM)
        if isinstance(v, (Stream, Kept))
        else v
        for v in ins
    ]

    def spec_of(v):
        if isinstance(v, (Stream, Kept, Out, KeptOut)):
            return pl.BlockSpec(memory_space=pltpu.HBM)
        if not isinstance(v, tuple) and v.ndim == 1 and v.dtype == I32:
            return pl.BlockSpec(memory_space=pltpu.SMEM)
        return pl.BlockSpec(memory_space=pltpu.VMEM)

    specs = [v.spec if isinstance(v, (Out, KeptOut)) else v for v in outs]
    sems = len(streams) + len(leaving) + semaphores

    def kernel(*refs):
        refs = list(refs)
        in_refs, refs = refs[: len(ins)], refs[len(ins) :]
        out_refs, refs = refs[: len(outs)], refs[len(outs) :]
        in_buffers, refs = refs[: len(streams)], refs[len(streams) :]
        out_buffers, refs = refs[: len(leaving)], refs[len(leaving) :]
        own, tail = refs[: len(scratch)], refs[len(scratch) :]
        place = 0
        args = []
        for v, ref in zip(ins, in_refs):
            if isinstance(v, Stream):
                copy = pltpu.make_async_copy(ref, in_buffers[place], tail[0].at[place])
                copy.start()
                ref = Arriving(in_buffers[place], copy)
                place += 1
            args.append(ref)
        results = []
        for v, ref in zip(outs, out_refs):
            if isinstance(v, Out):
                buffer = out_buffers[place - len(streams)]
                ref = Leaving(buffer, pltpu.make_async_copy(buffer, ref, tail[0].at[place]))
                place += 1
            results.append(ref)
        more = [tail[0].at[place + k] for k in range(semaphores)]
        body(*args, *results, *own, *more)
        for ref in args:
            if isinstance(ref, Arriving):
                ref.wait()
        sent = [ref for ref in results if isinstance(ref, Leaving)]
        for ref in sent:
            if not ref.started:
                ref.flush()
        for ref in sent:
            ref.copy.wait()

    shapes = [(v.shape, v.dtype) for v in streams] + leaving + list(scratch)
    scratch_shapes = [pltpu.VMEM(shape, dtype) for shape, dtype in shapes]
    if sems:
        scratch_shapes.append(pltpu.SemaphoreType.DMA((sems,)))
    return pl.pallas_call(
        kernel,
        in_specs=[spec_of(v) for v in ins],
        out_specs=[spec_of(v) for v in outs],
        out_shape=[
            (pltpu.HBM if isinstance(v, (Out, KeptOut)) else jax.ShapeDtypeStruct)(*spec)
            for v, spec in zip(outs, specs)
        ],
        scratch_shapes=scratch_shapes,
        compiler_params=pltpu.CompilerParams(vmem_limit_bytes=limit * MIB),
        cost_estimate=pl.CostEstimate(
            flops=int(MICROS[name] * 1e9), bytes_accessed=int(MICROS[name] * 1e6), transcendentals=0
        ),
        input_output_aliases=alias or {},
        name=name,
    )(*values)


def nn(left, right, precision=None):
    return lax.dot_general(
        left, right, (((1,), (0,)), ((), ())), precision=precision, preferred_element_type=F32
    )


def nt(left, right, precision=None):
    return lax.dot_general(
        left, right, (((1,), (1,)), ((), ())), precision=precision, preferred_element_type=F32
    )


def tn(left, right, precision=None):
    return lax.dot_general(
        left, right, (((0,), (0,)), ((), ())), precision=precision, preferred_element_type=F32
    )


def total(values):
    return jnp.sum(values, axis=0, keepdims=True)


def centre(values):
    return values - jnp.mean(values, axis=-1, keepdims=True)


def spread_of(centred):
    return lax.rsqrt(jnp.mean(centred * centred, axis=-1, keepdims=True) + EPS)


def norm_back(grad, normed, scale, gain):
    scaled = grad * gain
    mean_one = jnp.mean(scaled, axis=-1, keepdims=True)
    mean_two = jnp.mean(scaled * normed, axis=-1, keepdims=True)
    return scale * (scaled - mean_one - normed * mean_two)


def unit_rows(values):
    scale = lax.rsqrt(jnp.sum(values * values, axis=-1, keepdims=True) + NORM_EPS)
    return values * scale, scale


def unit_back(grad, unit, scale):
    return scale * (grad - unit * jnp.sum(grad * unit, axis=-1, keepdims=True))


def flagged(flag, shape):
    return (jnp.zeros(shape, I32) + flag) > 0


def project_body(first, second, weight, bias, query, key, value, *kept):
    count = first.shape[0]
    copies = []
    if kept:
        *kept, sem_one, sem_two = kept
        for source, out, sem in zip((first, second), kept, (sem_one, sem_two)):
            copy_out(copies, source, out, sem)
    for place, source in enumerate((first, second)):
        rows = slice(place * count, (place + 1) * count)
        block = source[...]
        query[rows, :] = (nn(block, weight[0]) + bias[0:1, :]).astype(BF)
        key[rows, :] = nn(block, weight[1]).astype(BF)
        value[rows, :] = (nn(block, weight[2]) + bias[1:2, :]).astype(BF)
    for copy in copies:
        copy.wait()


def head_masks(rows, heads):
    lanes = lax.broadcasted_iota(I32, rows.shape, 1) // HEAD_DIM
    return [jnp.where(lanes == head, rows, jnp.zeros_like(rows)) for head in range(heads)]


def allowed_pairs(seg_key, seg_query):
    return jnp.concatenate([seg_key] * (seg_query.shape[1] // LANES), axis=1) == seg_query


def attend_body(
    seg_key, seg_query, query, key_near, key_far, val_near, val_far,
    log_total, context_one, context_two, keys, values_t, context_t,
):
    half = key_near.shape[0]
    heads = query.shape[1] // HEAD_DIM
    keys[:half, :], keys[half:, :] = key_near[...], key_far[...]
    values_t[:, :half], values_t[:, half:] = val_near[...].T, val_far[...].T
    allowed = allowed_pairs(seg_key[...], seg_query[0:1, :])
    queries = head_masks(query[...] * BF(0.125), heads)

    def scores(head):
        return jnp.where(allowed, nt(keys[...], queries[head]), -1e30)

    current = scores(0)
    for head in range(heads):
        later = scores(head + 1) if head + 1 < heads else None
        rows = slice(head * HEAD_DIM, (head + 1) * HEAD_DIM)
        top = jnp.max(current, axis=0, keepdims=True)
        exp_terms = jnp.exp(current - top)
        norm = total(exp_terms)
        context_t[rows, :] = nn(values_t[rows, :], exp_terms.astype(BF)) * (1.0 / norm)
        log_total[head : head + 1, :] = top + jnp.log(norm)
        current = later
    log_total[heads:, :] = jnp.zeros((8 - heads, half), F32)
    log_total.flush()
    count = context_one.shape[0]
    context_one[...] = context_t[:, :count].T.astype(BF)
    context_two[...] = context_t[:, count:].T.astype(BF)


def attend_back_body(
    seg_key, seg_query, log_total, grad_one, grad_two, query, context_one, context_two,
    key_near, key_far, val_near, val_far, *refs, lanes, last,
):
    if last:
        key_before, value_before, gq, gk, gv, bias, keys, values, keys_t, grad_t = refs[:10]
        key_sum, value_sum, bias_before = refs[10], refs[11], None
    else:
        gq, key_sum, value_sum, bias, keys, values, keys_t, grad_t = refs
    half = key_near.shape[0]
    width = query.shape[1]
    heads = width // HEAD_DIM
    picked = (
        lax.broadcasted_iota(I32, (8, width), 1) // HEAD_DIM
        == lax.broadcasted_iota(I32, (8, width), 0)
    ).astype(F32)
    keys[:half, :], keys[half:, :] = key_near[...], key_far[...]
    values[:half, :], values[half:, :] = val_near[...], val_far[...]
    keys_t[...] = keys[...].T
    grad_context = jnp.concatenate(
        [grad[:, lane : lane + width] for grad, lane in zip((grad_one, grad_two), lanes)], axis=0
    )
    mixed = jnp.concatenate([context_one[...], context_two[...]], axis=0)
    allowed = allowed_pairs(seg_key[...], seg_query[0:1, :])
    dots = nt(picked, grad_context.astype(F32) * mixed.astype(F32), HIGH)
    queries = head_masks(query[...] * BF(0.125), heads)
    grad_heads = head_masks(grad_context, heads)

    def start(head):
        return nt(keys[...], queries[head]), nt(values[...], grad_heads[head])

    current = start(0)
    for head in range(heads):
        later = start(head + 1) if head + 1 < heads else None
        rows = slice(head * HEAD_DIM, (head + 1) * HEAD_DIM)
        raw, grad_probs = current
        probs = jnp.where(allowed, jnp.exp(raw - log_total[head : head + 1, :]), 0.0)
        grad_scores = (probs * (grad_probs - dots[head : head + 1, :])).astype(BF)
        add_v = nn(probs.astype(BF), grad_heads[head])
        add_k = nn(grad_scores, queries[head])
        if head:
            value_sum[...] += add_v
            key_sum[...] += add_k
        elif last:
            value_sum[...] = value_before[...] + add_v
            key_sum[...] = key_before[...] + add_k
        else:
            value_sum[...], key_sum[...] = add_v, add_k
        grad_t[rows, :] = nn(keys_t[rows, :], grad_scores)
        current = later
    grad_query = (grad_t[...].T * 0.125).astype(BF)
    gq[...] = grad_query
    bias[...] = jnp.zeros_like(bias)
    bias[0:1, :] = total(grad_query.astype(F32))
    if last:
        gk[...] = key_sum[...].astype(BF)
        grad_value = value_sum[...].astype(BF)
        gv[...] = grad_value
        bias[1:2, :] = total(grad_value.astype(F32))


def norm_one_body(
    tower, rows, mixed_0, mixed_1, mixed_2, mixed_3, w_0, w_1, w_2, w_3, w_2_more, w_3_more,
    b_out, gain, shift, hidden, centred,
):
    summed = rows[...].astype(F32) + b_out[...]
    summed = summed + nn(mixed_0[...], w_0[...]) + nn(mixed_1[...], w_1[...])
    here, there = lane_halves(tower, w_2)
    for mixed, weight, more in ((mixed_2, w_2, w_2_more), (mixed_3, w_3, w_3_more)):
        summed = summed + nn(mixed[:, here], weight[...]) + nn(mixed[:, there], more[...])
    middle = centre(summed)
    hidden[...] = (middle * spread_of(middle) * gain[...] + shift[...]).astype(BF)
    centred[...] = middle


def lane_halves(tower, part):
    size = part.shape[0]
    return (
        pl.ds(pl.multiple_of(tower[0] * size, size), size),
        pl.ds(pl.multiple_of((1 - tower[0]) * size, size), size),
    )


def gelu_pair(inner):
    cdf = 0.5 + 0.5 * lax.erf(inner * math.sqrt(0.5))
    density = jnp.exp(-0.5 * inner * inner) * (1.0 / math.sqrt(2.0 * math.pi))
    return (inner * cdf).astype(BF), (cdf + inner * density).astype(BF)


def ffn_body(
    first, second, w_up, b_up, w_down,
    active_one, active_two, slope_one, slope_two, part_one, part_two,
):
    inners = [nn(first[...], w_up[...]) + b_up[...]]
    inners.append(nn(second[...], w_up[...]) + b_up[...])
    places = ((active_one, slope_one, part_one), (active_two, slope_two, part_two))
    for inner, (active, slope, part) in zip(inners, places):
        act, active_slope = gelu_pair(inner)
        active[...] = act
        active.flush()
        slope[...] = active_slope
        slope.flush()
        part[...] = nn(act, w_down[...]).astype(BF)


def ffn_only_body(rows, w_up, b_up, w_down, part):
    inner = nn(rows[...], w_up[...]) + b_up[...]
    act = (inner * (0.5 + 0.5 * lax.erf(inner * math.sqrt(0.5)))).astype(BF)
    part[...] = nn(act, w_down[...]).astype(BF)


def ffn_keep_body(
    first, second, w_up, b_up,
    active_one, active_two, slope_one, slope_two, copy_one, copy_two,
):
    copy_one[...], copy_two[...] = first[...], second[...]
    copy_one.flush()
    copy_two.flush()
    for rows, active, slope in ((first, active_one, slope_one), (second, active_two, slope_two)):
        active[...], slope[...] = gelu_pair(nn(rows[...], w_up[...]) + b_up[...])
        active.flush()
        slope.flush()


def head_rows(centred, gain_one, shift_one, part, near, far, b_down, gain, shift):
    hidden = centred[...] * spread_of(centred[...]) * gain_one[...] + shift_one[...]
    summed = part[...].astype(F32) + near[...].astype(F32) + far[...].astype(F32)
    middle = centre(hidden + summed + b_down[...])
    return middle, middle * spread_of(middle) * gain[...] + shift[...]


def head_body(
    centred, gain_one, shift_one, part, near, far, b_down, gain, shift,
    col_weight, b_col, pick, cls_own, send, send_half,
):
    _, final = head_rows(centred, gain_one, shift_one, part, near, far, b_down, gain, shift)
    col, _ = unit_rows(nn(final.astype(BF), col_weight[...]) + b_col[...])
    cls, _ = unit_rows(nn(pick[...], final, HIGH))
    count = send_half.shape[0]
    col = col.astype(BF)
    cls_own[...] = jnp.concatenate([cls, jnp.zeros_like(cls)], axis=0).astype(BF)
    send[...] = col
    send_half[...] = col[count:]


def head_keep_body(
    centred, gain_one, shift_one, part, near, far, b_down, gain, shift,
    col_weight, b_col, pick, encoded, middle, col_pre, cls_raw,
):
    kept, final = head_rows(centred, gain_one, shift_one, part, near, far, b_down, gain, shift)
    middle[...] = kept
    middle.flush()
    encoded[...] = final.astype(BF)
    encoded.flush()
    col_pre[...] = nn(final.astype(BF), col_weight[...]) + b_col[...]
    col_pre.flush()
    cls_raw[...] = nn(pick[...], final, HIGH)


def similar_body(is_query, own, *refs):
    pieces, (weight_p, exp_terms, others, sums) = refs[:6], refs[6:]
    count = own.shape[0]
    row = 0
    for piece in pieces:
        rows = slice(row, row + piece.shape[0])
        others[rows, :] = piece[...]
        exp_terms[:, rows] = jnp.exp(SHARP * nt(own[...], piece[...]))
        row += piece.shape[0]
    weight = weight_p[...].astype(BF)
    terms = exp_terms[...]
    high = terms.astype(BF)
    low = (terms - high.astype(F32)).astype(BF)
    sums_q = nt(weight, high) + nt(weight, low)
    sums_p = nn(weight[:, :count], high) + nn(weight[:, :count], low)
    sums_q = jnp.concatenate([sums_q, jnp.zeros((sums_q.shape[0], 3 * count), F32)], axis=1)
    sums[...] = jnp.where(flagged(is_query[0], sums_p.shape), sums_q, sums_p)


def dense_body(is_query, vectors, targets, cls_raw, grad_cls, loss):
    block = vectors[...]
    shape = (block.shape[0], block.shape[0])
    segs = cls_raw.shape[0]
    kind_rows = block.shape[0] // 2
    query_kind = 1 - is_query[0]
    row_kind = lax.broadcasted_iota(I32, shape, 0) // kind_rows
    col_kind = lax.broadcasted_iota(I32, shape, 1) // kind_rows
    paired = jnp.logical_and(row_kind == query_kind, col_kind != query_kind)
    logits = jnp.where(paired, nt(block, block) * SCALE_DENSE, -1e30)
    onehot = targets[...]
    top = jnp.max(logits, axis=1, keepdims=True)
    exp_terms = jnp.where(paired, jnp.exp(logits - top), 0.0)
    norm = jnp.sum(exp_terms, axis=1, keepdims=True)
    norm = jnp.where(norm > 0.0, norm, 1.0)
    grad = ((exp_terms / norm - onehot) * (1.0 / segs)).astype(BF)
    grad = jnp.where(paired, grad, jnp.zeros_like(grad))
    hit = jnp.sum(jnp.where(paired, logits * onehot, 0.0), axis=1, keepdims=True)
    losses = top + jnp.log(norm) - hit
    rows = lax.broadcasted_iota(I32, losses.shape, 0) - query_kind * kind_rows
    mine = jnp.logical_and(rows >= 0, rows < segs)
    loss[...] = jnp.zeros_like(loss) + jnp.sum(jnp.where(mine, losses, 0.0))
    grad_rows = nn(grad[: 2 * segs], block)[:segs]
    grad_cols = tn(grad[:, : 2 * segs], block)[:segs]
    own = jnp.where(flagged(is_query[0], grad_rows.shape), grad_rows, grad_cols) * SCALE_DENSE
    grad_cls[...] = unit_back(own, *unit_rows(cls_raw[...]))


def score_body(
    is_query, sums, exp_terms, others, weight_q, weight_p, target, col_pre,
    grad_pre, scores,
):
    count = exp_terms.shape[0]
    segs = weight_q.shape[0]
    seg_sums = sums[...]
    w_q, w_p = weight_q[...], weight_p[...]
    size = jnp.sum(w_q, axis=1, keepdims=True)
    nearest = jnp.log(seg_sums) * (1.0 / SHARP)
    pair = nt(w_q, nearest, HIGH) / size
    scores[...] = pair
    logits = pair * SCALE_COL
    onehot = target[...]
    top = jnp.max(logits, axis=1, keepdims=True)
    terms = jnp.exp(logits - top)
    norm = jnp.sum(terms, axis=1, keepdims=True)
    grad_pair = (terms / norm - onehot) * (SCALE_COL / segs) / size
    grad_sums = tn(grad_pair, w_q, HIGH) / (SHARP * seg_sums)
    left = jnp.where(
        flagged(is_query[0], (segs, count)), grad_sums[:, :count], w_p[:, :count]
    )
    right = jnp.where(flagged(is_query[0], w_p.shape), w_p, grad_sums)
    grad_similar = (tn(left, right, HIGH) * (exp_terms[...] * SHARP)).astype(BF)
    grad_vec = nn(grad_similar, others[...])
    pre = unit_back(grad_vec, *unit_rows(col_pre[...])).astype(BF)
    grad_pre[...] = pre


def norm_two_back_rows(grad_pre, col_weight, grad_cls, pick, middle, gain):
    grad_final = nt(grad_pre[...], col_weight[...]) + tn(pick[...], grad_cls[...], HIGH)
    spread = spread_of(middle[...])
    unit = middle[...] * spread
    return norm_back(grad_final, unit, spread, gain[...]), grad_final, unit


def norm_two_back_body(grad_pre, col_weight, grad_cls, pick, middle, gain, grad_b):
    back, _, _ = norm_two_back_rows(grad_pre, col_weight, grad_cls, pick, middle, gain)
    grad_b[...] = back.astype(BF)


def norm_two_keep_body(
    grad_pre, col_weight, grad_cls, pick, middle, gain, scores, target, dense_loss,
    grad_two, grad_kept, small,
):
    back, grad_final, unit = norm_two_back_rows(
        grad_pre, col_weight, grad_cls, pick, middle, gain
    )
    grad_kept[...] = back.astype(BF)
    grad_kept.flush()
    grad_two[...] = back
    grad_two.flush()
    logits = scores[...] * SCALE_COL
    top = jnp.max(logits, axis=1, keepdims=True)
    norm = jnp.sum(jnp.exp(logits - top), axis=1, keepdims=True)
    losses = top + jnp.log(norm) - jnp.sum(logits * target[...], axis=1, keepdims=True)
    small[0:1, :] = total(grad_pre[...].astype(F32))
    small[1:2, :] = total(back)
    small[2:3, :] = total(grad_final * unit)
    small[3:4, :] = total(grad_final)
    small[4:5, :] = jnp.zeros((1, unit.shape[1]), F32) + (jnp.sum(losses) + dense_loss[0:1, 0:1])
    small[5:8, :] = jnp.zeros((3, unit.shape[1]), F32)


def ffn_back_body(
    first, second, slope_one, slope_two, w_down, w_up,
    inner_one, inner_two, part_one, part_two, bias,
):
    bias_sum = jnp.zeros((1, slope_one.shape[1]), F32)
    raws = [nt(second[...], w_down[...]), nt(first[...], w_down[...])]
    for raw, slope, inner in zip(raws, (slope_two, slope_one), (inner_two, inner_one)):
        grad = (raw * slope[...].astype(F32)).astype(BF)
        inner[...] = grad
        inner.flush()
        bias_sum = bias_sum + total(grad.astype(F32))
    part_two[...] = nt(inner_two[...], w_up[...]).astype(BF)
    part_one[...] = nt(inner_one[...], w_up[...]).astype(BF)
    bias[...] = bias_sum


def ffn_back_only_body(rows, slope, w_down, w_up, part):
    inner = (nt(rows[...], w_down[...]) * slope[...].astype(F32)).astype(BF)
    part[...] = nt(inner, w_up[...]).astype(BF)


def ffn_back_keep_body(first, second, slope_one, slope_two, w_down, inner_one, inner_two, bias):
    bias_sum = jnp.zeros((1, slope_one.shape[1]), F32)
    for rows, slope, inner in ((first, slope_one, inner_one), (second, slope_two, inner_two)):
        grad = (nt(rows[...], w_down[...]) * slope[...].astype(F32)).astype(BF)
        inner[...] = grad
        inner.flush()
        bias_sum = bias_sum + total(grad.astype(F32))
    bias[...] = bias_sum


def norm_one_back_body(
    tower, grad_two, part, near, far, centred, gain, w_0, w_1, w_2, w_3, w_2_more, w_3_more,
    grad_one, grad_b, small, mixed_0, mixed_2, mixed_13,
):
    grad = (
        grad_two[...]
        + part[...].astype(F32)
        + near[...].astype(F32)
        + far[...].astype(F32)
    )
    spread = spread_of(centred[...])
    unit = centred[...] * spread
    back = norm_back(grad, unit, spread, gain[...])
    grad_one[...] = back
    grad_one.flush()
    rounded = back.astype(BF)
    grad_b[...] = rounded
    grad_b.flush()
    width = mixed_0.shape[1]
    size = w_2.shape[0]
    for weight, more, mixed, lane in (
        (w_3, w_3_more, mixed_13, width), (w_2, w_2_more, mixed_2, 0)
    ):
        for part, side in ((weight, tower[0]), (more, 1 - tower[0])):
            lanes = pl.ds(pl.multiple_of(side * size + lane, size), size)
            mixed[:, lanes] = nt(rounded, part[...]).astype(BF)
    mixed_13[:, :width] = nt(rounded, w_1[...]).astype(BF)
    mixed_0[...] = nt(rounded, w_0[...]).astype(BF)
    small[0:1, :] = total(back)
    small[1:2, :] = total(grad * unit)
    small[2:3, :] = total(grad)
    small[3:8, :] = jnp.zeros((5, unit.shape[1]), F32)


def input_grad_body(
    query_near, query_far, grad_key, grad_value, weight, part_0, part_2, part_31
):
    count = part_0.shape[0]
    places = ((3, part_31, 0), (1, part_31, count), (2, part_2, 0), (0, part_0, 0))
    for block, out, row in places:
        own = slice(block % 2 * count, (block % 2 + 1) * count)
        rows = slice(block * count, (block + 1) * count)
        out[row : row + count, :] = (
            nt((query_near, query_far)[block // 2][own, :], weight[0])
            + nt(grad_key[rows, :], weight[1])
            + nt(grad_value[rows, :], weight[2])
        ).astype(BF)


def order_rows(place, source, out, size):
    for block in range(source.shape[1] // size):
        start = pl.multiple_of((jnp.int32(block) ^ place) * size, size)
        out[block * size : (block + 1) * size, :] = source[:, pl.ds(start, size)].T


def weight_grad_body(place, *refs, lefts, rights, cuts, first):
    left = refs[:lefts]
    right = refs[lefts : lefts + sum(rights)]
    outs, (ordered, joined) = refs[lefts + sum(rights) : -2], refs[-2:]
    token = 0
    for part in left:
        tokens = slice(token, token + part.shape[0])
        order_rows(place[0], part, ordered.at[:, tokens], LANES)
        token += part.shape[0]
    at = 0
    lane = 0
    for group in rights:
        token = 0
        for part in right[at : at + group]:
            rows = part.shape[0]
            lanes = min(part.shape[1], joined.shape[1])
            joined[token : token + rows, lane : lane + lanes] = part[:, first : first + lanes]
            token += rows
        at += group
        lane += lanes
    half = ordered.shape[0] // 2
    lane = 0
    for cut, (keep, send) in zip(cuts, zip(outs[::2], outs[1::2])):
        lanes = slice(lane, lane + cut)
        for rows, out in ((slice(half, 2 * half), send), (slice(0, half), keep)):
            out[...] = nn(ordered[rows, :], joined[:, lanes]).astype(BF)
            if isinstance(out, Leaving):
                out.flush()
        lane += cut


def turned_grad_body(place, mp_place, grad, *refs, rows):
    left, (part_0, part_2, part_31, ordered) = refs[:-4], refs[-4:]
    order_rows(place[0], grad, ordered, LANES)
    outs = ((0, part_0, 0), (2, part_2, 0), (3, part_31, 0), (1, part_31, rows))
    for block, out, lane in outs:
        if len(left) == 1:
            start = pl.multiple_of((jnp.int32(block) ^ mp_place[0]) * rows, rows)
            right = left[0][:, pl.ds(start, rows)]
        else:
            right = left[block][...]
        out[:, lane : lane + rows] = nn(ordered[...], right).astype(BF)
        if isinstance(out, Leaving):
            out.flush()


def norm_two_keep_turned_body(place, mp_place, encoded, grad_pre, *refs, rows):
    ins, (grad_two, grad_kept, small, part_0, part_2, part_31, ordered) = refs[:8], refs[8:]
    norm_two_keep_body(grad_pre, *ins, grad_two, grad_kept, small)
    turned_grad_body(
        place, mp_place, grad_pre, encoded, part_0, part_2, part_31, ordered, rows=rows
    )


def place_col_body(mp_place, tower, w_0, w_1, w_2, w_3, w_2_more, w_3_more, out):
    count = w_0.shape[0]
    here, there = lane_halves(tower, w_2)
    for block, parts in enumerate(((w_0,), (w_1,), (w_2, w_2_more), (w_3, w_3_more))):
        start = pl.multiple_of((jnp.int32(block) ^ mp_place[0]) * count, count)
        if len(parts) == 1:
            out[pl.ds(start, count), :] = parts[0][...]
        else:
            size = parts[0].shape[0]
            out[pl.ds(pl.multiple_of(start + tower[0] * size, size), size), :] = parts[0][...]
            out[pl.ds(pl.multiple_of(start + (1 - tower[0]) * size, size), size), :] = parts[1][...]


def copy_out(copies, source, target, sem):
    copies.append(pltpu.make_async_copy(source, target, sem))
    copies[-1].start()


def place_wide_body(place, *refs, size):
    *parts, out, buffer = refs[: -8]
    sems = refs[-8:]
    copies = []
    cut = parts[0].shape[1]
    for block in range(8):
        here = pl.ds(block * size, size)
        start = pl.multiple_of((jnp.int32(block) ^ place[0]) * size, size)
        row = block % 4 * size
        for column in range(len(parts) // 2):
            part = parts[2 * column + block // 4]
            lanes = slice(column * cut, (column + 1) * cut)
            buffer[here, lanes] = part[row : row + size, :].astype(F32)
        copy_out(copies, buffer.at[here], out.at[pl.ds(start, size)], sems[block])
    for copy in copies:
        copy.wait()


def place_qkv_body(place, one, one_more, qkv, buffer, *sems, size):
    copies = []
    width = qkv.shape[2]
    for block in range(8):
        here = pl.ds(block * size, size)
        start = pl.multiple_of((jnp.int32(block) ^ place[0]) * size, size)
        rows = slice(block % 4 * size, (block % 4 + 1) * size)
        part = (one, one_more)[block // 4]
        for kind in range(3):
            lanes = slice(kind * width, (kind + 1) * width)
            buffer[kind, here, :] = part[rows, lanes].astype(F32)
            copy_out(
                copies,
                buffer.at[kind, here],
                qkv.at[kind, pl.ds(start, size)],
                sems[3 * block + kind],
            )
    for copy in copies:
        copy.wait()


def place_last_body(place, one, one_more, out, col, *, size):
    width = out.shape[0]
    for target, lane in ((out, 0), (col, width)):
        for block in range(8):
            start = pl.multiple_of((jnp.int32(block) ^ place[0]) * size, size)
            rows = slice(block % 4 * size, (block % 4 + 1) * size)
            part = (one, one_more)[block // 4]
            target[:, pl.ds(start, size)] = part[rows, lane : lane + width].astype(F32).T
        target.flush()


def dp_bits():
    return [1 << k for k in range(int(math.log2(lax.axis_size("dp"))))]


def add(*values):
    return sum(value.astype(F32) for value in values).astype(BF)


def side_of(axis, bit):
    return jnp.minimum(lax.axis_index(axis) & bit, 1)


def join(value, other, axis, bit):
    return jnp.where(
        side_of(axis, bit) == 0,
        jnp.concatenate([value, other]),
        jnp.concatenate([other, value]),
    )


def more_bits():
    return [("dp", bit) for bit in dp_bits()[2:]]


def sum_more(value):
    for axis, bit in more_bits():
        half = value.shape[0] // 2
        side = side_of(axis, bit)
        sent = lax.dynamic_slice_in_dim(value, (1 - side) * half, half, 0)
        kept = lax.dynamic_slice_in_dim(value, side * half, half, 0)
        value = add(kept, swap(sent, axis, bit))
    for axis, bit in more_bits()[::-1]:
        value = join(value, swap(value, axis, bit), axis, bit)
    return value


HOPS = (("tower", 1), ("dp", 1), ("dp", 2))


class Unit:
    def __init__(self, keep, send):
        self.value, self.send, self.stage = keep, send, 0

    def hop(self):
        return HOPS[min(self.stage, 5 - self.stage)]

    def land(self, got):
        self.stage += 1
        if self.stage <= 3:
            value = self.value.astype(F32) + got.astype(F32)
            if self.stage < 3:
                half = value.shape[0] // 2
                self.value, self.send = value[:half], value[half:].astype(BF)
            else:
                self.send = sum_more(value.astype(BF))
        elif self.stage < 6:
            self.send = jnp.concatenate([self.send, got])
        else:
            self.halves = (self.send, got)


class Small:
    def __init__(self, value):
        self.send, self.stage = value, 0

    def hop(self):
        return HOPS[self.stage]

    def land(self, got):
        self.stage += 1
        self.send = self.send + got
        if self.stage == 3:
            for axis, bit in more_bits():
                self.send = self.send + swap(self.send, axis, bit)


def together(*values):
    return lax.optimization_barrier(values)


def launch(units):
    groups = {}
    for unit in units:
        groups.setdefault((unit.hop(), unit.send.dtype), []).append(unit)
    started = []
    for (hop, _), group in groups.items():
        send = group[0].send
        if len(group) > 1:
            send = jnp.concatenate([unit.send for unit in group], axis=1)
        started.append((group, send, swap(send, *hop)))
    return started


def land(started, *others):
    flights = [flight for _, _, flight in started]
    sizes = [value.size * value.dtype.itemsize for value in flights]
    soon = [k for k, size in enumerate(sizes) if size < max(sizes)]
    late = [k for k in range(len(flights)) if k not in soon]
    done = together(*[flights[k] for k in soon], *others)
    done = together(*done, *[flights[k] for k in late])
    others = done[len(soon) : len(soon) + len(others)]
    landed = done[: len(soon)] + done[len(soon) + len(others) :]
    arrived = []
    for k, got in sorted(zip(soon + late, landed), key=lambda pair: pair[0]):
        group = started[k][0]
        if group is None:
            arrived.append(got)
            continue
        lane = 0
        for unit in group:
            width = unit.send.shape[1]
            unit.land(got if len(group) == 1 else got[:, lane : lane + width])
            lane += width
    return arrived, list(others)


def move(value, hop):
    return (None, value, swap(value, *hop))


def phase(units=(), moves=(), fill=None, then=None, more=()):
    if moves:
        for unit in units:
            unit.send = after(unit.send, moves[0][0])
    started = [move(value, hop) for value, hop in moves] + launch(units)
    ready = [send for _, send, _ in started]
    filled = list(fill(lambda value: after(value, *ready))) if fill else []
    extra = launch([then(filled)]) if then else []
    arrived, filled = land(started + list(more), *filled)
    return (arrived, filled, extra) if then else (arrived, filled)


def place_of(hops):
    place = 0
    for axis, bit in hops:
        place = place * 2 + side_of(axis, bit)
    return place[None].astype(I32)


def relative(values, mp_index):
    size = values.shape[-1] // 4
    blocks = [values[..., k * size : (k + 1) * size] for k in range(4)]
    values = jnp.where(mp_index & 1, jnp.concatenate([blocks[k ^ 1] for k in range(4)], -1), values)
    blocks = [values[..., k * size : (k + 1) * size] for k in range(4)]
    return jnp.where(mp_index & 2, jnp.concatenate([blocks[k ^ 2] for k in range(4)], -1), values)


def flip(values, bit):
    size = values.shape[-1] // 4
    return jnp.concatenate([values[:, (k ^ bit) * size :][:, :size] for k in range(4)], axis=1)


def per_device(
    tokens,
    segment_ids,
    key_mask,
    positives,
    w_qkv,
    b_qv,
    w_out,
    b_out,
    gain_one,
    shift_one,
    w_up,
    b_up,
    w_down,
    b_down,
    gain_two,
    shift_two,
    w_col,
    b_col,
):
    own_rows = tokens[0, 0]
    count, model_dim = own_rows.shape
    pair, width = 2 * count, w_out.shape[0]
    half = count // 2
    units = w_up.shape[1]
    segs = positives.shape[1]
    dp_size = lax.axis_size("dp")
    mp_index = lax.axis_index("mp")
    dp_index = lax.axis_index("dp")
    tower = lax.axis_index("tower")
    is_query = tower == 0
    query_flag = (1 - tower)[None].astype(I32)
    mp_place = mp_index[None].astype(I32)
    rest_place = place_of(HOPS)
    tower_place = tower[None].astype(I32)
    labels = jnp.arange(segs, dtype=I32)
    row = lambda vector: vector[None, :]
    block_bf = ((count, model_dim), BF)
    block_f32 = ((count, model_dim), F32)

    def core(block):
        return swap(block, "mp", 1)

    def across(block):
        return swap(block, "mp", 2)

    x_0, x_1, x_2 = own_rows, core(own_rows), across(own_rows)
    w_three = jnp.transpose(w_qkv, (1, 0, 2))

    seg_pair = segment_ids[:, 0]
    starts = jnp.concatenate([jnp.ones((2, 1), bool), seg_pair[:, 1:] != seg_pair[:, :-1]], axis=1)
    valid_pair = jnp.logical_or(key_mask[:, 0] > 0, starts)
    codes = relative(seg_pair + 16 * valid_pair.astype(I32) + 32 * starts.astype(I32), mp_index)
    seg_rel, valid_rel = codes & 15, (codes & 16) > 0
    code_row = jnp.where(is_query, codes[0], codes[1])
    seg_row = code_row & 15
    seg_key = jnp.broadcast_to(
        jnp.where((code_row & 16) > 0, seg_row, -1)[:, None], (4 * count, LANES)
    )
    seg_query = jnp.broadcast_to(seg_row[None, :], (8, 4 * count))
    members = seg_rel[:, None, :] == labels[None, :, None]
    weights = jnp.logical_and(members, valid_rel[:, None, :]).astype(F32)
    weight_q, weight_p = weights[0], weights[1]
    pick = (code_row[None, :count] - 32 == labels[:, None] + 16).astype(F32)
    order = dp_index ^ jnp.arange(dp_size, dtype=I32)
    kinds = jnp.arange(2, dtype=I32)[:, None, None]
    targets = (
        (1 - tower) * dp_size * segs
        + jnp.arange(dp_size, dtype=I32)[None, :, None] * segs
        + positives[order][None]
    )
    targets = jnp.where(kinds == tower, targets, -1).reshape(2 * dp_size * segs)
    paired = (targets[:, None] == jnp.arange(2 * dp_size * segs, dtype=I32)).astype(F32)
    positive_row = lax.dynamic_index_in_dim(positives, dp_index, 0, keepdims=False)
    positive_row = (positive_row[:, None] == labels).astype(F32)

    half_bf = ((pair, width), BF)
    mixed_bf = ((count, width), BF)
    x_hop, core_hop, y_hop = ("mp", 2), ("mp", 1), ("tower", 1)

    def project(first, second, kept=()):
        return call(
            project_body,
            "project",
            [first, second, w_three, b_qv],
            [half_bf] * 3 + list(kept),
            semaphores=len(kept),
        )

    near_qkv = project(x_0, x_1)
    halves = [
        lax.dynamic_slice_in_dim(weight, tower * half, half, 0) for weight in (w_out, w_col)
    ]
    x_2, out_half, col_half, out_1, col_1 = together(
        x_2, *halves, core(w_out), core(w_col), near_qkv,
        seg_key, seg_query, weight_q, weight_p, pick, paired, positive_row,
    )[:5]
    x_3 = core(x_2)
    out_2, col_2 = across(out_half), across(col_half)
    far_qkv = project(x_2, x_3, [KeptOut(*block_bf)] * 2)
    x_2_kept, x_3_kept = far_qkv[3:]
    key_values = [near_qkv[1], far_qkv[1], near_qkv[2], far_qkv[2]]
    seg_query_near, seg_query_far = seg_query[:, :pair], seg_query[:, pair:]

    def attend(seg_half, query):
        return call(
            attend_body,
            "attend",
            [seg_key, seg_half, query, *key_values],
            [Out((8, pair), F32), mixed_bf, mixed_bf],
            [((4 * count, width), BF), ((width, 4 * count), BF), ((width, pair), F32)],
        )

    total_far, mixed_far_2, mixed_far_3 = attend(seg_query_far, far_qkv[0])
    mixed_far_2, mixed_far_3, out_2 = together(mixed_far_2, mixed_far_3, out_2)
    (out_2_more, mixed_2, mixed_1_2), (total_near, mixed_0, mixed_near_1, col_2) = phase(
        (),
        [(out_2, y_hop), (mixed_far_2, x_hop), (mixed_far_3, x_hop)],
        lambda late: [*attend(seg_query_near, late(near_qkv[0])), col_2],
    )
    (mixed_1, mixed_3, out_3, out_3_more), _ = phase(
        (),
        [(mixed_near_1, core_hop), (mixed_1_2, core_hop), (out_2, core_hop)]
        + [(out_2_more, core_hop)],
    )
    col_3 = core(col_2)
    mixed = [mixed_0, mixed_1, mixed_2, mixed_3]
    outs = [w_out, out_1, out_2, out_3, out_2_more, out_3_more]
    hidden, centred_one = call(
        norm_one_body,
        "norm_one",
        [tower_place, own_rows, *mixed, *outs, row(b_out), row(gain_one), row(shift_one)],
        [block_bf, block_f32],
    )

    h_0, h_1 = hidden, core(hidden)
    kept_bf = Out((count, units), BF)
    (h_2, col_2_more), (act_0, act_1, slope_0, slope_1, part_0, part_1) = phase(
        (),
        [(hidden, x_hop), (col_2, y_hop)],
        lambda late: call(
            ffn_body,
            "feed_forward",
            [h_0, h_1, w_up, row(b_up), w_down],
            [kept_bf] * 4 + [Out(*block_bf), block_bf],
        ),
    )
    h_3, col_3_more = core(h_2), core(col_2_more)

    def feed_far(rows):
        return call(
            ffn_only_body, "feed_far", [rows, w_up, row(b_up), w_down], [block_bf]
        )[0]

    part_2 = feed_far(h_2)
    part_3 = feed_far(after(h_3, part_2))
    near_sum = core(part_1)
    joined = add(part_2, core(part_3))
    joined, near_sum = together(joined, near_sum)
    (arrived,), (act_2, act_3, slope_2, slope_3, h_2_kept, h_3_kept, col_weight) = phase(
        (),
        [(joined, x_hop)],
        lambda late: [
            *call(
                ffn_keep_body,
                "feed_keep",
                [late(h_2), h_3, w_up, row(b_up)],
                [kept_bf] * 4 + [Out(*block_bf)] * 2,
            ),
            *call(
                place_col_body,
                "place_col",
                [mp_place, tower_place, w_col, late(col_1), col_2, col_3, col_2_more, col_3_more],
                [((model_dim, model_dim), BF)],
            ),
        ],
    )
    ins = [centred_one, row(gain_one), row(shift_one), part_0, near_sum, arrived]
    ins += [row(b_down), row(gain_two), row(shift_two), col_weight, row(b_col), pick]
    cls_own, send, send_half = call(
        head_body,
        "heads",
        ins,
        [((2 * segs, model_dim), BF), block_bf, ((half, model_dim), BF)],
    )

    cls_all = cls_own[:segs]
    started = [move(send, y_hop), move(send_half, x_hop)]
    cls_hop = move(cls_all, ("dp", 1))
    kept = call(
        head_keep_body,
        "heads_keep",
        [after(centred_one, send, send_half, cls_all)] + ins[1:],
        [Out(*block_bf), Out(*block_f32), Out(*block_f32), Out((segs, model_dim), F32)],
    )
    (cls_far,), kept = land([cls_hop], *kept)
    cls_all = jnp.concatenate([cls_all, cls_far])
    for bit in dp_bits()[1:]:
        (cls_far,), _ = land([move(cls_all, ("dp", bit))])
        cls_all = jnp.concatenate([cls_all, cls_far])
    (other, own_half), (cls_all, encoded, middle, col_pre, cls_raw) = land(
        started, cls_all, *kept
    )
    (far_b, far_a, cls_far), _ = phase(
        (), [(own_half, y_hop), (other[:half], x_hop), (cls_all, x_hop)]
    )
    cls_all = add(cls_all, cls_far)
    (near, diag_a, diag_b, cls_near), _ = phase(
        (),
        [(other, core_hop), (far_a, core_hop), (far_b, core_hop), (cls_all, core_hop)],
    )
    cls_all = add(cls_all, cls_near)
    pieces = [other, near, far_a, far_b, diag_a, diag_b]
    exp_terms, others, sums = call(
        similar_body,
        "similar",
        [query_flag, send, *pieces, weight_p],
        [((count, 4 * count), F32), ((4 * count, model_dim), BF), ((segs, 4 * count), F32)],
    )
    cls_all = after(cls_all, sums)
    (swapped, cls_other), _ = phase((), [(sums, x_hop), (cls_all, y_hop)])
    sums = sums + flip(swapped, 2)
    cls_all = jnp.concatenate([cls_all, cls_other])
    (swapped,), (grad_cls, dense_loss) = phase(
        (),
        [(sums, core_hop)],
        lambda late: call(
            dense_body,
            "dense",
            [query_flag, late(cls_all), paired, cls_raw],
            [((segs, model_dim), F32), ((8, LANES), F32)],
        ),
    )
    sums = sums + flip(swapped, 1)
    grad_pre, pair_score = call(
        score_body,
        "scores",
        [query_flag, sums, exp_terms, others, weight_q, weight_p, positive_row, col_pre],
        [block_bf, ((segs, segs), F32)],
    )
    ins = [grad_pre, col_weight, grad_cls, pick, middle, row(gain_two)]
    (grad_two_b,) = call(norm_two_back_body, "norm_two_back", ins, [block_bf])

    def streams(*values):
        return [Stream(value) for value in values]

    def feed_back(first, second, slope_one, slope_two, part):
        return call(
            ffn_back_body,
            "feed_back",
            [first, second, *streams(slope_one, slope_two), w_down, w_up],
            [kept_bf] * 2 + [part, block_bf, Out((1, units), F32)],
            limit=12,
        )

    def weight_grad(left, right, cuts, first=0):
        rows = getattr(left[0], "value", left[0]).shape[1]
        tokens = 4 * count
        outs = [Out((rows // 2, cut), BF) for cut in cuts for _ in range(2)]
        outs[1] = ((rows // 2, cuts[0]), BF)
        return call(
            functools.partial(
                weight_grad_body,
                lefts=len(left),
                rights=[len(parts) for parts in right],
                cuts=cuts,
                first=first,
            ),
            "weight_grad",
            [rest_place, *left, *[part for parts in right for part in parts]],
            outs,
            [((rows, tokens), BF), ((tokens, sum(cuts)), BF)],
            limit=20,
        )

    def turned_grad(grad, left):
        return call(
            functools.partial(turned_grad_body, rows=count),
            "turned_grad",
            [rest_place, mp_place, grad, *left],
            [Out((model_dim, count), BF)] * 2 + [((model_dim, 2 * count), BF)],
            [((model_dim, count), BF)],
        )

    def near_back(late):
        backs = feed_back(grad_two_b, g_1, slope_0, slope_1, Out(*block_bf))
        kept = call(
            functools.partial(norm_two_keep_turned_body, rows=count),
            "norm_two_keep",
            [rest_place, mp_place, Stream(encoded), after(grad_pre, backs[3])]
            + ins[1:]
            + [pair_score, positive_row, dense_loss],
            [Out(*block_f32), Out(*block_bf), Out((8, model_dim), F32)]
            + [Out((model_dim, count), BF)] * 2
            + [((model_dim, 2 * count), BF)],
            [((model_dim, count), BF)],
            limit=14,
        )
        return [*backs, *kept]

    g_1 = core(grad_two_b)
    (g_2,), (inner_0, inner_1, part_0, part_1, bias_near, *kept) = phase(
        (), [(grad_two_b, x_hop)], near_back
    )
    grad_two, grad_two_kept, small_two, col_own, col_joined, col_near = kept
    g_3 = core(g_2)

    def feed_back_far(rows, slope):
        return call(
            ffn_back_only_body, "feed_back_far", [rows, slope, w_down, w_up], [block_bf]
        )[0]

    part_2 = feed_back_far(g_2, slope_2)
    part_3 = feed_back_far(after(g_3, part_2), slope_3)
    cut = model_dim // 2

    def down_grad(late, start):
        return weight_grad(
            streams(act_0, act_1, act_2, act_3),
            [[Stream(grad_two_kept), Stream(g_1), late(g_2), g_3]],
            [cut],
            start,
        )

    (near_sum, arrived), down = phase(
        (), [(part_1, core_hop), (part_3, core_hop)], lambda late: down_grad(late, 0)
    )
    down = [Unit(*down)]
    joined = add(part_2, arrived)

    def unit_grads(late):
        more = down_grad(late, cut)
        inner_2, inner_3, bias_far = call(
            ffn_back_keep_body,
            "feed_back_keep",
            [after(g_2, more[1]), g_3, slope_2, slope_3, w_down],
            [kept_bf] * 2 + [Out((1, units), F32)],
        )
        up = weight_grad(
            [after(h_0, bias_far), h_1, *streams(h_2_kept, h_3_kept)],
            [streams(inner_0, inner_1, inner_2, inner_3)],
            [cut, cut],
        )
        return [*more, *up, bias_far]

    (arrived,), (_, _, *up, bias_far), more = phase(
        down, [(joined, x_hop)], unit_grads, then=lambda filled: Unit(*filled[:2])
    )
    down.append(more[0][0][0])
    up = [Unit(*up[:2]), Unit(*up[2:])]
    grad_one, grad_one_b, small_one, back_0, back_2, back_13 = call(
        norm_one_back_body,
        "norm_one_back",
        [tower_place, grad_two, part_0, near_sum, arrived, centred_one, row(gain_one), *outs],
        [Out(*block_f32), Out(*block_bf), ((8, model_dim), F32)]
        + [mixed_bf, mixed_bf, ((count, 2 * width), BF)],
        limit=12,
    )

    (back_13,), _ = phase((), [(back_13, core_hop)])
    back_23 = jnp.concatenate([back_2, back_13[:, width:]], axis=1)
    all_bf, all_f32 = ((4 * count, width), BF), ((4 * count, width), F32)
    back_scratch = [all_bf] * 2 + [((width, 4 * count), BF), ((width, pair), F32)]

    def back_ins(seg_half, log_total, grads, query, mixed_pair):
        return [seg_key, seg_half, log_total, *grads, query, *mixed_pair, *key_values]

    back_hop = move(back_23, x_hop)
    grad_q_near, key_sum, value_sum, bias_near_q = call(
        functools.partial(attend_back_body, lanes=(0, 0), last=False),
        "attend_back",
        back_ins(
            seg_query_near,
            total_near,
            [after(back_0, back_23), back_13],
            near_qkv[0],
            (mixed_0, mixed_near_1),
        ),
        [half_bf, all_f32, all_f32, ((8, width), F32)],
        back_scratch,
        limit=16,
    )
    _, (grad_q_near,) = land(more, grad_q_near)
    up[0].send = after(up[0].send, down[1].send)
    started = launch([*down, up[0]])
    out_own, out_joined, out_near = turned_grad(
        Stream(after(grad_one_b, *[send for _, send, _ in started])), streams(*mixed)
    )
    (back_23, col_near), (out_near,) = land([back_hop, move(col_near, core_hop)], out_near)
    grad_q_far, grad_k, grad_v, bias_far_v = call(
        functools.partial(attend_back_body, lanes=(0, width), last=True),
        "attend_back",
        back_ins(
            seg_query_far,
            total_far,
            [after(back_23, out_near), back_23],
            far_qkv[0],
            (mixed_far_2, mixed_far_3),
        )
        + [key_sum, value_sum],
        [half_bf, all_bf, all_bf, ((8, width), F32)],
        back_scratch + [all_f32, all_f32],
        limit=16,
    )
    _, (grad_v,) = land(started, grad_v)
    col_joined = add(col_joined, col_near[:, :count])
    col_own = add(col_own, col_near[:, count:])
    up[1].send = after(up[1].send, down[0].send)
    started = [move(out_near, core_hop), move(col_joined, x_hop)]
    started += launch([up[1], up[0], *down])
    qkv = Unit(
        *weight_grad(
            [after(x_0, grad_v, *[send for _, send, _ in started]), x_1, x_2_kept, x_3_kept],
            [[grad_q_near, grad_q_far], [grad_k], [grad_v]],
            [3 * width],
        )
    )
    sent = launch([qkv])
    part_0, part_2, part_31 = call(
        input_grad_body,
        "input_grad",
        streams(after(grad_q_near, qkv.send), grad_q_far, grad_k, grad_v, w_three),
        [Out(*block_bf)] * 2 + [((pair, model_dim), BF)],
    )
    (out_near, col_far), (part_31,) = land(started, part_31)
    out_joined = add(out_joined, out_near[:, :count])
    out_own = add(out_own, out_near[:, count:])
    small = jnp.concatenate([small_two, small_one])
    (out_far, small_far), _ = phase(
        [up[1], up[0], *down], [(out_joined, x_hop), (small, x_hop)], more=sent
    )
    small = small + small_far
    turned = jnp.concatenate([add(out_own, out_far), add(col_own, col_far)], axis=1)
    rows = model_dim // 2
    rest = Unit(turned[:rows], turned[rows:])
    (part_31, small_near), _ = phase(
        [rest, qkv, *down, up[1], up[0]], [(part_31, core_hop), (small, core_hop)]
    )
    bias_v = (bias_far_v + bias_near_q)[:2].reshape(1, 2 * width)
    small = Small(
        jnp.concatenate(
            [
                small + small_near,
                bias_near + bias_far,
                jnp.concatenate([bias_v, jnp.zeros((1, model_dim - 2 * width), F32)], axis=1),
            ]
        )
    )
    joined = add(part_2, part_31[:count])
    phase([*down, rest, up[0], qkv, up[1]])
    phase([up[0], up[1], rest, qkv, small])
    (arrived,), _ = phase([up[1], qkv, rest, small], [(joined, x_hop)])
    grad_input = (
        grad_one
        + part_0.astype(F32)
        + part_31[count:].astype(F32)
        + arrived.astype(F32)
    )
    d_tokens = grad_input.astype(BF).reshape(1, 1, count, model_dim)

    def place_wide(late, *parts):
        halves = [half for unit in parts for half in unit.halves]
        shape = (model_dim, model_dim)
        return call(
            functools.partial(place_wide_body, size=model_dim // 8),
            "place_wide",
            [rest_place, late(halves[0]), *halves[1:]],
            [KeptOut(shape, F32)],
            [(shape, F32)],
            semaphores=8,
        )

    _, (grad_down, d_tokens) = phase(
        [qkv, rest, small], fill=lambda late: [*place_wide(late, *down), d_tokens]
    )
    _, (grad_up, grad_qkv) = phase(
        [rest],
        fill=lambda late: [
            *place_wide(late, *up),
            *call(
                functools.partial(place_qkv_body, size=model_dim // 8),
                "place_qkv",
                [rest_place, late(qkv.halves[0]), qkv.halves[1]],
                [KeptOut((3, model_dim, width), F32)],
                [((3, model_dim, width), F32)],
                semaphores=24,
            ),
        ],
    )
    grad_out, grad_col = call(
        functools.partial(place_last_body, size=model_dim // 8),
        "place_last",
        [rest_place, *rest.halves],
        [Out((width, model_dim), F32)] * 2,
    )
    small = small.send
    loss = small[4, 0] * (1.0 / (segs * 2 * lax.axis_size("mp")))
    return (
        encoded.reshape(1, 1, count, model_dim),
        loss,
        pair_score.reshape(1, segs, segs),
        d_tokens,
        jnp.transpose(grad_qkv, (1, 0, 2)),
        small[17, : 2 * width].reshape(2, width),
        grad_out,
        small[8],
        small[9],
        small[10],
        grad_up,
        small[16],
        grad_down,
        small[1],
        small[2],
        small[3],
        grad_col,
        small[0],
    )


def solution(mesh):
    return jax.shard_map(
        per_device,
        mesh=mesh,
        in_specs=(
            P("tower", "dp", "mp", None),
            P(None, "dp", None),
            P(None, "dp", None),
            P(),
            P(None, None, "mp"),
            P(None, "mp"),
            P("mp", None),
            P(),
            P(),
            P(),
            P(None, "mp"),
            P("mp"),
            P("mp", None),
            P(),
            P(),
            P(),
            P("mp", None),
            P(),
        ),
        out_specs=(
            P("tower", "dp", "mp", None),
            P(),
            P("dp", None, None),
            P("tower", "dp", "mp", None),
            P(None, None, "mp"),
            P(None, "mp"),
            P("mp", None),
            P(),
            P(),
            P(),
            P(None, "mp"),
            P("mp"),
            P("mp", None),
            P(),
            P(),
            P(),
            P("mp", None),
            P(),
        ),
        check_vma=False,
    )
```
